128 devices in a mesh: dp: 4 (over y), ctx: 8 (over x, core), tensor: 4 (over z).
Axes of the slice: x: 4, y: 4, z: 4, core: 2. Of those that a mesh axis runs over, the one named last changes fastest.
Arguments:
- hidden_in: bfloat16 [4, 1536, 2048], P('dp', 'ctx'), may hold values from -6 to 6
- block_order: int32 [4, 16], P('dp'), may hold values from 0 to 15, each once within a row
- w_query: bfloat16 [2048, 2048], P(None, 'tensor'), may hold values from -0.125 to 0.125
- w_keyval: bfloat16 [2048, 512], P(None, 'tensor'), may hold values from -0.125 to 0.125
- w_output: bfloat16 [2048, 2048], P('tensor'), may hold values from -0.5 to 0.5
- w_gate: bfloat16 [2048, 5632], P(None, 'tensor'), may hold values from -0.125 to 0.125
- w_up: bfloat16 [2048, 5632], P(None, 'tensor'), may hold values from -0.125 to 0.125
- w_down: bfloat16 [5632, 2048], P('tensor'), may hold values from -0.078125 to 0.078125
- gain_attn: float32 [2048], replicated, may hold values from 0.5 to 1.5
- gain_ffn: float32 [2048], replicated, may hold values from 0.5 to 1.5
- cotangent: bfloat16 [4, 1536, 2048], P('dp', 'ctx'), may hold values from -6 to 6
Outputs:
- block_out: bfloat16 [4, 1536, 2048], P('dp', 'ctx')
- grad_input: float32 [4, 1536, 2048], P('dp', 'ctx')
- grad_query: float32 [2048, 2048], P(('dp', 'ctx'), 'tensor')
- grad_keyval: float32 [2048, 512], P(('dp', 'ctx'), 'tensor')
- grad_output: float32 [2048, 2048], P('tensor', ('dp', 'ctx'))
- grad_gate: float32 [2048, 5632], P(('dp', 'ctx'), 'tensor')
- grad_up: float32 [2048, 5632], P(('dp', 'ctx'), 'tensor')
- grad_down: float32 [5632, 2048], P('tensor', ('dp', 'ctx'))
- grad_gain_attn: float32 [2048], P(('dp', 'ctx'))
- grad_gain_ffn: float32 [2048], P(('dp', 'ctx'))
The draws below stay inside these ranges and needn't reach their ends.
Inputs may be any that keep to these rules, and one draw needn't show every extreme that they name: `block_order`: each row names each of the 16 position blocks of its sequence exactly once.
All inputs are finite; a program needn't handle non-finite values.
Results may differ from the reference program's by a relative error of at most 0.03.
Values may be sent and summed in bfloat16 or wider, within the bound.
A program may use at most 128 MiB of HBM per device.

```python
import jax
import jax.numpy as jnp
from jax import lax

D = 2048
H = 32
KV = 4
HD = 64
FF = 5632
SEQ = 1536
NSEQ = 4
BLOCKS = 16
BLOCK = 96


def levels(own_key, shape, shards, low, top_value):
    loudness = 1.0
    for position, shards_of in shards:
        heights = jax.random.uniform(jax.random.fold_in(jax.random.fold_in(own_key, 6), position), (shards_of,), jnp.float32, low / len(shards), top_value / len(shards))
        loudness = loudness * jnp.repeat(jnp.exp(heights), shape[position] // shards_of).reshape((-1,) + (1,) * (len(shape) - 1 - position))
    return loudness


def noise(key, dims, width, bound, split=(), kind=jnp.bfloat16):
    entries = width * jax.random.normal(key, dims, jnp.float32)
    if split:
        entries = entries * levels(key, dims, split, -0.22, 0.18)
    return jnp.clip(entries, -bound, bound).astype(kind)


def setup_inputs(seed: int = 0) -> dict:
    keys = jax.random.split(jax.random.key(seed), 12)
    hidden_in = noise(keys[0], (NSEQ, SEQ, D), 1.0, 6.0, ((0, 4), (1, 8)))
    block_order = jax.vmap(lambda own: jax.random.permutation(own, BLOCKS))(jax.random.split(keys[1], NSEQ)).reshape((NSEQ, BLOCKS)).astype(jnp.int32)
    w_query = noise(keys[2], (D, H * HD), D ** -0.5, 0.125, ((1, 4),))
    w_keyval = noise(keys[3], (D, 2 * KV * HD), D ** -0.5, 0.125, ((1, 4),))
    w_output = noise(keys[4], (H * HD, D), (H * HD // 16) ** -0.5, 0.5, ((0, 4),))
    w_gate = noise(keys[5], (D, FF), D ** -0.5, 0.125, ((1, 4),))
    w_up = noise(keys[6], (D, FF), D ** -0.5, 0.125, ((1, 4),))
    w_down = noise(keys[7], (FF, D), FF ** -0.5, 0.078125, ((0, 4),))
    gain_attn = jnp.clip(1.0 + 0.1 * jax.random.normal(keys[8], (D,), jnp.float32), 0.5, 1.5)
    gain_ffn = jnp.clip(1.0 + 0.1 * jax.random.normal(keys[9], (D,), jnp.float32), 0.5, 1.5)
    cotangent = noise(keys[10], (NSEQ, SEQ, D), 1.0, 6.0, ((0, 4), (1, 8)))
    return dict(hidden_in=hidden_in, block_order=block_order, w_query=w_query, w_keyval=w_keyval, w_output=w_output, w_gate=w_gate, w_up=w_up, w_down=w_down, gain_attn=gain_attn, gain_ffn=gain_ffn, cotangent=cotangent)


EPSILON = 1e-05
NEG_FILL = -1e+30
ROPE_BASE = 10000.0

@jax.custom_vjp
def low(v):
    return lax.optimization_barrier(v.astype(jnp.bfloat16)).astype(jnp.float32)

@jax.custom_vjp
def low_back(v):
    return v

def low_keep(v):
    return (low(v), None)

def low_pass(kept, grad):
    return (grad,)

def back_keep(v):
    return (v, None)

def back_low(kept, grad):
    return (low(grad),)
low.defvjp(low_keep, low_pass)
low_back.defvjp(back_keep, back_low)

def positions(order_row):
    row_index = jnp.arange(SEQ, dtype=jnp.int32)
    return order_row[row_index // BLOCK].astype(jnp.int32) * BLOCK + row_index % BLOCK

def angle_table(token_place):
    half_size = HD // 2
    freq_table = ROPE_BASE ** (-jnp.arange(half_size, dtype=jnp.float32) / half_size)
    phases = token_place.astype(jnp.float32)[:, None] * freq_table[None, :]
    return (jnp.cos(phases), jnp.sin(phases))

def rotate(values, cosine_table, sine_table):
    half_size = values.shape[-1] // 2
    first_half = values[..., :half_size]
    second_half = values[..., half_size:]
    return jnp.concatenate([first_half * cosine_table - second_half * sine_table, second_half * cosine_table + first_half * sine_table], -1)

def rms_scale(values):
    return values * lax.rsqrt(lax.optimization_barrier(jnp.mean(values * values, -1, keepdims=True)) + EPSILON)

def block_forward(hidden_rows, w_query, w_keyval, w_output, w_gate, w_up, w_down, gain_attn, gain_ffn, token_place):
    highest = lax.Precision.HIGHEST
    cosine_table, sine_table = angle_table(token_place)
    group_size = H // KV
    score_scale = HD ** (-0.5)
    normed = low(rms_scale(hidden_rows) * gain_attn)
    query_proj = low_back(jnp.dot(normed, w_query, precision=highest))
    keyval_proj = low_back(jnp.dot(normed, w_keyval, precision=highest))
    queries = low(rotate(query_proj.reshape(SEQ, KV, group_size, HD), cosine_table[:, None, None, :], sine_table[:, None, None, :]))
    keyval = keyval_proj.reshape(SEQ, KV, 2, HD)
    key_rows = low(rotate(keyval[:, :, 0], cosine_table[:, None, :], sine_table[:, None, :]))
    value_rows = low(keyval[:, :, 1])
    visible = token_place[None, :] <= token_place[:, None]

    def attend_group(operands):
        group_queries, group_keys, group_values = operands
        scores = low_back(jnp.einsum('gqd,kd->gqk', group_queries, group_keys, precision=highest) * score_scale)
        scores = jnp.where(visible[None], scores, NEG_FILL)
        shifted = jnp.exp(scores - lax.optimization_barrier(jnp.max(scores, -1, keepdims=True)))
        weights = low(shifted / lax.optimization_barrier(jnp.sum(shifted, -1, keepdims=True)))
        return jnp.einsum('gqk,kd->gqd', weights, group_values, precision=highest)
    attended = lax.map(jax.checkpoint(attend_group), (queries.transpose(1, 2, 0, 3), key_rows.transpose(1, 0, 2), value_rows.transpose(1, 0, 2)))
    attn_rows = low_back(low(attended.transpose(2, 0, 1, 3).reshape(SEQ, H * HD)))
    mid_stream = hidden_rows + low_back(jnp.dot(attn_rows, w_output, precision=highest))
    normed_mid = low(rms_scale(mid_stream) * gain_ffn)
    gate_proj = low_back(jnp.dot(normed_mid, w_gate, precision=highest))
    up_proj = low_back(jnp.dot(normed_mid, w_up, precision=highest))
    inner_act = low(gate_proj / (1.0 + jnp.exp(-gate_proj)) * up_proj)
    return mid_stream + low_back(jnp.dot(inner_act, w_down, precision=highest))

def reference(hidden_in, block_order, w_query, w_keyval, w_output, w_gate, w_up, w_down, gain_attn, gain_ffn, cotangent):
    weights = (w_query.astype(jnp.float32), w_keyval.astype(jnp.float32), w_output.astype(jnp.float32), w_gate.astype(jnp.float32), w_up.astype(jnp.float32), w_down.astype(jnp.float32), gain_attn.astype(jnp.float32), gain_ffn.astype(jnp.float32))

    def one_sequence(totals, sequence):
        seq_rows, order_row, seed_grad = sequence
        token_place = positions(order_row)

        def forward(rows_in, *params):
            return block_forward(rows_in, *params, token_place)
        result, pullback = jax.vjp(forward, seq_rows.astype(jnp.float32), *weights)
        gradients = pullback(seed_grad.astype(jnp.float32))
        totals = tuple((running + gradient for running, gradient in zip(totals, gradients[1:])))
        return (totals, (result.astype(jnp.bfloat16), gradients[0]))
    start_totals = tuple((jnp.zeros_like(weight) for weight in weights))
    totals, outputs = lax.scan(one_sequence, start_totals, (hidden_in, block_order, cotangent))
    return (outputs[0], outputs[1], totals[0], totals[1], totals[2], totals[3], totals[4], totals[5], totals[6], totals[7])
```

```python
import jax
import jax.numpy as jnp
import numpy as np
from jax import lax
from jax.experimental import pallas as pl
from jax.experimental.pallas import tpu as pltpu
from jax.sharding import PartitionSpec as P

MESH = pl.DeviceIdType.MESH
F32 = jnp.float32
BF16 = jnp.bfloat16
EPSILON = 1e-05
NEG_FILL = -1e30
ROPE_BASE = 10000.0

D = 2048
HD = 64
T = 192
BLOCK = 96
R = 48
QC = 512
FC = 1408
KEYS = 1536
PAIRS = 4
LANES = 384
GROUP = 384
FF_TILES = ((0, 384), (384, 384), (768, 384), (1152, 256))


def rope_tables():
    half = HD // 2
    freq = ROPE_BASE ** (-np.arange(half, dtype=np.float64) / half)
    freq = np.tile(freq, 4)[None, :]
    coarse = np.arange(16, dtype=np.float64)[:, None] * BLOCK * freq
    fine = np.arange(BLOCK, dtype=np.float64)[:, None] * freq
    coarse = np.stack([np.cos(coarse), np.sin(coarse)]).astype(np.float32)
    fine = np.stack([np.cos(fine), np.sin(fine)]).astype(np.float32)
    return coarse, fine


def dot(a, b):
    return jnp.dot(a, b, preferred_element_type=F32)


def dot_nt(a, b):
    return lax.dot_general(a, b, (((1,), (1,)), ((), ())), preferred_element_type=F32)


def tiles(total, size):
    return [(s, min(size, total - s)) for s in range(0, total, size)]


def lane_of(shape):
    return lax.broadcasted_iota(jnp.int32, shape, len(shape) - 1)


def swap_halves(t):
    first = lane_of(t.shape) % HD < HD // 2
    return jnp.where(first, pltpu.roll(t, 96, 1), pltpu.roll(t, 32, 1))


def layer_kernel(
    order, x_h, c_h, wq_h, wkv_h, wo_h, wg_h, wu_h, wd_h, ga, gf, coarse, fine,
    bo, gi, g_q, g_kv, g_o, g_g, g_u, g_d, gain_a, gain_f,
    x, cot, wq, wkv, wo, wg, wu, wd, row_g, row_u, row_q, row_kv,
    xn, kvall, kk, vv, kt, vt, qst, cos_t, sin_t, s_buf, pt, ob, rl,
    zs, zr, mid, dmid, hn, da, dinner, act, act_p,
    xn_t, c_t, hn_t, xn_p, c_p, hn_p, da_p, ob_p, dqp, dqp_p, dkvp, dkvp_p,
    dkv_r, delta,
    r1f, r2f, r3f, r4f, r1a, r2a, r3a, r4a, gain_s, gain_r,
    load_sem, send_sem, recv_sem,
):
    iy = lax.axis_index("dp")
    ictx = lax.axis_index("ctx")
    iz = lax.axis_index("tensor")
    ix = ictx // 2
    core = ictx % 2
    other = 1 - core

    def z_peer(k):
        return (iy, ictx, (iz + k) % 4)

    def ctx_peer(k):
        return (iy, (ictx + k) % 8, iz)

    def x_peer(k):
        return (iy, ((ix + k) % 4) * 2 + core, iz)

    def y_peer(k):
        return ((iy + k) % 4, ictx, iz)

    core_peer = (iy, ix * 2 + other, iz)

    loads = {}

    def load(name, src, dst):
        copy = pltpu.make_async_copy(src, dst, load_sem.at[len(loads)])
        copy.start()
        loads[name] = copy

    load("x", x_h, x)
    load("wkv", wkv_h, wkv)
    load("wq", wq_h, wq)
    load("cot", c_h, cot)
    load("wd", wd_h, wd)
    load("wo", wo_h, wo)
    load("wg", wg_h, wg)
    load("wu", wu_h, wu)
    own_h, own_a, own_b = iy // 2, (iy % 2) * 2 + ix // 2, (ix % 2) * 2 + core
    load("row_g", wg_h.at[own_h, own_a, own_b], row_g)
    load("row_u", wu_h.at[own_h, own_a, own_b], row_u)
    own_rows = pl.ds(pl.multiple_of(((iy * 4 + ix) * 2 + core) * 64, 64), 64)
    load("row_q", wq_h.at[own_rows], row_q)
    load("row_kv", wkv_h.at[own_rows], row_kv)

    barrier = pltpu.get_barrier_semaphore()
    greeted = (
        [ctx_peer(k) for k in range(1, 8)]
        + [z_peer(k) for k in range(1, 4)]
        + [y_peer(1), y_peer(3)]
    )
    for peer in greeted:
        pl.semaphore_signal(barrier, inc=1, device_id=peer, device_id_type=MESH)
    pl.semaphore_wait(barrier, len(greeted))

    sent = []

    def send(src, dst, peer):
        n = len(sent)
        copy = pltpu.make_async_remote_copy(
            src_ref=src, dst_ref=dst, send_sem=send_sem.at[n], recv_sem=recv_sem.at[n],
            device_id=peer, device_id_type=MESH,
        )
        copy.start()
        sent.append(copy)
        return copy

    def wait_recv(copies):
        for copy in copies:
            copy.wait_recv()

    released = set()

    def wait_send(copies):
        for copy in copies:
            copy.wait_send()
            released.add(id(copy))

    pick = lax.broadcasted_iota(jnp.int32, (16, 128), 0)
    sign = jnp.where(lane_of((BLOCK, 128)) % HD < HD // 2, -1.0, 1.0).astype(F32)
    for b in range(2):
        chosen = pick == order[0, ictx * 2 + b]
        ca = jnp.sum(jnp.where(chosen, coarse[0], 0.0), 0, keepdims=True)
        sa = jnp.sum(jnp.where(chosen, coarse[1], 0.0), 0, keepdims=True)
        cos_t[b * BLOCK : (b + 1) * BLOCK, :] = ca * fine[0] - sa * fine[1]
        sin_t[b * BLOCK : (b + 1) * BLOCK, :] = (sa * fine[0] + ca * fine[1]) * sign

    def rot(t):
        return t * cos_t[...] + swap_halves(t) * sin_t[...]

    def rot_back(t):
        return t * cos_t[...] - swap_halves(t) * sin_t[...]

    def inv_rms(v):
        return lax.rsqrt(jnp.mean(v * v, -1, keepdims=True) + EPSILON)

    low_lane = lane_of((T, 128)) < HD

    loads["x"].wait()
    for i in range(4):
        rows = x[i].astype(F32)
        xn[i] = (rows * inv_rms(rows) * ga[...]).astype(BF16)
    loads["wkv"].wait()
    normed = xn[...].reshape(T, D)
    kvp = dot(normed, wkv[...])
    kvall[ictx] = jnp.where(low_lane, rot(kvp), kvp).astype(BF16)
    kv_copies = [send(kvall.at[ictx], kvall.at[ictx], ctx_peer(k)) for k in range(1, 8)]

    loads["wq"].wait()
    for s, n in tiles(QC, 256):
        qp = dot(normed, wq[:, s : s + n])
        for j in range(n // 128):
            p = s // 128 + j
            q = rot(qp[:, j * 128 : (j + 1) * 128]) * (HD ** -0.5)
            qst[p, 0:T, :] = jnp.where(low_lane, q, 0.0).astype(BF16)
            qst[p, T : 2 * T, :] = jnp.where(low_lane, 0.0, q).astype(BF16)

    xn_t[...] = normed.T.reshape(16, 2, 64, T)
    xnt_copy = send(xn_t.at[:, other], xn_p, core_peer)
    loads["cot"].wait()
    cot_rows = cot[...].reshape(T, D)
    c_t[...] = cot_rows.T.reshape(16, 2, 64, T)
    ct_copy = send(c_t.at[:, other], c_p, core_peer)
    loads["wd"].wait()
    for s, n in tiles(FC, 256):
        dinner[:, s : s + n] = dot_nt(cot_rows, wd[s : s + n, :])

    wait_recv(kv_copies)
    for j in range(8):
        t = kvall[j]
        wide = t.astype(F32)
        turned = pltpu.roll(wide, HD, 1)
        rows = pl.ds(j * T, T)
        kk[rows, :] = jnp.where(low_lane, wide, turned).astype(BF16)
        vv[rows, :] = jnp.where(low_lane, turned, wide).astype(BF16)
    kv_t = kvall[...].reshape(KEYS, 128).T
    kt[0:HD, :] = kv_t[0:HD]
    kt[HD : 2 * HD, :] = kv_t[0:HD]
    vt[0:HD, :] = kv_t[HD : 2 * HD]
    vt[HD : 2 * HD, :] = kv_t[HD : 2 * HD]
    vt[2 * HD : 2 * HD + 16, :] = jnp.ones((16, KEYS), BF16)

    token = lane_of((1, LANES))
    token = jnp.where(token >= T, token - T, token)
    q_place = jnp.where(
        token >= BLOCK,
        order[0, ictx * 2 + 1] * BLOCK + token - BLOCK,
        order[0, ictx * 2] * BLOCK + token,
    )
    key_row = lax.broadcasted_iota(jnp.int32, (BLOCK, LANES), 0)
    n_groups = KEYS // GROUP

    for p in range(PAIRS):

        def score_group(i, top):
            r0 = pl.multiple_of(i * GROUP, GROUP)
            scores = dot_nt(kk[pl.ds(r0, GROUP), :], qst[p])
            parts = []
            for b in range(GROUP // BLOCK):
                limit = q_place - order[0, i * (GROUP // BLOCK) + b] * BLOCK
                parts.append(
                    jnp.where(key_row <= limit, scores[b * BLOCK : (b + 1) * BLOCK], NEG_FILL)
                )
            scores = jnp.concatenate(parts, 0)
            s_buf[pl.ds(r0, GROUP), :] = scores
            return jnp.maximum(top, jnp.max(scores, 0, keepdims=True))

        top = lax.fori_loop(0, n_groups, score_group, jnp.full((1, LANES), NEG_FILL, F32))

        def weight_group(i, carry):
            r0 = pl.multiple_of(i * GROUP, GROUP)
            pt[p, pl.ds(r0, GROUP), :] = jnp.exp(s_buf[pl.ds(r0, GROUP), :] - top).astype(BF16)
            return carry

        lax.fori_loop(0, n_groups, weight_group, 0)
        summed = dot(vt[...], pt[p])
        inv = 1.0 / summed[2 * HD : 2 * HD + 1]
        out = summed[0 : 2 * HD] * inv
        pair = slice(p * 128, (p + 1) * 128)
        ob[:, pair] = jnp.where(low_lane, out[:, 0:T].T, out[:, T : 2 * T].T).astype(BF16)
        inv_wide = jnp.broadcast_to(inv, (2 * HD, LANES))
        rl[:, pair] = jnp.where(low_lane, inv_wide[:, 0:T].T, inv_wide[:, T : 2 * T].T)

    ob_copy = send(ob, ob_p, core_peer)

    def z_scatter(slot, n):
        return [
            send(slot.at[(iz + k) % 4], zr.at[n, k - 1], z_peer(k)) for k in range(1, 4)
        ]

    def z_sum(slot, n):
        total = slot[iz].astype(F32)
        for k in range(3):
            total = total + zr[n, k].astype(F32)
        return total

    def z_gather(buf):
        return [send(buf.at[iz], buf.at[iz], z_peer(k)) for k in range(1, 4)]

    loads["wo"].wait()
    rows_o = ob[...]
    for s, n in tiles(D, 512):
        zs[:, :, s : s + n] = dot(rows_o, wo[:, s : s + n]).astype(BF16).reshape(4, R, n)
    attn_copies = z_scatter(zs, 0)
    wait_recv(attn_copies)
    mid[...] = x[iz].astype(F32) + z_sum(zs, 0)
    m = mid[...]
    hn[iz] = (m * inv_rms(m) * gf[...]).astype(BF16)
    hn_copies = z_gather(hn)

    loads["wg"].wait()
    loads["wu"].wait()
    wait_recv(hn_copies)
    hidden = hn[...].reshape(T, D)
    for s, n in FF_TILES:
        cols = slice(s, s + n)
        g = dot(hidden, wg[:, :, :, :, :, cols].reshape(D, n))
        u = dot(hidden, wu[:, :, :, :, :, cols].reshape(D, n))
        sig = 1.0 / (1.0 + jnp.exp(-g))
        a = g * sig
        di = dinner[:, cols]
        act[0, :, cols] = (a * u).astype(BF16)
        act[1, :, cols] = (di * u * sig * (1.0 + g * (1.0 - sig))).astype(BF16)
        act[2, :, cols] = (di * a).astype(BF16)
    act_copies = [send(act.at[i], act_p.at[i], core_peer) for i in range(3)]

    wait_send(attn_copies)

    def dhn_tile(t, carry):
        r = dot_nt(act[1], wg[t // 4, t % 4].reshape(256, FC))
        r = r + dot_nt(act[2], wu[t // 4, t % 4].reshape(256, FC))
        zs[:, :, pl.ds(pl.multiple_of(t * 256, 256), 256)] = r.astype(BF16).reshape(4, R, 256)
        return carry

    lax.fori_loop(0, 8, dhn_tile, 0)
    dhn_copies = z_scatter(zs, 1)

    hn_t[...] = hidden.T.reshape(16, 2, 64, T)
    hnt_copy = send(hn_t.at[:, other], hn_p, core_peer)
    inner = act[0]
    for s, n in tiles(D, 512):
        xn[:, :, s : s + n] = dot(inner, wd[:, s : s + n]).astype(BF16).reshape(4, R, n)

    def weight_grad(own_t, partner_t, own_b, partner_b, ref, half, c0, n):
        a_own = own_t[:, core].reshape(1024, T)
        a_partner = partner_t[...].reshape(1024, T)
        for s, w in tiles(n, 256):
            r = dot(a_own, own_b[:, s : s + w]) + dot(a_partner, partner_b[:, s : s + w])
            ref[half, :, :, :, :, c0 + s : c0 + s + w] = r.astype(BF16).reshape(4, 4, 2, 32, w)

    xp, xm, x2 = (ix + 1) % 4, (ix + 3) % 4, (ix + 2) % 4
    yp, ym, y2 = (iy + 1) % 4, (iy + 3) % 4, (iy + 2) % 4
    f_bufs = [[r.at[i] for r in (r1f, r2f, r3f, r4f)] for i in range(3)]
    a_bufs = [r1a, r2a, r3a, r4a]
    parts = [
        (wg, 1, 0, FC, f_bufs[0], 0),
        (wg, 0, 0, FC, f_bufs[1], 0),
        (wu, 0, 0, FC, f_bufs[2], 0),
        (wu, 1, 0, 512, a_bufs, 0),
        (wu, 1, 512, 640, a_bufs, 512),
    ]
    flights = {}
    lo2, hi2, all4 = pl.ds(0, 2), pl.ds(2, 2), pl.ds(0, 4)
    all32, lo16, hi16 = pl.ds(0, 32), pl.ds(0, 16), pl.ds(16, 16)

    def g_index(part, dy, dx, h, rows=None):
        ref, half, c0, n, _, _ = parts[part]
        return (half, dy, dx, h, all32 if rows is None else rows, pl.ds(c0, n))

    def outgoing(part, step):
        if step == 0:
            return (
                (g_index(part, lo2, x2, 0), g_index(part, hi2, x2, 0)),
                (g_index(part, y2, lo2, 1), g_index(part, y2, hi2, 1)),
            )
        if step == 1:
            return (
                (g_index(part, all4, xp, 0), g_index(part, all4, xm, 0)),
                (g_index(part, yp, all4, 1), g_index(part, ym, all4, 1)),
            )
        if step == 2:
            return (
                (g_index(part, y2, ix, 0, lo16), g_index(part, y2, ix, 0, hi16)),
                (g_index(part, iy, x2, 1, lo16), g_index(part, iy, x2, 1, hi16)),
            )
        return (
            (g_index(part, yp, ix, 0), g_index(part, ym, ix, 0)),
            (g_index(part, iy, xp, 1), g_index(part, iy, xm, 1)),
        )

    def landing(part, step, flow, way):
        _, _, _, n, bufs, b0 = parts[part]
        return bufs[step].at[flow, way, ..., pl.ds(b0, n)]

    def rs_send(part, step):
        ref = parts[part][0]
        out = outgoing(part, step)
        for flow in range(2):
            along_x = (flow == 0) == (step < 2)
            for way, k in ((0, 1), (1, 3)):
                peer = x_peer(k) if along_x else y_peer(k)
                flights[part, step, flow, way] = send(
                    ref.at[out[flow][way]], landing(part, step, flow, way), peer
                )

    def add_in(ref, index, *arrived):
        total = ref[index].astype(F32)
        for a in arrived:
            total = total + a[...].astype(F32)
        ref[index] = total.astype(BF16)

    def rs_recv(part, step):
        ref = parts[part][0]
        for flow in range(2):
            wait_recv([flights[part, step, flow, way] for way in range(2)])
            got = [landing(part, step, flow, way) for way in range(2)]
            if step == 0:
                if flow == 0:
                    add_in(ref, g_index(part, lo2, xp, 0), got[0])
                    add_in(ref, g_index(part, hi2, xm, 0), got[1])
                else:
                    add_in(ref, g_index(part, yp, lo2, 1), got[0])
                    add_in(ref, g_index(part, ym, hi2, 1), got[1])
            elif step == 1:
                if flow == 0:
                    add_in(ref, g_index(part, all4, ix, 0), *got)
                else:
                    add_in(ref, g_index(part, iy, all4, 1), *got)
            elif step == 2:
                if flow == 0:
                    add_in(ref, g_index(part, yp, ix, 0, lo16), got[0])
                    add_in(ref, g_index(part, ym, ix, 0, hi16), got[1])
                else:
                    add_in(ref, g_index(part, iy, xp, 1, lo16), got[0])
                    add_in(ref, g_index(part, iy, xm, 1, hi16), got[1])

    def rs_turn(part, step):
        rs_recv(part, step)
        rs_send(part, step + 1)

    def rs_last(part, outs):
        rs_recv(part, 3)
        ref = parts[part][0]
        for flow in range(2):
            total = ref[g_index(part, iy, ix, flow)].astype(F32)
            for way in range(2):
                total = total + landing(part, 3, flow, way)[...].astype(F32)
            for out, s, n in outs:
                out[flow * 32 : (flow + 1) * 32, :] = total[:, s : s + n]

    wait_recv([ct_copy, act_copies[0]])
    weight_grad(c_t, c_p, act.at[0], act_p.at[0], wg, 1, 0, FC)
    rs_send(0, 0)
    wait_recv([hnt_copy, act_copies[1]])
    weight_grad(hn_t, hn_p, act.at[1], act_p.at[1], wg, 0, 0, FC)
    rs_send(1, 0)
    wait_recv([act_copies[2]])
    weight_grad(hn_t, hn_p, act.at[2], act_p.at[2], wu, 0, 0, FC)
    rs_send(2, 0)

    wait_recv(dhn_copies)
    m = mid[...]
    r2 = inv_rms(m)
    mhat = m * r2
    scaled = z_sum(zs, 1) * gf[...]
    dm = cot[iz].astype(F32) + r2 * (
        scaled - mhat * jnp.mean(scaled * mhat, -1, keepdims=True)
    )
    dmid[...] = dm
    da[iz] = dm.astype(BF16)
    da_copies = z_gather(da)
    ffn_copies = z_scatter(xn, 2)

    rs_turn(0, 0)
    rs_turn(1, 0)
    rs_turn(2, 0)

    wait_recv(da_copies)
    grad_attn = da[...].reshape(T, D)
    for s, n in tiles(QC, 256):
        grad_rows = dot_nt(grad_attn, wo[s : s + n, :])
        for j in range(n // 128):
            p = s // 128 + j
            pair = slice(p * 128, (p + 1) * 128)
            g = grad_rows[:, j * 128 : (j + 1) * 128] * rl[:, pair]
            dob = kk.at[p * LANES : (p + 1) * LANES]
            dob[0:T, :] = jnp.where(low_lane, g, 0.0).astype(BF16)
            dob[T : 2 * T, :] = jnp.where(low_lane, 0.0, g).astype(BF16)
            by_row = (g * ob[:, pair].astype(F32)).T
            delta[p] = jnp.concatenate(
                [
                    jnp.sum(by_row[0:HD], 0, keepdims=True),
                    jnp.sum(by_row[HD : 2 * HD], 0, keepdims=True),
                ],
                1,
            )
    wait_send([ct_copy])
    c_t[...] = grad_attn.T.reshape(16, 2, 64, T)
    dat_copy = send(c_t.at[:, other], da_p, core_peer)

    wait_send(kv_copies)
    for p in range(PAIRS):
        dob = kk.at[p * LANES : (p + 1) * LANES]

        def grad_group(i, carry):
            r0 = pl.multiple_of(i * GROUP, GROUP)
            rows = pl.ds(r0, GROUP)
            weights = pt[p, rows, :]
            grad_weights = dot_nt(vv[rows, :], dob[...])
            grad_scores = (weights.astype(F32) * (grad_weights - delta[p])).astype(BF16)
            pt[p, rows, :] = grad_scores
            dv = dot(weights, dob[...])
            dk = dot(grad_scores, qst[p])
            if p > 0:
                dk = dk + s_buf[rows, 0:128]
                dv = dv + s_buf[rows, 128:256]
            s_buf[rows, 0:128] = dk
            s_buf[rows, 128:256] = dv
            return carry

        lax.fori_loop(0, n_groups, grad_group, 0)
        dq = dot(kt[...], pt[p]) * (HD ** -0.5)
        dq = jnp.where(low_lane, dq[:, 0:T].T, dq[:, T : 2 * T].T)
        dqp[:, p * 128 : (p + 1) * 128] = rot_back(dq).astype(BF16)

    for j in range(8):
        rows = slice(j * T, (j + 1) * T)
        dk, dv = s_buf[rows, 0:128], s_buf[rows, 128:256]
        kvall[j] = jnp.where(
            low_lane, dk + pltpu.roll(dk, HD, 1), dv + pltpu.roll(dv, HD, 1)
        ).astype(BF16)
    dkv_copies = [
        send(kvall.at[(ictx + k) % 8], dkv_r.at[k - 1], ctx_peer(k)) for k in range(1, 8)
    ]
    dqp_copy = send(dqp, dqp_p, core_peer)

    wait_recv(ffn_copies)
    bo[iz] = (mid[...] + z_sum(xn, 2)).astype(BF16)
    bo_copies = z_gather(bo)

    wait_recv([dat_copy, ob_copy])
    weight_grad(c_t, da_p, ob, ob_p, wu, 1, 0, 512)
    rs_send(3, 0)
    rs_turn(0, 1)

    wait_recv(dkv_copies)
    home = kvall[ictx].astype(F32)
    for k in range(7):
        home = home + dkv_r[k].astype(F32)
    dkvp[...] = jnp.where(low_lane, rot_back(home), home).astype(BF16)
    dkvp_copy = send(dkvp, dkvp_p, core_peer)
    wait_send(dhn_copies)
    q_rows, kv_rows = dqp[...], dkvp[...]
    for s, n in tiles(D, 512):
        r = dot_nt(q_rows, wq[s : s + n, :]) + dot_nt(kv_rows, wkv[s : s + n, :])
        zs[:, :, s : s + n] = r.astype(BF16).reshape(4, R, n)
    dxn_copies = z_scatter(zs, 3)

    wait_recv([xnt_copy, dqp_copy])
    weight_grad(xn_t, xn_p, dqp, dqp_p, wu, 1, 512, 512)
    wait_recv([dkvp_copy])
    weight_grad(xn_t, xn_p, dkvp, dkvp_p, wu, 1, 1024, 128)
    rs_send(4, 0)
    rs_turn(1, 1)

    wait_recv(dxn_copies)
    rows = x[iz].astype(F32)
    r1 = inv_rms(rows)
    xhat = rows * r1
    scaled = z_sum(zs, 3) * ga[...]
    gi[iz] = (
        dmid[...] + r1 * (scaled - xhat * jnp.mean(scaled * xhat, -1, keepdims=True))
    ).astype(BF16)
    gi_copies = z_gather(gi)

    rs_turn(2, 1)
    rs_turn(3, 0)
    rs_turn(4, 0)
    rs_turn(0, 2)
    rs_turn(1, 2)
    rs_turn(2, 2)
    rs_turn(3, 1)
    rs_turn(4, 1)
    rs_turn(3, 2)
    rs_turn(4, 2)
    rs_last(0, [(g_d, 0, FC)])
    rs_last(1, [(g_g, 0, FC)])
    rs_last(2, [(g_u, 0, FC)])
    rs_last(3, [(g_o, 0, 512)])
    rs_last(4, [(g_q, 0, 512), (g_kv, 512, 128)])

    for name in ("row_g", "row_u", "row_q", "row_kv"):
        loads[name].wait()

    def row_products(pairs):
        total = jnp.zeros((64, 128), F32)
        for grad, weight in pairs:
            n = grad.shape[-1]
            w = weight[...].reshape(64, n)
            for s, _ in tiles(n, 128):
                total = total + grad[:, s : s + 128] * w[:, s : s + 128].astype(F32)
        return jnp.sum(total.T, 0, keepdims=True)

    gain_s[...] = jnp.zeros((8, 128), F32)
    gain_s[0:1, 0:64] = row_products([(g_g, row_g), (g_u, row_u)])
    gain_s[1:2, 0:64] = row_products([(g_q, row_q), (g_kv, row_kv)])
    gain_copies = [send(gain_s, gain_r.at[k - 1], z_peer(k)) for k in range(1, 4)]
    wait_recv(gain_copies)
    total = gain_s[...]
    for k in range(3):
        total = total + gain_r[k]
    chip_cols = pl.ds(pl.multiple_of((iy * 4 + ix) * 128, 128), 128)

    def own_gain(ref):
        v = ref[:, chip_cols]
        return jnp.where(core == 1, pltpu.roll(v, 64, 1), v)[:, 0:64]

    gain_f[...] = total[0:1, 0:64] / own_gain(gf)
    gain_a[...] = total[1:2, 0:64] / own_gain(ga)

    wait_recv(bo_copies)
    wait_recv(gi_copies)
    wait_send([copy for copy in sent if id(copy) not in released])


N_SENDS = 131


def per_device(
    hidden_in, block_order, w_query, w_keyval, w_output, w_gate, w_up, w_down,
    gain_attn, gain_ffn, cotangent,
):
    coarse, fine = rope_tables()
    any_spec = pl.BlockSpec(memory_space=pl.ANY)
    vmem = pl.BlockSpec(memory_space=pltpu.VMEM)
    smem = pl.BlockSpec(memory_space=pltpu.SMEM)
    shape = jax.ShapeDtypeStruct
    wide = (2, 4, 4, 2, 32, FC)
    turned = (16, 2, 64, T)
    half_turned = (16, 64, T)
    scratch = [
        pltpu.VMEM(s, t)
        for s, t in (
            ((4, R, D), BF16), ((4, R, D), BF16),
            ((D, QC), BF16), ((D, 128), BF16), ((QC, D), BF16),
            (wide, BF16), (wide, BF16), ((FC, D), BF16),
            ((2, 32, FC), BF16), ((2, 32, FC), BF16), ((64, QC), BF16), ((64, 128), BF16),
            ((4, R, D), BF16), ((8, T, 128), BF16),
            ((KEYS, 128), BF16), ((KEYS, 128), BF16),
            ((128, KEYS), BF16), ((144, KEYS), BF16),
            ((PAIRS, LANES, 128), BF16), ((T, 128), F32), ((T, 128), F32),
            ((KEYS, LANES), F32), ((PAIRS, KEYS, LANES), BF16),
            ((T, QC), BF16), ((T, QC), F32),
            ((4, R, D), BF16), ((4, 3, R, D), BF16),
            ((R, D), F32), ((R, D), F32),
            ((4, R, D), BF16), ((4, R, D), BF16), ((T, FC), F32),
            ((3, T, FC), BF16), ((3, T, FC), BF16),
            (turned, BF16), (turned, BF16), (turned, BF16),
            (half_turned, BF16), (half_turned, BF16), (half_turned, BF16), (half_turned, BF16),
            ((T, QC), BF16), ((T, QC), BF16), ((T, QC), BF16),
            ((T, 128), BF16), ((T, 128), BF16),
            ((7, T, 128), BF16),
            ((PAIRS, 1, LANES), F32),
            ((3, 2, 2, 2, 32, FC), BF16), ((3, 2, 2, 4, 32, FC), BF16),
            ((3, 2, 2, 16, FC), BF16), ((3, 2, 2, 32, FC), BF16),
            ((2, 2, 2, 32, 1152), BF16), ((2, 2, 4, 32, 1152), BF16),
            ((2, 2, 16, 1152), BF16), ((2, 2, 32, 1152), BF16),
            ((8, 128), F32), ((3, 8, 128), F32),
        )
    ] + [
        pltpu.SemaphoreType.DMA((12,)),
        pltpu.SemaphoreType.DMA((N_SENDS,)),
        pltpu.SemaphoreType.DMA((N_SENDS,)),
    ]
    outs = pl.pallas_call(
        layer_kernel,
        out_shape=(
            shape((4, R, D), BF16), shape((4, R, D), BF16),
            shape((64, QC), F32), shape((64, 128), F32), shape((64, QC), F32),
            shape((64, FC), F32), shape((64, FC), F32), shape((64, FC), F32),
            shape((1, 64), F32), shape((1, 64), F32),
        ),
        in_specs=[smem] + [any_spec] * 8 + [vmem] * 4,
        out_specs=(vmem,) * 10,
        scratch_shapes=scratch,
        compiler_params=pltpu.CompilerParams(
            collective_id=0, has_side_effects=True, vmem_limit_bytes=65200 * 1024
        ),
    )(
        block_order, hidden_in.reshape(4, R, D), cotangent.reshape(4, R, D),
        w_query, w_keyval, w_output, w_gate.reshape(wide), w_up.reshape(wide), w_down,
        gain_attn.reshape(1, D), gain_ffn.reshape(1, D), coarse, fine,
    )
    bo, gi, g_q, g_kv, g_o, g_g, g_u, g_d, gain_a, gain_f = outs
    return (
        bo.reshape(1, T, D),
        gi.reshape(1, T, D).astype(F32),
        g_q,
        g_kv,
        g_o.T,
        g_g,
        g_u,
        g_d.T,
        gain_a.reshape(64),
        gain_f.reshape(64),
    )


def solution(mesh):
    return jax.shard_map(
        per_device,
        mesh=mesh,
        in_specs=(
            P("dp", "ctx", None),
            P("dp", None),
            P(None, "tensor"),
            P(None, "tensor"),
            P("tensor", None),
            P(None, "tensor"),
            P(None, "tensor"),
            P("tensor", None),
            P(),
            P(),
            P("dp", "ctx", None),
        ),
        out_specs=(
            P("dp", "ctx", None),
            P("dp", "ctx", None),
            P(("dp", "ctx"), "tensor"),
            P(("dp", "ctx"), "tensor"),
            P("tensor", ("dp", "ctx")),
            P(("dp", "ctx"), "tensor"),
            P(("dp", "ctx"), "tensor"),
            P("tensor", ("dp", "ctx")),
            P(("dp", "ctx")),
            P(("dp", "ctx")),
        ),
        check_vma=False,
    )
```

```python
import jax
import jax.numpy as jnp
import numpy as np
from jax import lax
from jax.experimental import pallas as pl
from jax.experimental.pallas import tpu as pltpu
from jax.sharding import PartitionSpec as P

MESH = pl.DeviceIdType.MESH
F32 = jnp.float32
BF16 = jnp.bfloat16
EPSILON = 1e-05
NEG_FILL = -1e30
ROPE_BASE = 10000.0

D = 2048
HD = 64
T = 192
BLOCK = 96
TA = 128
R = 48
QC = 512
FC = 1408
KEYS = 1536
PAIRS = 4
QUERIES = 1536
CHUNK = 512
GROUP = 768
CHIP_KEYS = 384
FF_TILES = ((0, 384), (384, 384), (768, 384), (1152, 256))


def rope_tables():
    half = HD // 2
    freq = ROPE_BASE ** (-np.arange(half, dtype=np.float64) / half)
    freq = np.tile(freq, 4)[None, :]
    coarse = np.arange(16, dtype=np.float64)[:, None] * BLOCK * freq
    fine = np.arange(BLOCK, dtype=np.float64)[:, None] * freq
    coarse = np.stack([np.cos(coarse), np.sin(coarse)]).astype(np.float32)
    fine = np.stack([np.cos(fine), np.sin(fine)]).astype(np.float32)
    return coarse, fine


def dot(a, b):
    return jnp.dot(a, b, preferred_element_type=F32)


def dot_nt(a, b):
    return lax.dot_general(a, b, (((1,), (1,)), ((), ())), preferred_element_type=F32)


def tiles(total, size):
    return [(s, min(size, total - s)) for s in range(0, total, size)]


def lane_of(shape):
    return lax.broadcasted_iota(jnp.int32, shape, len(shape) - 1)


def swap_halves(t):
    first = lane_of(t.shape) % HD < HD // 2
    return jnp.where(first, pltpu.roll(t, 96, 1), pltpu.roll(t, 32, 1))


def layer_kernel(
    order, x_h, c_h, wq_h, wkv_h, wo_h, wg_h, wu_h, wd_h, ga, gf, coarse, fine,
    bo, gi, o_q, o_kv, o_o, o_g, o_u, o_d, gain_a, gain_f,
    x, cot, wq, wkv, wo, wg, wu, wd, row_g, row_u, row_q, row_kv,
    xn, kvall, kk, vv, kt, vt, qst, cos_t, sin_t, s_buf, pt, ob, rl,
    zs, zr, mid, dmid, hn, da, bo_s, gi_s, dinner, act, act_p, g_first,
    xn_t, c_t, hn_t, xn_p, c_p, hn_p, da_p, ob_p, dqp, dqp_p, dkvp, dkvp_p,
    dkv_r, delta, r1f, r2f, r3f, r4f, r1a, r2a, r3a, r4a,
    g_q, g_kv, g_o, g_g, g_u, g_d, gain_s, gain_r,
    local_sem, send_sem, recv_sem,
):
    iy = lax.axis_index("dp")
    ictx = lax.axis_index("ctx")
    iz = lax.axis_index("tensor")
    ix = ictx // 2
    core = ictx % 2
    other = 1 - core

    def z_peer(k):
        return (iy, ictx, (iz + k) % 4)

    def ctx_peer(k):
        return (iy, (ictx + k) % 8, iz)

    def x_peer(k):
        return (iy, ((ix + k) % 4) * 2 + core, iz)

    def y_peer(k):
        return ((iy + k) % 4, ictx, iz)

    core_peer = (iy, ix * 2 + other, iz)

    local = []
    local_done = set()

    def copy_local(src, dst):
        copy = pltpu.make_async_copy(src, dst, local_sem.at[len(local)])
        copy.start()
        local.append(copy)
        return copy

    def wait_local(*copies):
        for copy in copies:
            copy.wait()
            local_done.add(id(copy))

    x_load = copy_local(x_h, x)
    wkv_load = copy_local(wkv_h, wkv)
    wq_load = copy_local(wq_h, wq)

    barrier = pltpu.get_barrier_semaphore()
    greeted = (
        [ctx_peer(k) for k in range(1, 8)]
        + [z_peer(k) for k in range(1, 4)]
        + [y_peer(1), y_peer(3)]
    )
    for peer in greeted:
        pl.semaphore_signal(barrier, inc=1, device_id=peer, device_id_type=MESH)

    sent = []
    arrived, released = set(), set()

    def send(src, dst, peer):
        n = len(sent)
        copy = pltpu.make_async_remote_copy(
            src_ref=src, dst_ref=dst, send_sem=send_sem.at[n], recv_sem=recv_sem.at[n],
            device_id=peer, device_id_type=MESH,
        )
        copy.start()
        sent.append(copy)
        return copy

    def wait_recv(copies):
        for copy in copies:
            copy.wait_recv()
            arrived.add(id(copy))

    def wait_send(copies):
        for copy in copies:
            copy.wait_send()
            released.add(id(copy))

    pick = lax.broadcasted_iota(jnp.int32, (16, 128), 0)
    sign = jnp.where(lane_of((BLOCK, 128)) % HD < HD // 2, -1.0, 1.0).astype(F32)
    for b in range(2):
        chosen = pick == order[0, ictx * 2 + b]
        ca = jnp.sum(jnp.where(chosen, coarse[0], 0.0), 0, keepdims=True)
        sa = jnp.sum(jnp.where(chosen, coarse[1], 0.0), 0, keepdims=True)
        cos_t[b * BLOCK : (b + 1) * BLOCK, :] = ca * fine[0] - sa * fine[1]
        sin_t[b * BLOCK : (b + 1) * BLOCK, :] = (sa * fine[0] + ca * fine[1]) * sign

    def rot(t):
        return t * cos_t[...] + swap_halves(t) * sin_t[...]

    def rot_back(t):
        return t * cos_t[...] - swap_halves(t) * sin_t[...]

    def inv_rms(v):
        return lax.rsqrt(jnp.mean(v * v, -1, keepdims=True) + EPSILON)

    low_lane = lane_of((T, 128)) < HD
    low_a, low_b = low_lane[0:TA], low_lane[0 : T - TA]

    wait_local(x_load)
    for i in range(4):
        rows = x[i * R : (i + 1) * R, :].astype(F32)
        xn[i * R : (i + 1) * R, :] = (rows * inv_rms(rows) * ga[...]).astype(BF16)
    wait_local(wkv_load)
    cot_load = copy_local(c_h, cot)
    wd_load = copy_local(wd_h, wd)
    normed = xn[...]
    kvp = dot(normed, wkv[...])
    kvall[ictx] = jnp.where(low_lane, rot(kvp), kvp).astype(BF16)
    pl.semaphore_wait(barrier, len(greeted))
    kv_copies = [send(kvall.at[ictx], kvall.at[ictx], ctx_peer(k)) for k in range(1, 8)]
    wait_local(wq_load)
    wo_load = copy_local(wo_h, wo)
    wg_load = copy_local(wg_h, wg)
    wu_load = copy_local(wu_h, wu)
    own_h, own_a, own_b = iy // 2, (iy % 2) * 2 + ix // 2, (ix % 2) * 2 + core
    own_rows = pl.ds(pl.multiple_of(((iy * 4 + ix) * 2 + core) * 64, 64), 64)
    row_loads = [
        copy_local(wg_h.at[own_h, own_a, own_b], row_g),
        copy_local(wu_h.at[own_h, own_a, own_b], row_u),
        copy_local(wq_h.at[own_rows], row_q),
        copy_local(wkv_h.at[own_rows], row_kv),
    ]

    def by_query(pair, value, ref):
        for i in range(2):
            h = pair * 2 + i
            one = jnp.where(low_lane, value, 0.0) if i == 0 else jnp.where(low_lane, 0.0, value)
            one = one.astype(BF16)
            ref[h * TA : (h + 1) * TA, :] = one[0:TA]
            ref[8 * TA + h * 64 : 8 * TA + (h + 1) * 64, :] = one[TA:T]

    for s, n in tiles(QC, 256):
        qp = dot(normed, wq[:, s : s + n])
        for j in range(n // 128):
            by_query(s // 128 + j, rot(qp[:, j * 128 : (j + 1) * 128]) * (HD ** -0.5), qst)

    turned = (4, 4, 2, 2, 32, T)
    xn_t[...] = normed.T.reshape(turned)
    xnt_copy = send(xn_t.at[:, :, other], xn_p, core_peer)
    wait_local(cot_load)
    cot_rows = cot[...]
    c_t[...] = cot_rows.T.reshape(turned)
    ct_copy = send(c_t.at[:, :, other], c_p, core_peer)
    wait_local(wd_load)
    for s, n in tiles(FC, 512):
        dinner[:, s : s + n] = dot_nt(cot_rows, wd[s : s + n, :])

    wait_recv(kv_copies)
    for j in range(8):
        wide = kvall[j].astype(F32)
        rolled = pltpu.roll(wide, HD, 1)
        rows = pl.ds(j * T, T)
        kk[rows, :] = jnp.where(low_lane, wide, rolled).astype(BF16)
        vv[rows, :] = jnp.where(low_lane, rolled, wide).astype(BF16)
    kv_t = kvall[...].reshape(KEYS, 128).T
    kt[0:HD, :] = kv_t[0:HD]
    kt[HD : 2 * HD, :] = kv_t[0:HD]
    vt[0:HD, :] = kv_t[HD : 2 * HD]
    vt[HD : 2 * HD, :] = kv_t[HD : 2 * HD]
    vt[2 * HD : 2 * HD + 16, :] = jnp.ones((16, KEYS), BF16)

    lane = lane_of((1, CHUNK))
    token = lane % TA
    start_0, start_1 = order[0, ictx * 2] * BLOCK, order[0, ictx * 2 + 1] * BLOCK
    place_a = jnp.where(token >= BLOCK, start_1 + token - BLOCK, start_0 + token)
    place_b = start_1 + (TA - BLOCK) + lane % 64
    key_row = lax.broadcasted_iota(jnp.int32, (BLOCK, CHUNK), 0)

    def attend(chunk):
        q_place = place_a if chunk < 2 else place_b
        lanes = slice(chunk * CHUNK, (chunk + 1) * CHUNK)
        top = jnp.full((8, CHUNK), NEG_FILL, F32)
        for r0 in range(0, KEYS, GROUP):
            scores = dot_nt(kk[r0 : r0 + GROUP, :], qst[lanes, :])
            for b in range(GROUP // BLOCK):
                limit = q_place - order[0, r0 // BLOCK + b] * BLOCK
                rows = slice(b * BLOCK, (b + 1) * BLOCK)
                seen = jnp.where(key_row <= limit, scores[rows], NEG_FILL)
                s_buf[r0 + b * BLOCK : r0 + (b + 1) * BLOCK, :] = seen
                top = jnp.maximum(top, jnp.max(seen.reshape(BLOCK // 8, 8, CHUNK), 0))
        top = jnp.max(top, 0, keepdims=True)
        for r0 in range(0, KEYS, GROUP):
            rows = slice(r0, r0 + GROUP)
            pt[rows, lanes] = jnp.exp(s_buf[rows, :] - top).astype(BF16)
        summed = dot(vt[...], pt[:, lanes])
        inv = 1.0 / summed[2 * HD : 2 * HD + 1]
        out = summed[0 : 2 * HD] * inv
        inv = jnp.broadcast_to(inv, (2 * HD, CHUNK))
        if chunk < 2:
            for j in range(2):
                pair = slice((chunk * 2 + j) * 128, (chunk * 2 + j + 1) * 128)
                one, two = slice(j * 256, j * 256 + 128), slice(j * 256 + 128, j * 256 + 256)
                ob[0:TA, pair] = jnp.where(low_a, out[:, one].T, out[:, two].T).astype(BF16)
                rl[0:TA, pair] = jnp.where(low_a, inv[:, one].T, inv[:, two].T)
        else:
            for p in range(PAIRS):
                pair = slice(p * 128, (p + 1) * 128)
                o2, i2 = out[:, pair].T, inv[:, pair].T
                ob[TA:T, pair] = jnp.where(low_b, o2[0:64], o2[64:128]).astype(BF16)
                rl[TA:T, pair] = jnp.where(low_b, i2[0:64], i2[64:128])

    def z_rows(part, z):
        if part == 0:
            return pl.ds(pl.multiple_of(z * 32, 32), 32)
        return pl.ds(pl.multiple_of(TA + z * 16, 16), 16)

    kept = (slice(0, 32), slice(32, 48))
    all_cols = pl.ds(0, D)

    def z_scatter(src, n, part, cols=all_cols):
        return [
            send(
                src.at[z_rows(part, (iz + k) % 4), cols], zr.at[n, k - 1, kept[part], cols],
                z_peer(k),
            )
            for k in (2, 1, 3)
        ]

    def z_sum(src, n, part):
        total = src[z_rows(part, iz), :].astype(F32)
        for k in range(3):
            total = total + zr[n, k, kept[part], :].astype(F32)
        return total

    def z_gather(buf, part, own=None):
        rows = z_rows(part, iz)
        src = buf.at[rows] if own is None else own.at[kept[part]]
        return [send(src, buf.at[rows], z_peer(k)) for k in (2, 1, 3)]

    def project_out(part):
        rows = slice(0, TA) if part == 0 else slice(TA, T)
        copies = []
        for s, n in tiles(D, 1024):
            zs[rows, s : s + n] = dot(ob[rows, :], wo[:, s : s + n]).astype(BF16)
            copies += z_scatter(zs, 0, part, pl.ds(s, n))
        return copies

    attend(0)
    attend(1)
    wait_local(wo_load)
    attn_copies = [project_out(0)]
    attend(2)
    attn_copies.append(project_out(1))
    ob_copy = send(ob, ob_p, core_peer)

    hn_copies = []
    for part in range(2):
        wait_recv(attn_copies[part])
        m = x[z_rows(part, iz), :].astype(F32) + z_sum(zs, 0, part)
        mid[kept[part], :] = m
        hn[z_rows(part, iz), :] = (m * inv_rms(m) * gf[...]).astype(BF16)
        hn_copies += z_gather(hn, part)

    wait_local(wg_load, wu_load)
    wait_recv(hn_copies)
    hidden = hn[...]
    act_copies = [[], [], []]
    for s, n in FF_TILES:
        cols = slice(s, s + n)
        g = dot(hidden, wg[:, :, :, :, :, cols].reshape(D, n))
        u = dot(hidden, wu[:, :, :, :, :, cols].reshape(D, n))
        sig = 1.0 / (1.0 + jnp.exp(-g))
        a = g * sig
        di = dinner[:, cols]
        act[0, :, cols] = (a * u).astype(BF16)
        act[1, :, cols] = (di * u * sig * (1.0 + g * (1.0 - sig))).astype(BF16)
        act[2, :, cols] = (di * a).astype(BF16)
        for i in range(3):
            act_copies[i].append(
                send(act.at[i, :, pl.ds(s, n)], act_p.at[i, :, pl.ds(s, n)], core_peer)
            )

    xp, xm, x2 = (ix + 1) % 4, (ix + 3) % 4, (ix + 2) % 4
    yp, ym, y2 = (iy + 1) % 4, (iy + 3) % 4, (iy + 2) % 4

    def own_part(ref):
        return lambda dy, dx, h: ref[dy, dx, core, h]

    def partner_part(ref):
        return lambda dy, dx, h: ref[dy, dx, h]

    all4 = pl.ds(0, 4)
    first_rows = [(all4, x2, 0), (y2, all4, 1)]
    other_rows = [(all4, dx, 0) for dx in (xp, xm, ix)] + [(dy, all4, 1) for dy in (yp, ym, iy)]

    def weight_grad(part, which, own_t, partner_t, own_b, partner_b, store=None, c0=0, n=None):
        ref, half, part_c0, part_n, _, _ = parts[part]
        n = part_n if n is None else n
        get_own, get_partner = own_part(own_t), partner_part(partner_t)
        a_own = jnp.concatenate([get_own(*i).reshape(128, T) for i in which], 0)
        a_partner = jnp.concatenate([get_partner(*i).reshape(128, T) for i in which], 0)
        for s, w in tiles(n, 256):
            r = dot(a_own, own_b[:, s : s + w]) + dot(a_partner, partner_b[:, s : s + w])
            r = r.astype(BF16)
            cols = slice(part_c0 + c0 + s, part_c0 + c0 + s + w)
            for i, (dy, dx, h) in enumerate(which):
                rows = r[i * 128 : (i + 1) * 128].reshape(4, 32, w)
                if store is None:
                    ref[half, dy, dx, h, :, cols] = rows
                else:
                    store[i, :, :, cols] = rows

    f_bufs = [[r.at[i] for r in (r1f, r2f, r3f, r4f)] for i in range(3)]
    a_bufs = [r1a, r2a, r3a, r4a]
    parts = [
        (wg, 1, 0, FC, f_bufs[0], 0),
        (wg, 0, 0, FC, f_bufs[1], 0),
        (wu, 0, 0, FC, f_bufs[2], 0),
        (wu, 1, 0, 512, a_bufs, 0),
        (wu, 1, 512, 640, a_bufs, 512),
    ]
    flights = {}
    lo2, hi2 = pl.ds(0, 2), pl.ds(2, 2)
    all32, lo16, hi16 = pl.ds(0, 32), pl.ds(0, 16), pl.ds(16, 16)

    def g_index(part, dy, dx, h, rows=None):
        ref, half, c0, n, _, _ = parts[part]
        return (half, dy, dx, h, all32 if rows is None else rows, pl.ds(c0, n))

    def outgoing(part, step):
        if step == 0 and part == 0:
            return (
                (g_first.at[0, lo2], g_first.at[0, hi2]),
                (g_first.at[1, lo2], g_first.at[1, hi2]),
            )
        if step == 0:
            index = (
                (g_index(part, lo2, x2, 0), g_index(part, hi2, x2, 0)),
                (g_index(part, y2, lo2, 1), g_index(part, y2, hi2, 1)),
            )
        elif step == 1:
            index = (
                (g_index(part, all4, xp, 0), g_index(part, all4, xm, 0)),
                (g_index(part, yp, all4, 1), g_index(part, ym, all4, 1)),
            )
        elif step == 2:
            index = (
                (g_index(part, y2, ix, 0, lo16), g_index(part, y2, ix, 0, hi16)),
                (g_index(part, iy, x2, 1, lo16), g_index(part, iy, x2, 1, hi16)),
            )
        else:
            index = (
                (g_index(part, yp, ix, 0), g_index(part, ym, ix, 0)),
                (g_index(part, iy, xp, 1), g_index(part, iy, xm, 1)),
            )
        ref = parts[part][0]
        return tuple(tuple(ref.at[i] for i in flow) for flow in index)

    def landing(part, step, flow, way):
        _, _, _, n, bufs, b0 = parts[part]
        return bufs[step].at[flow, way, ..., pl.ds(b0, n)]

    def rs_send(part, step):
        out = outgoing(part, step)
        for flow in range(2):
            along_x = (flow == 0) == (step < 2)
            for way, k in ((0, 1), (1, 3)):
                peer = x_peer(k) if along_x else y_peer(k)
                flights[part, step, flow, way] = send(
                    out[flow][way], landing(part, step, flow, way), peer
                )

    def add_in(ref, index, *arrived):
        total = ref[index].astype(F32)
        for a in arrived:
            total = total + a[...].astype(F32)
        ref[index] = total.astype(BF16)

    def rs_recv(part, step):
        ref = parts[part][0]
        for flow in range(2):
            wait_recv([flights[part, step, flow, way] for way in range(2)])
            got = [landing(part, step, flow, way) for way in range(2)]
            if step == 0:
                if flow == 0:
                    add_in(ref, g_index(part, lo2, xp, 0), got[0])
                    add_in(ref, g_index(part, hi2, xm, 0), got[1])
                else:
                    add_in(ref, g_index(part, yp, lo2, 1), got[0])
                    add_in(ref, g_index(part, ym, hi2, 1), got[1])
            elif step == 1:
                if flow == 0:
                    add_in(ref, g_index(part, all4, ix, 0), *got)
                else:
                    add_in(ref, g_index(part, iy, all4, 1), *got)
            elif step == 2:
                if flow == 0:
                    add_in(ref, g_index(part, yp, ix, 0, lo16), got[0])
                    add_in(ref, g_index(part, ym, ix, 0, hi16), got[1])
                else:
                    add_in(ref, g_index(part, iy, xp, 1, lo16), got[0])
                    add_in(ref, g_index(part, iy, xm, 1, hi16), got[1])

    def rs_turn(part, step):
        rs_recv(part, step)
        rs_send(part, step + 1)

    def rs_last(part, outs):
        rs_recv(part, 3)
        ref = parts[part][0]
        for flow in range(2):
            total = ref[g_index(part, iy, ix, flow)].astype(F32)
            for way in range(2):
                total = total + landing(part, 3, flow, way)[...].astype(F32)
            for stage, out, s, n in outs:
                stage[flow * 32 : (flow + 1) * 32, :] = total[:, s : s + n]
        for stage, out, s, n in outs:
            copy_local(stage, out)

    hn_t[...] = hidden.T.reshape(turned)
    hnt_copy = send(hn_t.at[:, :, other], hn_p, core_peer)
    wait_recv([ct_copy] + act_copies[0])
    weight_grad(0, first_rows, c_t, c_p, act.at[0], act_p.at[0], store=g_first)
    rs_send(0, 0)

    wait_send([copy for copies in attn_copies for copy in copies])
    dhn_copies = [[], []]
    for t in range(4):
        cols = slice(t * 512, (t + 1) * 512)
        block = (t // 2, slice((t % 2) * 2, (t % 2) * 2 + 2))
        r = dot_nt(act[1], wg[block].reshape(512, FC)) + dot_nt(act[2], wu[block].reshape(512, FC))
        zs[:, cols] = r.astype(BF16)
        dhn_copies[0] += z_scatter(zs, 1, 0, pl.ds(t * 512, 512))
    dhn_copies[1] += z_scatter(zs, 1, 1)
    wait_recv([hnt_copy] + act_copies[1])
    weight_grad(1, first_rows, hn_t, hn_p, act.at[1], act_p.at[1])
    rs_send(1, 0)
    wait_recv(act_copies[2])
    weight_grad(2, first_rows, hn_t, hn_p, act.at[2], act_p.at[2])
    rs_send(2, 0)
    weight_grad(0, other_rows, c_t, c_p, act.at[0], act_p.at[0])
    rs_turn(0, 0)

    da_copies = []

    def norm_back(part):
        wait_recv(dhn_copies[part])
        m = mid[kept[part], :]
        r2 = inv_rms(m)
        mhat = m * r2
        scaled = z_sum(zs, 1, part) * gf[...]
        rows = z_rows(part, iz)
        dm = cot[rows, :].astype(F32) + r2 * (
            scaled - mhat * jnp.mean(scaled * mhat, -1, keepdims=True)
        )
        dmid[kept[part], :] = dm
        da[rows, :] = dm.astype(BF16)
        da_copies.extend(z_gather(da, part))

    norm_back(0)
    weight_grad(1, other_rows, hn_t, hn_p, act.at[1], act_p.at[1])
    norm_back(1)
    weight_grad(2, other_rows, hn_t, hn_p, act.at[2], act_p.at[2])
    rs_turn(1, 0)
    inner = act[0]
    for s, n in tiles(D, 512):
        xn[:, s : s + n] = dot(inner, wd[:, s : s + n]).astype(BF16)
    rs_turn(2, 0)

    wait_recv(da_copies)
    ffn_copies = [z_scatter(xn, 2, part) for part in range(2)]
    grad_attn = da[...]
    for s, n in tiles(QC, 256):
        grad_rows = dot_nt(grad_attn, wo[s : s + n, :])
        for j in range(n // 128):
            p = s // 128 + j
            pair = slice(p * 128, (p + 1) * 128)
            g = grad_rows[:, j * 128 : (j + 1) * 128] * rl[:, pair]
            by_query(p, g, kk)
            by_row = (g * ob[:, pair].astype(F32)).T
            for i in range(2):
                h = p * 2 + i
                sums = jnp.sum(by_row[i * HD : (i + 1) * HD], 0, keepdims=True)
                delta[:, h * TA : (h + 1) * TA] = sums[:, 0:TA]
                delta[:, 8 * TA + h * 64 : 8 * TA + (h + 1) * 64] = sums[:, TA:T]
    wait_send([ct_copy])
    c_t[...] = grad_attn.T.reshape(turned)
    dat_copy = send(c_t.at[:, :, other], da_p, core_peer)
    dob = kk

    wait_send(kv_copies)
    dkv_copies = []
    for i, step in enumerate((2, 1, 3, 0)):
        chip = (ix + step) % 4
        rows = pl.ds(pl.multiple_of(chip * CHIP_KEYS, CHIP_KEYS), CHIP_KEYS)
        weights = pt[rows, :]
        dv = dot(weights, dob[...])
        for s, n in tiles(QUERIES, CHUNK):
            lanes = slice(s, s + n)
            grad_weights = dot_nt(vv[rows, :], dob[lanes, :])
            pt[rows, lanes] = (
                weights[:, lanes].astype(F32) * (grad_weights - delta[:, lanes])
            ).astype(BF16)
        dk = dot(pt[rows, :], qst[...])
        both = jnp.where(
            lane_of((CHIP_KEYS, 128)) < HD, dk + pltpu.roll(dk, HD, 1), dv + pltpu.roll(dv, HD, 1)
        ).astype(BF16)
        for c in range(2):
            kvall[chip * 2 + c] = both[c * T : (c + 1) * T]
        for c, goal in ((0, core), (1, other)):
            if step != 0 or c == 1:
                dkv_copies.append(
                    send(kvall.at[chip * 2 + goal], dkv_r.at[i, c], (iy, chip * 2 + goal, iz))
                )
        if i == 1:
            wait_recv([dat_copy, ob_copy])
            weight_grad(3, first_rows, c_t, da_p, ob, ob_p)
            rs_send(3, 0)
    dq_t = dot(kt[...], pt[...]) * (HD ** -0.5)
    for p in range(PAIRS):
        a0 = dq_t[:, p * 256 : p * 256 + 128].T
        a1 = dq_t[:, p * 256 + 128 : p * 256 + 256].T
        b = dq_t[:, 8 * TA + p * 128 : 8 * TA + (p + 1) * 128].T
        dq = jnp.concatenate(
            [jnp.where(low_a, a0, a1), jnp.where(low_b, b[0:64], b[64:128])], 0
        )
        dqp[:, p * 128 : (p + 1) * 128] = rot_back(dq).astype(BF16)
    dqp_copy = send(dqp, dqp_p, core_peer)

    wait_recv(dkv_copies)
    home = kvall[ictx].astype(F32) + dkv_r[3, 1].astype(F32)
    for i in range(3):
        for c in range(2):
            home = home + dkv_r[i, c].astype(F32)
    dkvp[...] = jnp.where(low_lane, rot_back(home), home).astype(BF16)
    dkvp_copy = send(dkvp, dkvp_p, core_peer)
    wait_send([copy for copies in dhn_copies for copy in copies])
    q_rows, kv_rows = dqp[...], dkvp[...]
    dxn_copies = [[], []]
    for s, n in tiles(D, 512):
        r = dot_nt(q_rows, wq[s : s + n, :]) + dot_nt(kv_rows, wkv[s : s + n, :])
        zs[:, s : s + n] = r.astype(BF16)
        dxn_copies[0] += z_scatter(zs, 3, 0, pl.ds(s, n))
    dxn_copies[1] += z_scatter(zs, 3, 1)

    wait_recv([xnt_copy, dqp_copy])
    weight_grad(4, first_rows, xn_t, xn_p, dqp, dqp_p, c0=0, n=512)
    wait_recv([dkvp_copy])
    weight_grad(4, first_rows, xn_t, xn_p, dkvp, dkvp_p, c0=512, n=128)
    rs_send(4, 0)
    rs_turn(0, 1)
    weight_grad(3, other_rows, c_t, da_p, ob, ob_p)
    weight_grad(4, other_rows, xn_t, xn_p, dqp, dqp_p, c0=0, n=512)
    weight_grad(4, other_rows, xn_t, xn_p, dkvp, dkvp_p, c0=512, n=128)
    rs_turn(1, 1)

    own_rows_out = []
    bo_copies = []
    for part in range(2):
        wait_recv(ffn_copies[part])
        bo_s[kept[part], :] = (mid[kept[part], :] + z_sum(xn, 2, part)).astype(BF16)
        copy_local(bo_s.at[kept[part]], bo.at[z_rows(part, iz)])
        bo_copies += z_gather(bo, part, bo_s)

    rs_turn(3, 0)
    rs_turn(4, 0)

    for part in range(2):
        wait_recv(dxn_copies[part])
        rows = x[z_rows(part, iz), :].astype(F32)
        r1 = inv_rms(rows)
        xhat = rows * r1
        scaled = z_sum(zs, 3, part) * ga[...]
        gi_s[kept[part], :] = (
            dmid[kept[part], :]
            + r1 * (scaled - xhat * jnp.mean(scaled * xhat, -1, keepdims=True))
        ).astype(BF16)
        copy_local(gi_s.at[kept[part]], gi.at[z_rows(part, iz)])
        z_gather(gi, part, gi_s)

    rs_turn(2, 1)
    rs_turn(0, 2)
    rs_turn(1, 2)
    rs_turn(3, 1)
    rs_turn(4, 1)
    rs_turn(2, 2)
    rs_last(0, [(g_d, o_d, 0, FC)])
    rs_last(1, [(g_g, o_g, 0, FC)])
    rs_turn(3, 2)
    rs_turn(4, 2)
    rs_last(2, [(g_u, o_u, 0, FC)])
    rs_last(3, [(g_o, o_o, 0, 512)])
    rs_last(4, [(g_q, o_q, 0, 512), (g_kv, o_kv, 512, 128)])

    wait_local(*row_loads)

    def row_products(pairs):
        total = jnp.zeros((64, 128), F32)
        for grad, weight in pairs:
            n = grad.shape[-1]
            w = weight[...].reshape(64, n)
            for s, _ in tiles(n, 128):
                total = total + grad[:, s : s + 128] * w[:, s : s + 128].astype(F32)
        return jnp.sum(total.T, 0, keepdims=True)

    gain_s[...] = jnp.zeros((8, 128), F32)
    gain_s[0:1, 0:64] = row_products([(g_g, row_g), (g_u, row_u)])
    gain_s[1:2, 0:64] = row_products([(g_q, row_q), (g_kv, row_kv)])
    gain_copies = [send(gain_s, gain_r.at[k - 1], z_peer(k)) for k in range(1, 4)]
    wait_recv(gain_copies)
    total = gain_s[...]
    for k in range(3):
        total = total + gain_r[k]
    chip_cols = pl.ds(pl.multiple_of((iy * 4 + ix) * 128, 128), 128)

    def own_gain(ref):
        v = ref[:, chip_cols]
        return jnp.where(core == 1, pltpu.roll(v, 64, 1), v)[:, 0:64]

    gain_f[...] = total[0:1, 0:64] / own_gain(gf)
    gain_a[...] = total[1:2, 0:64] / own_gain(ga)

    wait_recv([copy for copy in sent if id(copy) not in arrived])
    wait_send([copy for copy in sent if id(copy) not in released])
    wait_local(*[copy for copy in local if id(copy) not in local_done])


def store_kernel(*refs):
    n = 10
    src, dst, held = refs[:n], refs[n : 2 * n], refs[2 * n : 3 * n]
    wide, in_sem, out_sem = refs[3 * n :]
    moves = []
    for i in range(n):
        if i < 2:
            for j in range(4):
                rows = pl.ds(j * R, R)
                moves.append((src[i].at[rows], held[i].at[rows], dst[i].at[rows], (i, rows)))
        else:
            moves.append((src[i], held[i], dst[i], (i, None)))
    moves.sort(key=lambda move: move[3][0] != 1)
    fetches = []
    for k, (a, b, _, _) in enumerate(moves):
        copy = pltpu.make_async_copy(a, b, in_sem.at[k])
        copy.start()
        fetches.append(copy)
    stores = []
    for k, (_, b, c, (i, rows)) in enumerate(moves):
        fetches[k].wait()
        if i == 1:
            wide[rows, :] = b[...].astype(F32)
            b = wide.at[rows]
        copy = pltpu.make_async_copy(b, c, out_sem.at[k])
        copy.start()
        stores.append(copy)
    for copy in stores:
        copy.wait()


N_SENDS = 224
N_LOCAL = 40


def per_device(
    hidden_in, block_order, w_query, w_keyval, w_output, w_gate, w_up, w_down,
    gain_attn, gain_ffn, cotangent,
):
    coarse, fine = rope_tables()
    any_spec = pl.BlockSpec(memory_space=pl.ANY)
    vmem = pl.BlockSpec(memory_space=pltpu.VMEM)
    smem = pl.BlockSpec(memory_space=pltpu.SMEM)
    shape = jax.ShapeDtypeStruct
    wide = (2, 4, 4, 2, 32, FC)
    turned = (4, 4, 2, 2, 32, T)
    half_turned = (4, 4, 2, 32, T)
    scratch = [
        pltpu.VMEM(s, t)
        for s, t in (
            ((T, D), BF16), ((T, D), BF16),
            ((D, QC), BF16), ((D, 128), BF16), ((QC, D), BF16),
            (wide, BF16), (wide, BF16), ((FC, D), BF16),
            ((2, 32, FC), BF16), ((2, 32, FC), BF16), ((64, QC), BF16), ((64, 128), BF16),
            ((T, D), BF16), ((8, T, 128), BF16),
            ((KEYS, 128), BF16), ((KEYS, 128), BF16),
            ((128, KEYS), BF16), ((144, KEYS), BF16),
            ((QUERIES, 128), BF16), ((T, 128), F32), ((T, 128), F32),
            ((KEYS, CHUNK), F32), ((KEYS, QUERIES), BF16),
            ((T, QC), BF16), ((T, QC), F32),
            ((T, D), BF16), ((4, 3, R, D), BF16),
            ((R, D), F32), ((R, D), F32),
            ((T, D), BF16), ((T, D), BF16), ((R, D), BF16), ((R, D), BF16),
            ((T, FC), F32), ((3, T, FC), BF16), ((3, T, FC), BF16),
            ((2, 4, 32, FC), BF16),
            (turned, BF16), (turned, BF16), (turned, BF16),
            (half_turned, BF16), (half_turned, BF16), (half_turned, BF16), (half_turned, BF16),
            ((T, QC), BF16), ((T, QC), BF16), ((T, QC), BF16),
            ((T, 128), BF16), ((T, 128), BF16),
            ((4, 2, T, 128), BF16), ((1, QUERIES), F32),
            ((3, 2, 2, 2, 32, FC), BF16), ((3, 2, 2, 4, 32, FC), BF16),
            ((3, 2, 2, 16, FC), BF16), ((3, 2, 2, 32, FC), BF16),
            ((2, 2, 2, 32, 1152), BF16), ((2, 2, 4, 32, 1152), BF16),
            ((2, 2, 16, 1152), BF16), ((2, 2, 32, 1152), BF16),
            ((64, QC), F32), ((64, 128), F32), ((64, QC), F32),
            ((64, FC), F32), ((64, FC), F32), ((64, FC), F32),
            ((8, 128), F32), ((3, 8, 128), F32),
        )
    ] + [
        pltpu.SemaphoreType.DMA((N_LOCAL,)),
        pltpu.SemaphoreType.DMA((N_SENDS,)),
        pltpu.SemaphoreType.DMA((N_SENDS,)),
    ]
    grads = (
        shape((64, QC), F32), shape((64, 128), F32), shape((64, QC), F32),
        shape((64, FC), F32), shape((64, FC), F32), shape((64, FC), F32),
        shape((1, 64), F32), shape((1, 64), F32),
    )
    outs = pl.pallas_call(
        layer_kernel,
        out_shape=(shape((T, D), BF16), shape((T, D), BF16)) + grads,
        in_specs=[smem] + [any_spec] * 8 + [vmem] * 4,
        out_specs=(any_spec,) * 8 + (vmem,) * 2,
        scratch_shapes=scratch,
        compiler_params=pltpu.CompilerParams(
            collective_id=0, has_side_effects=True, vmem_limit_bytes=65200 * 1024
        ),
    )(
        block_order, hidden_in.reshape(T, D), cotangent.reshape(T, D),
        w_query, w_keyval, w_output, w_gate.reshape(wide), w_up.reshape(wide), w_down,
        gain_attn.reshape(1, D), gain_ffn.reshape(1, D), coarse, fine,
    )
    outs = pl.pallas_call(
        store_kernel,
        out_shape=(shape((T, D), BF16), shape((T, D), F32)) + grads,
        in_specs=[any_spec] * 10,
        out_specs=(any_spec,) * 10,
        scratch_shapes=[pltpu.VMEM((T, D), BF16)] * 2
        + [pltpu.VMEM(g.shape, F32) for g in grads]
        + [
            pltpu.VMEM((T, D), F32),
            pltpu.SemaphoreType.DMA((16,)), pltpu.SemaphoreType.DMA((16,)),
        ],
        compiler_params=pltpu.CompilerParams(vmem_limit_bytes=65200 * 1024),
    )(*outs)
    bo, gi, g_q, g_kv, g_o, g_g, g_u, g_d, gain_a, gain_f = outs
    return (
        bo.reshape(1, T, D),
        gi.reshape(1, T, D),
        g_q,
        g_kv,
        g_o.T,
        g_g,
        g_u,
        g_d.T,
        gain_a.reshape(64),
        gain_f.reshape(64),
    )


def solution(mesh):
    return jax.shard_map(
        per_device,
        mesh=mesh,
        in_specs=(
            P("dp", "ctx", None),
            P("dp", None),
            P(None, "tensor"),
            P(None, "tensor"),
            P("tensor", None),
            P(None, "tensor"),
            P(None, "tensor"),
            P("tensor", None),
            P(),
            P(),
            P("dp", "ctx", None),
        ),
        out_specs=(
            P("dp", "ctx", None),
            P("dp", "ctx", None),
            P(("dp", "ctx"), "tensor"),
            P(("dp", "ctx"), "tensor"),
            P("tensor", ("dp", "ctx")),
            P(("dp", "ctx"), "tensor"),
            P(("dp", "ctx"), "tensor"),
            P("tensor", ("dp", "ctx")),
            P(("dp", "ctx")),
            P(("dp", "ctx")),
        ),
        check_vma=False,
    )
```

```python
import jax
import jax.numpy as jnp
import numpy as np
from jax import lax
from jax.experimental import pallas as pl
from jax.experimental.pallas import tpu as pltpu
from jax.sharding import PartitionSpec as P

MESH = pl.DeviceIdType.MESH
F32 = jnp.float32
BF16 = jnp.bfloat16
EPSILON = 1e-05
NEG_FILL = -1e30
ROPE_BASE = 10000.0

D = 2048
HD = 64
T = 192
BLOCK = 96
TA = 128
R = 48
QC = 512
FC = 1408
KEYS = 1536
PAIRS = 4
QUERIES = 1536
CHUNK = 512
GROUP = 768
CHIP_KEYS = 384
FF_TILES = ((0, 384), (384, 384), (768, 384), (1152, 256))


def rope_tables():
    half = HD // 2
    freq = ROPE_BASE ** (-np.arange(half, dtype=np.float64) / half)
    freq = np.tile(freq, 4)[None, :]
    coarse = np.arange(16, dtype=np.float64)[:, None] * BLOCK * freq
    fine = np.arange(BLOCK, dtype=np.float64)[:, None] * freq
    coarse = np.stack([np.cos(coarse), np.sin(coarse)]).astype(np.float32)
    fine = np.stack([np.cos(fine), np.sin(fine)]).astype(np.float32)
    return coarse, fine


def dot(a, b):
    return jnp.dot(a, b, preferred_element_type=F32)


def dot_nt(a, b):
    return lax.dot_general(a, b, (((1,), (1,)), ((), ())), preferred_element_type=F32)


def tiles(total, size):
    return [(s, min(size, total - s)) for s in range(0, total, size)]


def lane_of(shape):
    return lax.broadcasted_iota(jnp.int32, shape, len(shape) - 1)


def swap_halves(t):
    first = lane_of(t.shape) % HD < HD // 2
    return jnp.where(first, pltpu.roll(t, 96, 1), pltpu.roll(t, 32, 1))


def layer_kernel(
    order, x_h, c_h, wq_h, wkv_h, wo_h, wg_h, wu_h, wd_h, ga_h, gf_h, coarse_h, fine_h,
    bo, gi, o_q, o_kv, o_o, o_g, o_u, o_d, gain_a, gain_f,
    ga, gf, coarse, fine, x, cot, wq, wkv, wo, wg, wu, wd, row_g, row_u, row_q, row_kv,
    xn, kvall, kk, vv, kt, vt, qst, cos_t, sin_t, s_buf, pt, ob, rl,
    zs, z_near, z_far, mid, dmid, hn, da, bo_s, gi_s, dinner, act, act_p, down_first,
    xn_t, c_t, hn_t, xn_p, c_p, hn_p, da_p, ob_p, dqp, dqp_p, dkvp, dkvp_p,
    dkv_r, delta, r1f, r2f, r3f, r4f, r1a, r2a, r3a, r4a,
    g_q, g_kv, g_o, g_g, g_u, g_d, gain_s, gain_r,
    local_sem, send_sem, recv_sem,
):
    iy = lax.axis_index("dp")
    ictx = lax.axis_index("ctx")
    iz = lax.axis_index("tensor")
    ix = ictx // 2
    core = ictx % 2
    other = 1 - core

    def z_peer(k):
        return (iy, ictx, (iz + k) % 4)

    def ctx_peer(k):
        return (iy, (ictx + k) % 8, iz)

    def x_peer(k):
        return (iy, ((ix + k) % 4) * 2 + core, iz)

    def y_peer(k):
        return ((iy + k) % 4, ictx, iz)

    core_peer = (iy, ix * 2 + other, iz)

    local = []
    local_done = set()

    def copy_local(src, dst):
        copy = pltpu.make_async_copy(src, dst, local_sem.at[len(local)])
        copy.start()
        local.append(copy)
        return copy

    def wait_local(*copies):
        for copy in copies:
            copy.wait()
            local_done.add(id(copy))

    x_load = copy_local(x_h, x)
    table_loads = [
        copy_local(ga_h, ga), copy_local(gf_h, gf),
        copy_local(coarse_h, coarse), copy_local(fine_h, fine),
    ]
    wkv_load = copy_local(wkv_h, wkv)
    wq_load = copy_local(wq_h, wq)

    barrier = pltpu.get_barrier_semaphore()
    greeted = (
        [ctx_peer(k) for k in range(1, 8)]
        + [z_peer(k) for k in range(1, 4)]
        + [y_peer(1), y_peer(3)]
    )
    for peer in greeted:
        pl.semaphore_signal(barrier, inc=1, device_id=peer, device_id_type=MESH)

    groups = []

    class Group:
        def __init__(self, size):
            self.n = len(groups)
            self.size = size
            self.arrived = self.released = self.used = False
            groups.append(self)

        def copy(self, src, dst, peer):
            return pltpu.make_async_remote_copy(
                src_ref=src, dst_ref=dst, send_sem=send_sem.at[self.n],
                recv_sem=recv_sem.at[self.n], device_id=peer, device_id_type=MESH,
            )

        def send(self, src, dst, peer):
            self.used = True
            self.copy(src, dst, peer).start()

        def wait_recv(self):
            if self.used and not self.arrived:
                self.copy(self.size, self.size, core_peer).wait_recv()
                self.arrived = True

        def wait_send(self):
            if self.used and not self.released:
                self.copy(self.size, self.size, core_peer).wait_send()
                self.released = True

    def send_one(src, dst, peer):
        group = Group(dst)
        group.send(src, dst, peer)
        return group

    wait_local(*table_loads)
    pick = lax.broadcasted_iota(jnp.int32, (16, 128), 0)
    sign = jnp.where(lane_of((BLOCK, 128)) % HD < HD // 2, -1.0, 1.0).astype(F32)
    for b in range(2):
        chosen = pick == order[0, ictx * 2 + b]
        ca = jnp.sum(jnp.where(chosen, coarse[0], 0.0), 0, keepdims=True)
        sa = jnp.sum(jnp.where(chosen, coarse[1], 0.0), 0, keepdims=True)
        cos_t[b * BLOCK : (b + 1) * BLOCK, :] = ca * fine[0] - sa * fine[1]
        sin_t[b * BLOCK : (b + 1) * BLOCK, :] = (sa * fine[0] + ca * fine[1]) * sign

    def rot(t):
        return t * cos_t[...] + swap_halves(t) * sin_t[...]

    def rot_back(t):
        return t * cos_t[...] - swap_halves(t) * sin_t[...]

    def inv_rms(v):
        return lax.rsqrt(jnp.mean(v * v, -1, keepdims=True) + EPSILON)

    low_lane = lane_of((T, 128)) < HD
    low_a, low_b = low_lane[0:TA], low_lane[0 : T - TA]

    wait_local(x_load)
    for i in range(4):
        rows = x[i * R : (i + 1) * R, :].astype(F32)
        xn[i * R : (i + 1) * R, :] = (rows * inv_rms(rows) * ga[...]).astype(BF16)
    wait_local(wkv_load)
    cot_load = copy_local(c_h, cot)
    wd_load = copy_local(wd_h, wd)
    normed = xn[...]
    kvp = dot(normed, wkv[...])
    kvall[ictx] = jnp.where(low_lane, rot(kvp), kvp).astype(BF16)
    pl.semaphore_wait(barrier, len(greeted))
    kv_group = Group(kvall.at[pl.ds(0, 7)])
    for k in (4, 5, 3, 2, 6, 7, 1):
        kv_group.send(kvall.at[ictx], kvall.at[ictx], ctx_peer(k))
    wait_local(wq_load)
    wo_load = copy_local(wo_h, wo)
    wg_load = copy_local(wg_h, wg)
    wu_load = copy_local(wu_h, wu)
    own_h, own_a, own_b = iy // 2, (iy % 2) * 2 + ix // 2, (ix % 2) * 2 + core
    own_rows = pl.ds(pl.multiple_of(((iy * 4 + ix) * 2 + core) * 64, 64), 64)
    row_loads = [
        copy_local(wg_h.at[own_h, own_a, own_b], row_g),
        copy_local(wu_h.at[own_h, own_a, own_b], row_u),
        copy_local(wq_h.at[own_rows], row_q),
        copy_local(wkv_h.at[own_rows], row_kv),
    ]

    def by_query(pair, value, ref):
        for i in range(2):
            h = pair * 2 + i
            one = jnp.where(low_lane, value, 0.0) if i == 0 else jnp.where(low_lane, 0.0, value)
            one = one.astype(BF16)
            ref[h * TA : (h + 1) * TA, :] = one[0:TA]
            ref[8 * TA + h * 64 : 8 * TA + (h + 1) * 64, :] = one[TA:T]

    for s, n in tiles(QC, 256):
        qp = dot(normed, wq[:, s : s + n])
        for j in range(n // 128):
            by_query(s // 128 + j, rot(qp[:, j * 128 : (j + 1) * 128]) * (HD ** -0.5), qst)

    turned = (4, 4, 2, 2, 32, T)
    xn_t[...] = normed.T.reshape(turned)
    xnt_copy = send_one(xn_t.at[:, :, other], xn_p, core_peer)
    wait_local(cot_load)
    cot_rows = cot[...]
    c_t[...] = cot_rows.T.reshape(turned)
    ct_copy = send_one(c_t.at[:, :, other], c_p, core_peer)
    wait_local(wd_load)
    for s, n in tiles(FC, 512):
        rows = slice(s // 128, (s + n) // 128)
        dinner[:, s : s + n] = dot_nt(cot_rows, wd[rows].reshape(n, D))

    kv_group.wait_recv()
    for j in range(8):
        wide = kvall[j].astype(F32)
        rolled = pltpu.roll(wide, HD, 1)
        rows = pl.ds(j * T, T)
        kk[rows, :] = jnp.where(low_lane, wide, rolled).astype(BF16)
        vv[rows, :] = jnp.where(low_lane, rolled, wide).astype(BF16)
    kv_t = kvall[...].reshape(KEYS, 128).T
    kt[0:HD, :] = kv_t[0:HD]
    kt[HD : 2 * HD, :] = kv_t[0:HD]
    vt[0:HD, :] = kv_t[HD : 2 * HD]
    vt[HD : 2 * HD, :] = kv_t[HD : 2 * HD]
    vt[2 * HD : 2 * HD + 16, :] = jnp.ones((16, KEYS), BF16)

    lane = lane_of((1, CHUNK))
    token = lane % TA
    start_0, start_1 = order[0, ictx * 2] * BLOCK, order[0, ictx * 2 + 1] * BLOCK
    place_a = jnp.where(token >= BLOCK, start_1 + token - BLOCK, start_0 + token)
    place_b = start_1 + (TA - BLOCK) + lane % 64
    key_row = lax.broadcasted_iota(jnp.int32, (BLOCK, CHUNK), 0)

    def attend(chunk):
        q_place = place_a if chunk < 2 else place_b
        lanes = slice(chunk * CHUNK, (chunk + 1) * CHUNK)
        top = jnp.full((8, CHUNK), NEG_FILL, F32)
        for r0 in range(0, KEYS, GROUP):
            scores = dot_nt(kk[r0 : r0 + GROUP, :], qst[lanes, :])
            for b in range(GROUP // BLOCK):
                limit = q_place - order[0, r0 // BLOCK + b] * BLOCK
                rows = slice(b * BLOCK, (b + 1) * BLOCK)
                seen = jnp.where(key_row <= limit, scores[rows], NEG_FILL)
                s_buf[r0 + b * BLOCK : r0 + (b + 1) * BLOCK, :] = seen
                top = jnp.maximum(top, jnp.max(seen.reshape(BLOCK // 8, 8, CHUNK), 0))
        top = jnp.max(top, 0, keepdims=True)
        for r0 in range(0, KEYS, GROUP):
            rows = slice(r0, r0 + GROUP)
            pt[rows, lanes] = jnp.exp(s_buf[rows, :] - top).astype(BF16)
        summed = dot(vt[...], pt[:, lanes])
        inv = 1.0 / summed[2 * HD : 2 * HD + 1]
        out = summed[0 : 2 * HD] * inv
        inv = jnp.broadcast_to(inv, (2 * HD, CHUNK))
        if chunk < 2:
            for j in range(2):
                pair = slice((chunk * 2 + j) * 128, (chunk * 2 + j + 1) * 128)
                one, two = slice(j * 256, j * 256 + 128), slice(j * 256 + 128, j * 256 + 256)
                ob[0:TA, pair] = jnp.where(low_a, out[:, one].T, out[:, two].T).astype(BF16)
                rl[0:TA, pair] = jnp.where(low_a, inv[:, one].T, inv[:, two].T)
        else:
            for p in range(PAIRS):
                pair = slice(p * 128, (p + 1) * 128)
                o2, i2 = out[:, pair].T, inv[:, pair].T
                ob[TA:T, pair] = jnp.where(low_b, o2[0:64], o2[64:128]).astype(BF16)
                rl[TA:T, pair] = jnp.where(low_b, i2[0:64], i2[64:128])

    def z_rows(part, z):
        if part == 0:
            return pl.ds(pl.multiple_of(z * 32, 32), 32)
        return pl.ds(pl.multiple_of(TA + z * 16, 16), 16)

    kept = (slice(0, 32), slice(32, 48))
    cols_l, cols_r, all_cols = pl.ds(0, D // 2), pl.ds(D // 2, D // 2), pl.ds(0, D)
    zp, zm, z2 = (iz + 1) % 4, (iz + 3) % 4, (iz + 2) % 4

    class ZScatter:
        def __init__(self, src, n, part):
            self.src, self.n, self.part = src, n, part
            self.far = Group(z_far.at[n, :, kept[part]])
            self.near = Group(z_near.at[n, :, kept[part]])

        def first(self, cols=(0, D // 2, D // 2)):
            l, r, width = cols
            src, n, part = self.src, self.n, self.part
            keep = kept[part]
            left, right = pl.ds(l, width), pl.ds(r, width)
            if l is not None:
                far = z_far.at[n, 0, keep, left]
                self.far.send(src.at[z_rows(part, z2), left], far, z_peer(1))
            if r is not None:
                far = z_far.at[n, 1, keep, pl.ds(r - D // 2, width)]
                self.far.send(src.at[z_rows(part, z2), right], far, z_peer(3))
            if l is not None:
                near = z_near.at[n, 1, keep, left]
                self.near.send(src.at[z_rows(part, zm), left], near, z_peer(3))
            if r is not None:
                near = z_near.at[n, 0, keep, right]
                self.near.send(src.at[z_rows(part, zp), right], near, z_peer(1))

        def second(self):
            src, n, part = self.src, self.n, self.part
            keep = kept[part]
            self.far.wait_recv()
            for way, z, cols, k in ((0, zp, cols_l, 1), (1, zm, cols_r, 3)):
                rows = z_rows(part, z)
                total = src[rows, cols].astype(F32) + z_far[n, way, keep, :].astype(F32)
                src[rows, cols] = total.astype(BF16)
                self.near.send(src.at[rows, cols], z_near.at[n, way, keep, cols], z_peer(k))

        def result(self):
            self.near.wait_recv()
            total = self.src[z_rows(self.part, iz), :].astype(F32)
            for way in range(2):
                total = total + z_near[self.n, way, kept[self.part], :].astype(F32)
            return total

        def wait_send(self):
            self.far.wait_send()
            self.near.wait_send()

    class ZGather:
        def __init__(self, buf, part, own=None):
            self.buf, self.part = buf, part
            self.far = Group(z_far.at[0, :, kept[part]])
            self.near = Group(z_near.at[0, :, kept[part]])
            rows = z_rows(part, iz)
            for cols, way, k, group in (
                (cols_l, 0, 1, self.far), (cols_r, 1, 3, self.far),
                (cols_r, 0, 1, self.near), (cols_l, 1, 3, self.near),
            ):
                src = buf.at[rows, cols] if own is None else own.at[kept[part], cols]
                group.send(src, buf.at[rows, cols], z_peer(k))

        def second(self):
            self.far.wait_recv()
            for z, cols, k in ((zm, cols_l, 1), (zp, cols_r, 3)):
                piece = self.buf.at[z_rows(self.part, z), cols]
                self.near.send(piece, piece, z_peer(k))

        def wait_recv(self):
            self.near.wait_recv()

    def project_out(part):
        rows = slice(0, TA) if part == 0 else slice(TA, T)
        scatter = ZScatter(zs, 0, part)
        for l in (0, 512):
            for s in (l, l + D // 2):
                zs[rows, s : s + 512] = dot(ob[rows, :], wo[:, s : s + 512]).astype(BF16)
            scatter.first((l, l + D // 2, 512))
        return scatter

    attend(0)
    attend(1)
    wait_local(wo_load)
    attn_sums = [project_out(0)]
    attend(2)
    attn_sums.append(project_out(1))
    ob_copy = send_one(ob, ob_p, core_peer)

    hn_parts = []

    def norm(part):
        m = x[z_rows(part, iz), :].astype(F32) + attn_sums[part].result()
        mid[kept[part], :] = m
        hn[z_rows(part, iz), :] = (m * inv_rms(m) * gf[...]).astype(BF16)
        hn_parts.append(ZGather(hn, part))

    attn_sums[0].second()
    attn_sums[1].second()
    norm(0)
    norm(1)
    hn_parts[0].second()
    hn_parts[1].second()

    xp, xm, x2 = (ix + 1) % 4, (ix + 3) % 4, (ix + 2) % 4
    yp, ym, y2 = (iy + 1) % 4, (iy + 3) % 4, (iy + 2) % 4

    def own_part(ref):
        return lambda dy, dx, h: ref[dy, dx, core, h]

    def partner_part(ref):
        return lambda dy, dx, h: ref[dy, dx, h]

    all4 = pl.ds(0, 4)
    first_rows = [(all4, x2, 0), (y2, all4, 1)]
    other_rows = [(all4, dx, 0) for dx in (xp, xm, ix)] + [(dy, all4, 1) for dy in (yp, ym, iy)]

    def weight_grad(part, which, own_t, partner_t, own_b, partner_b, b0=0, n=None, shift=0):
        ref, half, part_c0, part_n, _, _ = parts[part]
        n = part_n if n is None else n
        early = which is first_rows and part < 3
        get_own, get_partner = own_part(own_t), partner_part(partner_t)
        a_own = jnp.concatenate([get_own(*i).reshape(128, T) for i in which], 0)
        a_partner = jnp.concatenate([get_partner(*i).reshape(128, T) for i in which], 0)
        for s, w in tiles(n, 256):
            s = s + b0
            r = dot(a_own, own_b[:, s : s + w]) + dot(a_partner, partner_b[:, s : s + w])
            r = r.astype(BF16)
            cols = slice(part_c0 + shift + s, part_c0 + shift + s + w)
            for i, (dy, dx, h) in enumerate(which):
                rows = r[i * 128 : (i + 1) * 128].reshape(4, 32, w)
                if early:
                    g_first[part][i, :, :, cols] = rows
                else:
                    ref[half, dy, dx, h, :, cols] = rows

    f_bufs = [[r.at[i] for r in (r1f, r2f, r3f, r4f)] for i in range(3)]
    a_bufs = [r1a, r2a, r3a, r4a]
    parts = [
        (wg, 1, 0, FC, f_bufs[0], 0),
        (wg, 0, 0, FC, f_bufs[1], 0),
        (wu, 0, 0, FC, f_bufs[2], 0),
        (wu, 1, 0, 512, a_bufs, 0),
        (wu, 1, 512, 640, a_bufs, 512),
    ]
    g_first = [down_first.at[0:2], wd.at[0:2], wd.at[2:4]]
    flights = {}
    lo2, hi2 = pl.ds(0, 2), pl.ds(2, 2)
    all32, lo16, hi16 = pl.ds(0, 32), pl.ds(0, 16), pl.ds(16, 16)

    def g_index(part, dy, dx, h, rows=None):
        ref, half, c0, n, _, _ = parts[part]
        return (half, dy, dx, h, all32 if rows is None else rows, pl.ds(c0, n))

    def first_piece(part, flow, pair, s, n):
        if part < 3:
            return g_first[part].at[flow, pair, :, pl.ds(s, n)]
        ref, half, c0, _, _, _ = parts[part]
        dy, dx = (pair, x2) if flow == 0 else (y2, pair)
        return ref.at[half, dy, dx, flow, :, pl.ds(c0 + s, n)]

    def outgoing(part, step, s, n):
        if step == 0:
            return tuple(
                tuple(first_piece(part, flow, pair, s, n) for pair in (lo2, hi2))
                for flow in range(2)
            )
        if step == 1:
            index = (
                (g_index(part, all4, xp, 0), g_index(part, all4, xm, 0)),
                (g_index(part, yp, all4, 1), g_index(part, ym, all4, 1)),
            )
        elif step == 2:
            index = (
                (g_index(part, y2, ix, 0, lo16), g_index(part, y2, ix, 0, hi16)),
                (g_index(part, iy, x2, 1, lo16), g_index(part, iy, x2, 1, hi16)),
            )
        else:
            index = (
                (g_index(part, yp, ix, 0), g_index(part, ym, ix, 0)),
                (g_index(part, iy, xp, 1), g_index(part, iy, xm, 1)),
            )
        ref = parts[part][0]
        return tuple(tuple(ref.at[i] for i in flow) for flow in index)

    def landing(part, step, flow, way, s=0, n=None):
        _, _, _, part_n, bufs, b0 = parts[part]
        return bufs[step].at[flow, way, ..., pl.ds(b0 + s, part_n if n is None else n)]

    def rs_send(part, step, s=0, n=None):
        _, _, _, part_n, bufs, b0 = parts[part]
        n = part_n if n is None else n
        out = outgoing(part, step, s, n)
        if (part, step) not in flights:
            flights[part, step] = Group(bufs[step].at[..., pl.ds(b0, part_n)])
        group = flights[part, step]
        for flow in range(2):
            along_x = (flow == 0) == (step < 2)
            for way, k in ((0, 1), (1, 3)):
                peer = x_peer(k) if along_x else y_peer(k)
                group.send(out[flow][way], landing(part, step, flow, way, s, n), peer)

    def add_in(ref, index, *arrived):
        total = ref[index].astype(F32)
        for a in arrived:
            total = total + a[...].astype(F32)
        ref[index] = total.astype(BF16)

    def rs_recv(part, step):
        ref = parts[part][0]
        flights[part, step].wait_recv()
        for flow in range(2):
            got = [landing(part, step, flow, way) for way in range(2)]
            if step == 0:
                if flow == 0:
                    add_in(ref, g_index(part, lo2, xp, 0), got[0])
                    add_in(ref, g_index(part, hi2, xm, 0), got[1])
                else:
                    add_in(ref, g_index(part, yp, lo2, 1), got[0])
                    add_in(ref, g_index(part, ym, hi2, 1), got[1])
            elif step == 1:
                if flow == 0:
                    add_in(ref, g_index(part, all4, ix, 0), *got)
                else:
                    add_in(ref, g_index(part, iy, all4, 1), *got)
            elif step == 2:
                if flow == 0:
                    add_in(ref, g_index(part, yp, ix, 0, lo16), got[0])
                    add_in(ref, g_index(part, ym, ix, 0, hi16), got[1])
                else:
                    add_in(ref, g_index(part, iy, xp, 1, lo16), got[0])
                    add_in(ref, g_index(part, iy, xm, 1, hi16), got[1])

    def rs_turn(part, step):
        rs_recv(part, step)
        rs_send(part, step + 1)

    def rs_last(part, outs):
        rs_recv(part, 3)
        ref = parts[part][0]
        for flow in range(2):
            total = ref[g_index(part, iy, ix, flow)].astype(F32)
            for way in range(2):
                total = total + landing(part, 3, flow, way)[...].astype(F32)
            for stage, out, s, n in outs:
                stage[flow * 32 : (flow + 1) * 32, :] = total[:, s : s + n]
        for stage, out, s, n in outs:
            copy_local(stage, out)

    wait_local(wg_load, wu_load)
    for part in hn_parts:
        part.wait_recv()
    hidden = hn[...]
    inner_groups = [Group(act_p.at[0, :, pl.ds(s, n)]) for s, n in FF_TILES]
    act_groups = [None, Group(act_p.at[1]), Group(act_p.at[2])]

    def first_of_down(i):
        s, n = FF_TILES[i]
        inner_groups[i].wait_recv()
        weight_grad(0, first_rows, c_t, c_p, act.at[0], act_p.at[0], s, n)
        rs_send(0, 0, s, n)

    ct_copy.wait_recv()
    for t, (s, n) in enumerate(FF_TILES):
        cols = slice(s, s + n)
        g = dot(hidden, wg[:, :, :, :, :, cols].reshape(D, n))
        u = dot(hidden, wu[:, :, :, :, :, cols].reshape(D, n))
        sig = 1.0 / (1.0 + jnp.exp(-g))
        a = g * sig
        di = dinner[:, cols]
        act[0, :, cols] = (a * u).astype(BF16)
        piece = pl.ds(s, n)
        inner_groups[t].send(act.at[0, :, piece], act_p.at[0, :, piece], core_peer)
        act[1, :, cols] = (di * u * sig * (1.0 + g * (1.0 - sig))).astype(BF16)
        act[2, :, cols] = (di * a).astype(BF16)
        for i in (1, 2):
            act_groups[i].send(act.at[i, :, piece], act_p.at[i, :, piece], core_peer)
        if t > 0:
            first_of_down(t - 1)
    hn_t[...] = hidden.T.reshape(turned)
    hnt_copy = send_one(hn_t.at[:, :, other], hn_p, core_peer)
    first_of_down(3)
    inner = act[0]
    for s, n in tiles(D, 512):
        xn[:, s : s + n] = dot(inner, wd[..., s : s + n].reshape(FC, n)).astype(BF16)
    hnt_copy.wait_recv()
    act_groups[1].wait_recv()
    weight_grad(1, first_rows, hn_t, hn_p, act.at[1], act_p.at[1])
    rs_send(1, 0)

    for scatter in attn_sums:
        scatter.wait_send()
    dhn_sums = [ZScatter(zs, 1, part) for part in range(2)]
    for t in (0, 2, 1, 3):
        cols = slice(t * 512, (t + 1) * 512)
        block = (t // 2, slice((t % 2) * 2, (t % 2) * 2 + 2))
        r = dot_nt(act[1], wg[block].reshape(512, FC)) + dot_nt(act[2], wu[block].reshape(512, FC))
        zs[:, cols] = r.astype(BF16)
        dhn_sums[0].first((t * 512, None, 512) if t < 2 else (None, t * 512, 512))
        if t == 2:
            act_groups[2].wait_recv()
            weight_grad(2, first_rows, hn_t, hn_p, act.at[2], act_p.at[2])
            rs_send(2, 0)
    dhn_sums[1].first()
    weight_grad(0, other_rows, c_t, c_p, act.at[0], act_p.at[0])
    rs_turn(0, 0)
    dhn_sums[0].second()
    dhn_sums[1].second()
    weight_grad(1, other_rows, hn_t, hn_p, act.at[1], act_p.at[1])
    weight_grad(2, other_rows, hn_t, hn_p, act.at[2], act_p.at[2])

    da_parts = []

    def norm_back(part):
        m = mid[kept[part], :]
        r2 = inv_rms(m)
        mhat = m * r2
        scaled = dhn_sums[part].result() * gf[...]
        rows = z_rows(part, iz)
        dm = cot[rows, :].astype(F32) + r2 * (
            scaled - mhat * jnp.mean(scaled * mhat, -1, keepdims=True)
        )
        dmid[kept[part], :] = dm
        da[rows, :] = dm.astype(BF16)
        da_parts.append(ZGather(da, part))

    norm_back(0)
    norm_back(1)
    rs_turn(1, 0)
    da_parts[0].second()
    da_parts[1].second()
    rs_turn(2, 0)
    rs_turn(0, 1)

    for part in da_parts:
        part.wait_recv()
    ffn_sums = [ZScatter(xn, 2, part) for part in range(2)]
    for scatter in ffn_sums:
        scatter.first()
    grad_attn = da[...]
    for s, n in tiles(QC, 256):
        grad_rows = dot_nt(grad_attn, wo[s : s + n, :])
        for j in range(n // 128):
            p = s // 128 + j
            pair = slice(p * 128, (p + 1) * 128)
            g = grad_rows[:, j * 128 : (j + 1) * 128] * rl[:, pair]
            by_query(p, g, kk)
            by_row = (g * ob[:, pair].astype(F32)).T
            for i in range(2):
                h = p * 2 + i
                sums = jnp.sum(by_row[i * HD : (i + 1) * HD], 0, keepdims=True)
                delta[:, h * TA : (h + 1) * TA] = sums[:, 0:TA]
                delta[:, 8 * TA + h * 64 : 8 * TA + (h + 1) * 64] = sums[:, TA:T]
    ct_copy.wait_send()
    c_t[...] = grad_attn.T.reshape(turned)
    dat_copy = send_one(c_t.at[:, :, other], da_p, core_peer)
    dob = kk

    kv_group.wait_send()
    dkv_group = Group(kvall.at[pl.ds(0, 7)])
    for i, step in enumerate((2, 1, 3, 0)):
        chip = (ix + step) % 4
        rows = pl.ds(pl.multiple_of(chip * CHIP_KEYS, CHIP_KEYS), CHIP_KEYS)
        weights = pt[rows, :]
        dv = dot(weights, dob[...])
        for s, n in tiles(QUERIES, CHUNK):
            lanes = slice(s, s + n)
            grad_weights = dot_nt(vv[rows, :], dob[lanes, :])
            pt[rows, lanes] = (
                weights[:, lanes].astype(F32) * (grad_weights - delta[:, lanes])
            ).astype(BF16)
        dk = dot(pt[rows, :], qst[...])
        both = jnp.where(
            lane_of((CHIP_KEYS, 128)) < HD, dk + pltpu.roll(dk, HD, 1), dv + pltpu.roll(dv, HD, 1)
        ).astype(BF16)
        for c in range(2):
            kvall[chip * 2 + c] = both[c * T : (c + 1) * T]
        for c, goal in ((0, core), (1, other)):
            if step != 0 or c == 1:
                dkv_group.send(kvall.at[chip * 2 + goal], dkv_r.at[i, c], (iy, chip * 2 + goal, iz))
        if i == 1:
            for scatter in ffn_sums:
                scatter.second()
    dq_t = dot(kt[...], pt[...]) * (HD ** -0.5)
    for p in range(PAIRS):
        a0 = dq_t[:, p * 256 : p * 256 + 128].T
        a1 = dq_t[:, p * 256 + 128 : p * 256 + 256].T
        b = dq_t[:, 8 * TA + p * 128 : 8 * TA + (p + 1) * 128].T
        dq = jnp.concatenate(
            [jnp.where(low_a, a0, a1), jnp.where(low_b, b[0:64], b[64:128])], 0
        )
        dqp[:, p * 128 : (p + 1) * 128] = rot_back(dq).astype(BF16)
    dqp_copy = send_one(dqp, dqp_p, core_peer)

    bo_parts = []
    for part in range(2):
        bo_s[kept[part], :] = (mid[kept[part], :] + ffn_sums[part].result()).astype(BF16)
        copy_local(bo_s.at[kept[part]], bo.at[z_rows(part, iz)])
        bo_parts.append(ZGather(bo, part, bo_s))
    dat_copy.wait_recv()
    ob_copy.wait_recv()
    weight_grad(3, first_rows, c_t, da_p, ob, ob_p)
    rs_send(3, 0)
    weight_grad(3, other_rows, c_t, da_p, ob, ob_p)
    rs_turn(1, 1)

    dkv_group.wait_recv()
    home = kvall[ictx].astype(F32) + dkv_r[3, 1].astype(F32)
    for i in range(3):
        for c in range(2):
            home = home + dkv_r[i, c].astype(F32)
    dkvp[...] = jnp.where(low_lane, rot_back(home), home).astype(BF16)
    dkvp_copy = send_one(dkvp, dkvp_p, core_peer)
    for scatter in dhn_sums:
        scatter.wait_send()
    q_rows, kv_rows = dqp[...], dkvp[...]
    dxn_sums = [ZScatter(zs, 3, part) for part in range(2)]
    for l in (0, 512):
        for s in (l, l + D // 2):
            cols = slice(s, s + 512)
            r = dot_nt(q_rows, wq[cols, :]) + dot_nt(kv_rows, wkv[cols, :])
            zs[:, cols] = r.astype(BF16)
        dxn_sums[0].first((l, l + D // 2, 512))
    dxn_sums[1].first()

    for part in bo_parts:
        part.second()
    xnt_copy.wait_recv()
    dqp_copy.wait_recv()
    weight_grad(4, first_rows, xn_t, xn_p, dqp, dqp_p, n=512)
    dkvp_copy.wait_recv()
    weight_grad(4, first_rows, xn_t, xn_p, dkvp, dkvp_p, n=128, shift=512)
    rs_send(4, 0)
    dxn_sums[0].second()
    dxn_sums[1].second()
    weight_grad(4, other_rows, xn_t, xn_p, dqp, dqp_p, n=512)
    weight_grad(4, other_rows, xn_t, xn_p, dkvp, dkvp_p, n=128, shift=512)
    rs_turn(3, 0)

    gi_parts = []

    def first_norm_back(part):
        rows = x[z_rows(part, iz), :].astype(F32)
        r1 = inv_rms(rows)
        xhat = rows * r1
        scaled = dxn_sums[part].result() * ga[...]
        gi_s[kept[part], :] = (
            dmid[kept[part], :]
            + r1 * (scaled - xhat * jnp.mean(scaled * xhat, -1, keepdims=True))
        ).astype(BF16)
        copy_local(gi_s.at[kept[part]], gi.at[z_rows(part, iz)])
        gi_parts.append(ZGather(gi, part, gi_s))

    rs_turn(4, 0)
    rs_turn(2, 1)
    first_norm_back(0)
    first_norm_back(1)
    rs_turn(1, 2)
    rs_turn(4, 1)
    gi_parts[0].second()
    gi_parts[1].second()
    rs_turn(2, 2)
    rs_turn(3, 1)
    rs_turn(0, 2)
    rs_turn(4, 2)
    rs_last(1, [(g_g, o_g, 0, FC)])
    rs_turn(3, 2)
    rs_last(2, [(g_u, o_u, 0, FC)])

    wait_local(*row_loads)

    def row_products(pairs):
        total = jnp.zeros((64, 128), F32)
        for grad, weight in pairs:
            n = grad.shape[-1]
            w = weight[...].reshape(64, n)
            for s, _ in tiles(n, 128):
                total = total + grad[:, s : s + 128] * w[:, s : s + 128].astype(F32)
        return jnp.sum(total.T, 0, keepdims=True)

    def exchange_gain(i, pairs):
        gain_s[i] = jnp.broadcast_to(row_products(pairs), (8, 64))
        group = Group(gain_r.at[i])
        for k in range(1, 4):
            group.send(gain_s.at[i], gain_r.at[i, k - 1], z_peer(k))
        return group

    def gain_total(i, group):
        group.wait_recv()
        total = gain_s[i]
        for k in range(3):
            total = total + gain_r[i, k]
        return total[0:1]

    gain_f_group = exchange_gain(0, [(g_g, row_g), (g_u, row_u)])
    rs_last(4, [(g_q, o_q, 0, 512), (g_kv, o_kv, 512, 128)])
    gain_a_group = exchange_gain(1, [(g_q, row_q), (g_kv, row_kv)])
    rs_last(0, [(g_d, o_d, 0, FC)])
    rs_last(3, [(g_o, o_o, 0, 512)])
    chip_cols = pl.ds(pl.multiple_of((iy * 4 + ix) * 128, 128), 128)

    def own_gain(ref):
        v = ref[:, chip_cols]
        return jnp.where(core == 1, pltpu.roll(v, 64, 1), v)[:, 0:64]

    gain_f[...] = gain_total(0, gain_f_group) / own_gain(gf)
    gain_a[...] = gain_total(1, gain_a_group) / own_gain(ga)

    for group in groups:
        group.wait_recv()
    for group in groups:
        group.wait_send()
    wait_local(*[copy for copy in local if id(copy) not in local_done])


def store_kernel(*refs):
    n = 10
    src, dst, held = refs[:n], refs[n : 2 * n], refs[2 * n : 3 * n]
    wide, in_sem, out_sem = refs[3 * n :]
    moves = []
    for i in range(n):
        if i < 2:
            for j in range(4):
                rows = pl.ds(j * R, R)
                moves.append((src[i].at[rows], held[i].at[rows], dst[i].at[rows], (i, rows)))
        else:
            moves.append((src[i], held[i], dst[i], (i, None)))
    moves.sort(key=lambda move: move[3][0] != 1)
    fetches = []
    for k, (a, b, _, _) in enumerate(moves):
        copy = pltpu.make_async_copy(a, b, in_sem.at[k])
        copy.start()
        fetches.append(copy)
    stores = []
    for k, (_, b, c, (i, rows)) in enumerate(moves):
        fetches[k].wait()
        if i == 1:
            wide[rows, :] = b[...].astype(F32)
            b = wide.at[rows]
        copy = pltpu.make_async_copy(b, c, out_sem.at[k])
        copy.start()
        stores.append(copy)
    for copy in stores:
        copy.wait()


N_GROUPS = 76
N_LOCAL = 32


def per_device(
    hidden_in, block_order, w_query, w_keyval, w_output, w_gate, w_up, w_down,
    gain_attn, gain_ffn, cotangent,
):
    coarse, fine = rope_tables()
    any_spec = pl.BlockSpec(memory_space=pl.ANY)
    vmem = pl.BlockSpec(memory_space=pltpu.VMEM)
    smem = pl.BlockSpec(memory_space=pltpu.SMEM)
    shape = jax.ShapeDtypeStruct
    wide = (2, 4, 4, 2, 32, FC)
    turned = (4, 4, 2, 2, 32, T)
    half_turned = (4, 4, 2, 32, T)
    scratch = [
        pltpu.VMEM(s, t)
        for s, t in (
            ((1, D), F32), ((1, D), F32), ((2, 16, 128), F32), ((2, BLOCK, 128), F32),
            ((T, D), BF16), ((T, D), BF16),
            ((D, QC), BF16), ((D, 128), BF16), ((QC, D), BF16),
            (wide, BF16), (wide, BF16), ((11, 4, 32, D), BF16),
            ((2, 32, FC), BF16), ((2, 32, FC), BF16), ((64, QC), BF16), ((64, 128), BF16),
            ((T, D), BF16), ((8, T, 128), BF16),
            ((KEYS, 128), BF16), ((KEYS, 128), BF16),
            ((128, KEYS), BF16), ((144, KEYS), BF16),
            ((QUERIES, 128), BF16), ((T, 128), F32), ((T, 128), F32),
            ((KEYS, CHUNK), F32), ((KEYS, QUERIES), BF16),
            ((T, QC), BF16), ((T, QC), F32),
            ((T, D), BF16), ((4, 2, R, D), BF16), ((4, 2, R, D // 2), BF16),
            ((R, D), F32), ((R, D), F32),
            ((T, D), BF16), ((T, D), BF16), ((R, D), BF16), ((R, D), BF16),
            ((T, FC), F32), ((3, T, FC), BF16), ((3, T, FC), BF16),
            ((2, 4, 32, FC), BF16),
            (turned, BF16), (turned, BF16), (turned, BF16),
            (half_turned, BF16), (half_turned, BF16), (half_turned, BF16), (half_turned, BF16),
            ((T, QC), BF16), ((T, QC), BF16), ((T, QC), BF16),
            ((T, 128), BF16), ((T, 128), BF16),
            ((4, 2, T, 128), BF16), ((1, QUERIES), F32),
            ((3, 2, 2, 2, 32, FC), BF16), ((3, 2, 2, 4, 32, FC), BF16),
            ((3, 2, 2, 16, FC), BF16), ((3, 2, 2, 32, FC), BF16),
            ((2, 2, 2, 32, 1152), BF16), ((2, 2, 4, 32, 1152), BF16),
            ((2, 2, 16, 1152), BF16), ((2, 2, 32, 1152), BF16),
            ((64, QC), F32), ((64, 128), F32), ((64, QC), F32),
            ((64, FC), F32), ((64, FC), F32), ((64, FC), F32),
            ((2, 8, 64), F32), ((2, 3, 8, 64), F32),
        )
    ] + [
        pltpu.SemaphoreType.DMA((N_LOCAL,)),
        pltpu.SemaphoreType.DMA((N_GROUPS,)),
        pltpu.SemaphoreType.DMA((N_GROUPS,)),
    ]
    grads = (
        shape((64, QC), F32), shape((64, 128), F32), shape((64, QC), F32),
        shape((64, FC), F32), shape((64, FC), F32), shape((64, FC), F32),
        shape((1, 64), F32), shape((1, 64), F32),
    )
    outs = pl.pallas_call(
        layer_kernel,
        out_shape=(shape((T, D), BF16), shape((T, D), BF16)) + grads,
        in_specs=[smem] + [any_spec] * 12,
        out_specs=(any_spec,) * 8 + (vmem,) * 2,
        scratch_shapes=scratch,
        compiler_params=pltpu.CompilerParams(
            collective_id=0, has_side_effects=True, vmem_limit_bytes=65200 * 1024
        ),
    )(
        block_order, hidden_in.reshape(T, D), cotangent.reshape(T, D),
        w_query, w_keyval, w_output, w_gate.reshape(wide), w_up.reshape(wide),
        w_down.reshape(11, 4, 32, D),
        gain_attn.reshape(1, D), gain_ffn.reshape(1, D), coarse, fine,
    )
    outs = pl.pallas_call(
        store_kernel,
        out_shape=(shape((T, D), BF16), shape((T, D), F32)) + grads,
        in_specs=[any_spec] * 10,
        out_specs=(any_spec,) * 10,
        scratch_shapes=[pltpu.VMEM((T, D), BF16)] * 2
        + [pltpu.VMEM(g.shape, F32) for g in grads]
        + [
            pltpu.VMEM((T, D), F32),
            pltpu.SemaphoreType.DMA((16,)), pltpu.SemaphoreType.DMA((16,)),
        ],
        compiler_params=pltpu.CompilerParams(vmem_limit_bytes=65200 * 1024),
    )(*outs)
    bo, gi, g_q, g_kv, g_o, g_g, g_u, g_d, gain_a, gain_f = outs
    return (
        bo.reshape(1, T, D),
        gi.reshape(1, T, D),
        g_q,
        g_kv,
        g_o.T,
        g_g,
        g_u,
        g_d.T,
        gain_a.reshape(64),
        gain_f.reshape(64),
    )


def solution(mesh):
    return jax.shard_map(
        per_device,
        mesh=mesh,
        in_specs=(
            P("dp", "ctx", None),
            P("dp", None),
            P(None, "tensor"),
            P(None, "tensor"),
            P("tensor", None),
            P(None, "tensor"),
            P(None, "tensor"),
            P("tensor", None),
            P(),
            P(),
            P("dp", "ctx", None),
        ),
        out_specs=(
            P("dp", "ctx", None),
            P("dp", "ctx", None),
            P(("dp", "ctx"), "tensor"),
            P(("dp", "ctx"), "tensor"),
            P("tensor", ("dp", "ctx")),
            P(("dp", "ctx"), "tensor"),
            P(("dp", "ctx"), "tensor"),
            P("tensor", ("dp", "ctx")),
            P(("dp", "ctx")),
            P(("dp", "ctx")),
        ),
        check_vma=False,
    )
```

```python
import jax
import jax.numpy as jnp
import numpy as np
from jax import lax
from jax.experimental import pallas as pl
from jax.experimental.pallas import tpu as pltpu
from jax.sharding import PartitionSpec as P

MESH = pl.DeviceIdType.MESH
F32 = jnp.float32
BF16 = jnp.bfloat16
EPSILON = 1e-05
NEG_FILL = -1e30
ROPE_BASE = 10000.0

D = 2048
HD = 64
T = 192
BLOCK = 96
TA = 128
R = 48
QC = 512
FC = 1408
KEYS = 1536
PAIRS = 4
QUERIES = 1536
CHUNK = 512
GROUP = 768
CHIP_KEYS = 384
FF_TILES = ((0, 384), (384, 384), (768, 384), (1152, 256))


def rope_tables():
    half = HD // 2
    freq = ROPE_BASE ** (-np.arange(half, dtype=np.float64) / half)
    freq = np.tile(freq, 4)[None, :]
    coarse = np.arange(16, dtype=np.float64)[:, None] * BLOCK * freq
    fine = np.arange(BLOCK, dtype=np.float64)[:, None] * freq
    coarse = np.stack([np.cos(coarse), np.sin(coarse)]).astype(np.float32)
    fine = np.stack([np.cos(fine), np.sin(fine)]).astype(np.float32)
    return coarse, fine


def dot(a, b):
    return jnp.dot(a, b, preferred_element_type=F32)


def dot_nt(a, b):
    return lax.dot_general(a, b, (((1,), (1,)), ((), ())), preferred_element_type=F32)


def tiles(total, size):
    return [(s, min(size, total - s)) for s in range(0, total, size)]


def lane_of(shape):
    return lax.broadcasted_iota(jnp.int32, shape, len(shape) - 1)


def swap_halves(t):
    first = lane_of(t.shape) % HD < HD // 2
    return jnp.where(first, pltpu.roll(t, 96, 1), pltpu.roll(t, 32, 1))


def layer_kernel(
    order, x_h, c_h, wq_h, wkv_h, wo_h, wg_h, wu_h, wd_h, ga_h, gf_h, coarse_h, fine_h,
    bo, gi, o_q, o_kv, o_o, o_g, o_u, o_d, gain_a, gain_f,
    ga, gf, coarse, fine, x, cot, wq, wkv, wo, wg, wu, wd, row_g, row_u, row_q, row_kv,
    xn, kvall, kk, vv, kt, vt, qst, cos_t, sin_t, s_buf, pt, ob, rl,
    zs, z_near, z_far, mid, dmid, hn, da, bo_s, gi_s, dinner, act, act_p, g_first,
    xn_t, c_t, hn_t, xn_p, c_p, hn_p, da_p, ob_p, dqp, dqp_p, dkvp, dkvp_p,
    dkv_r, delta, r1f, r2f, r3f, r4f, r1a, r2a, r3a, r4a,
    gain_s, gain_r,
    local_sem, send_sem, recv_sem,
):
    g_g, g_u, g_d = (dinner.at[i * 64 : (i + 1) * 64] for i in range(3))
    g_q, g_o, g_kv = (s_buf.at[i * 64 : (i + 1) * 64] for i in range(3))
    g_kv = g_kv.at[:, 0:128]

    iy = lax.axis_index("dp")
    ictx = lax.axis_index("ctx")
    iz = lax.axis_index("tensor")
    ix = ictx // 2
    core = ictx % 2
    other = 1 - core

    def z_peer(k):
        return (iy, ictx, (iz + k) % 4)

    def ctx_peer(k):
        return (iy, (ictx + k) % 8, iz)

    def x_peer(k):
        return (iy, ((ix + k) % 4) * 2 + core, iz)

    def y_peer(k):
        return ((iy + k) % 4, ictx, iz)

    core_peer = (iy, ix * 2 + other, iz)

    local = []
    local_done = set()

    def copy_local(src, dst):
        copy = pltpu.make_async_copy(src, dst, local_sem.at[len(local)])
        copy.start()
        local.append(copy)
        return copy

    def wait_local(*copies):
        for copy in copies:
            copy.wait()
            local_done.add(id(copy))

    x_load = copy_local(x_h, x)
    table_loads = [
        copy_local(ga_h, ga), copy_local(gf_h, gf),
        copy_local(coarse_h, coarse), copy_local(fine_h, fine),
    ]
    wkv_load = copy_local(wkv_h, wkv)
    wq_load = copy_local(wq_h, wq)

    barrier = pltpu.get_barrier_semaphore()
    greeted = (
        [ctx_peer(k) for k in range(1, 8)]
        + [z_peer(k) for k in range(1, 4)]
        + [y_peer(1), y_peer(3)]
    )
    for peer in greeted:
        pl.semaphore_signal(barrier, inc=1, device_id=peer, device_id_type=MESH)

    groups = []

    class Group:
        def __init__(self, size):
            self.n = len(groups)
            self.size = size
            self.arrived = self.released = self.used = False
            groups.append(self)

        def copy(self, src, dst, peer):
            return pltpu.make_async_remote_copy(
                src_ref=src, dst_ref=dst, send_sem=send_sem.at[self.n],
                recv_sem=recv_sem.at[self.n], device_id=peer, device_id_type=MESH,
            )

        def send(self, src, dst, peer):
            self.used = True
            self.copy(src, dst, peer).start()

        def wait_recv(self):
            if self.used and not self.arrived:
                self.copy(self.size, self.size, core_peer).wait_recv()
                self.arrived = True

        def wait_send(self):
            if self.used and not self.released:
                self.copy(self.size, self.size, core_peer).wait_send()
                self.released = True

    def send_one(src, dst, peer):
        group = Group(dst)
        group.send(src, dst, peer)
        return group

    wait_local(*table_loads)
    pick = lax.broadcasted_iota(jnp.int32, (16, 128), 0)
    sign = jnp.where(lane_of((BLOCK, 128)) % HD < HD // 2, -1.0, 1.0).astype(F32)
    for b in range(2):
        chosen = pick == order[0, ictx * 2 + b]
        ca = jnp.sum(jnp.where(chosen, coarse[0], 0.0), 0, keepdims=True)
        sa = jnp.sum(jnp.where(chosen, coarse[1], 0.0), 0, keepdims=True)
        cos_t[b * BLOCK : (b + 1) * BLOCK, :] = ca * fine[0] - sa * fine[1]
        sin_t[b * BLOCK : (b + 1) * BLOCK, :] = (sa * fine[0] + ca * fine[1]) * sign

    def rot(t):
        return t * cos_t[...] + swap_halves(t) * sin_t[...]

    def rot_back(t):
        return t * cos_t[...] - swap_halves(t) * sin_t[...]

    def inv_rms(v):
        return lax.rsqrt(jnp.mean(v * v, -1, keepdims=True) + EPSILON)

    low_lane = lane_of((T, 128)) < HD
    low_a, low_b = low_lane[0:TA], low_lane[0 : T - TA]

    wait_local(x_load)
    for i in range(4):
        rows = x[i * R : (i + 1) * R, :].astype(F32)
        xn[i * R : (i + 1) * R, :] = (rows * inv_rms(rows) * ga[...]).astype(BF16)
    wait_local(wkv_load)
    cot_load = copy_local(c_h, cot)
    wd_load = copy_local(wd_h, wd)
    normed = xn[...]
    kvp = dot(normed, wkv[...])
    kvall[ictx] = jnp.where(low_lane, rot(kvp), kvp).astype(BF16)
    pl.semaphore_wait(barrier, len(greeted))
    kv_group = Group(kvall.at[pl.ds(0, 7)])
    for k in (4, 5, 3, 2, 6, 7, 1):
        kv_group.send(kvall.at[ictx], kvall.at[ictx], ctx_peer(k))
    wait_local(wq_load)
    wo_load = copy_local(wo_h, wo)
    wg_load = copy_local(wg_h, wg)
    wu_load = copy_local(wu_h, wu)
    own_h, own_a, own_b = iy // 2, (iy % 2) * 2 + ix // 2, (ix % 2) * 2 + core
    own_rows = pl.ds(pl.multiple_of(((iy * 4 + ix) * 2 + core) * 64, 64), 64)
    row_loads = [
        copy_local(wg_h.at[own_h, own_a, own_b], row_g),
        copy_local(wu_h.at[own_h, own_a, own_b], row_u),
        copy_local(wq_h.at[own_rows], row_q),
        copy_local(wkv_h.at[own_rows], row_kv),
    ]

    def by_query(pair, value, ref):
        for i in range(2):
            h = pair * 2 + i
            one = jnp.where(low_lane, value, 0.0) if i == 0 else jnp.where(low_lane, 0.0, value)
            one = one.astype(BF16)
            ref[h * TA : (h + 1) * TA, :] = one[0:TA]
            ref[8 * TA + h * 64 : 8 * TA + (h + 1) * 64, :] = one[TA:T]

    for s, n in tiles(QC, 256):
        qp = dot(normed, wq[:, s : s + n])
        for j in range(n // 128):
            by_query(s // 128 + j, rot(qp[:, j * 128 : (j + 1) * 128]) * (HD ** -0.5), qst)

    turned = (4, 4, 2, 2, 32, T)
    xn_t[...] = normed.T.reshape(turned)
    xnt_copy = send_one(xn_t.at[:, :, other], xn_p, core_peer)
    wait_local(cot_load)
    cot_rows = cot[...]
    c_t[...] = cot_rows.T.reshape(turned)
    ct_copy = send_one(c_t.at[:, :, other], c_p, core_peer)
    wait_local(wd_load)
    for s, n in tiles(FC, 512):
        rows = slice(s // 128, (s + n) // 128)
        dinner[:, s : s + n] = dot_nt(cot_rows, wd[rows].reshape(n, D))

    kv_group.wait_recv()
    for j in range(8):
        wide = kvall[j].astype(F32)
        rolled = pltpu.roll(wide, HD, 1)
        rows = pl.ds(j * T, T)
        kk[rows, :] = jnp.where(low_lane, wide, rolled).astype(BF16)
        vv[rows, :] = jnp.where(low_lane, rolled, wide).astype(BF16)
    kv_t = kvall[...].reshape(KEYS, 128).T
    kt[0:HD, :] = kv_t[0:HD]
    kt[HD : 2 * HD, :] = kv_t[0:HD]
    vt[0:HD, :] = kv_t[HD : 2 * HD]
    vt[HD : 2 * HD, :] = kv_t[HD : 2 * HD]
    vt[2 * HD : 2 * HD + 16, :] = jnp.ones((16, KEYS), BF16)

    lane = lane_of((1, CHUNK))
    token = lane % TA
    start_0, start_1 = order[0, ictx * 2] * BLOCK, order[0, ictx * 2 + 1] * BLOCK
    place_a = jnp.where(token >= BLOCK, start_1 + token - BLOCK, start_0 + token)
    place_b = start_1 + (TA - BLOCK) + lane % 64
    key_row = lax.broadcasted_iota(jnp.int32, (BLOCK, CHUNK), 0)

    def attend(chunk):
        q_place = place_a if chunk < 2 else place_b
        lanes = slice(chunk * CHUNK, (chunk + 1) * CHUNK)
        top = jnp.full((8, CHUNK), NEG_FILL, F32)
        for r0 in range(0, KEYS, GROUP):
            scores = dot_nt(kk[r0 : r0 + GROUP, :], qst[lanes, :])
            for b in range(GROUP // BLOCK):
                limit = q_place - order[0, r0 // BLOCK + b] * BLOCK
                rows = slice(b * BLOCK, (b + 1) * BLOCK)
                seen = jnp.where(key_row <= limit, scores[rows], NEG_FILL)
                s_buf[r0 + b * BLOCK : r0 + (b + 1) * BLOCK, :] = seen
                top = jnp.maximum(top, jnp.max(seen.reshape(BLOCK // 8, 8, CHUNK), 0))
        top = jnp.max(top, 0, keepdims=True)
        for r0 in range(0, KEYS, GROUP):
            rows = slice(r0, r0 + GROUP)
            pt[rows, lanes] = jnp.exp(s_buf[rows, :] - top).astype(BF16)
        summed = dot(vt[...], pt[:, lanes])
        inv = 1.0 / summed[2 * HD : 2 * HD + 1]
        out = summed[0 : 2 * HD] * inv
        inv = jnp.broadcast_to(inv, (2 * HD, CHUNK))
        if chunk < 2:
            for j in range(2):
                pair = slice((chunk * 2 + j) * 128, (chunk * 2 + j + 1) * 128)
                one, two = slice(j * 256, j * 256 + 128), slice(j * 256 + 128, j * 256 + 256)
                ob[0:TA, pair] = jnp.where(low_a, out[:, one].T, out[:, two].T).astype(BF16)
                rl[0:TA, pair] = jnp.where(low_a, inv[:, one].T, inv[:, two].T)
        else:
            for p in range(PAIRS):
                pair = slice(p * 128, (p + 1) * 128)
                o2, i2 = out[:, pair].T, inv[:, pair].T
                ob[TA:T, pair] = jnp.where(low_b, o2[0:64], o2[64:128]).astype(BF16)
                rl[TA:T, pair] = jnp.where(low_b, i2[0:64], i2[64:128])

    def z_rows(part, z):
        if part == 0:
            return pl.ds(pl.multiple_of(z * 32, 32), 32)
        return pl.ds(pl.multiple_of(TA + z * 16, 16), 16)

    kept = (slice(0, 32), slice(32, 48))
    cols_l, cols_r, all_cols = pl.ds(0, D // 2), pl.ds(D // 2, D // 2), pl.ds(0, D)
    zp, zm, z2 = (iz + 1) % 4, (iz + 3) % 4, (iz + 2) % 4

    class ZScatter:
        def __init__(self, src, n, part):
            self.src, self.n, self.part = src, n, part
            self.far = Group(z_far.at[n, :, kept[part]])
            self.near = Group(z_near.at[n, :, kept[part]])

        def first(self, cols=(0, D // 2, D // 2)):
            l, r, width = cols
            src, n, part = self.src, self.n, self.part
            keep = kept[part]
            left, right = pl.ds(l, width), pl.ds(r, width)
            if l is not None:
                far = z_far.at[n, 0, keep, left]
                self.far.send(src.at[z_rows(part, z2), left], far, z_peer(1))
            if r is not None:
                far = z_far.at[n, 1, keep, pl.ds(r - D // 2, width)]
                self.far.send(src.at[z_rows(part, z2), right], far, z_peer(3))
            if l is not None:
                near = z_near.at[n, 1, keep, left]
                self.near.send(src.at[z_rows(part, zm), left], near, z_peer(3))
            if r is not None:
                near = z_near.at[n, 0, keep, right]
                self.near.send(src.at[z_rows(part, zp), right], near, z_peer(1))

        def second(self):
            src, n, part = self.src, self.n, self.part
            keep = kept[part]
            self.far.wait_recv()
            for way, z, cols, k in ((0, zp, cols_l, 1), (1, zm, cols_r, 3)):
                rows = z_rows(part, z)
                total = src[rows, cols].astype(F32) + z_far[n, way, keep, :].astype(F32)
                src[rows, cols] = total.astype(BF16)
                self.near.send(src.at[rows, cols], z_near.at[n, way, keep, cols], z_peer(k))

        def result(self):
            self.near.wait_recv()
            total = self.src[z_rows(self.part, iz), :].astype(F32)
            for way in range(2):
                total = total + z_near[self.n, way, kept[self.part], :].astype(F32)
            return total

        def wait_send(self):
            self.far.wait_send()
            self.near.wait_send()

    class ZGather:
        def __init__(self, buf, part, own=None):
            self.buf, self.part = buf, part
            self.far = Group(z_far.at[0, :, kept[part]])
            self.near = Group(z_near.at[0, :, kept[part]])
            rows = z_rows(part, iz)
            for cols, way, k, group in (
                (cols_l, 0, 1, self.far), (cols_r, 1, 3, self.far),
                (cols_r, 0, 1, self.near), (cols_l, 1, 3, self.near),
            ):
                src = buf.at[rows, cols] if own is None else own.at[kept[part], cols]
                group.send(src, buf.at[rows, cols], z_peer(k))

        def second(self):
            self.far.wait_recv()
            for z, cols, k in ((zm, cols_l, 1), (zp, cols_r, 3)):
                piece = self.buf.at[z_rows(self.part, z), cols]
                self.near.send(piece, piece, z_peer(k))

        def wait_recv(self):
            self.near.wait_recv()

    def project_out(part):
        rows = slice(0, TA) if part == 0 else slice(TA, T)
        scatter = ZScatter(zs, 0, part)
        for l in (0, 512):
            for s in (l, l + D // 2):
                zs[rows, s : s + 512] = dot(ob[rows, :], wo[:, s : s + 512]).astype(BF16)
            scatter.first((l, l + D // 2, 512))
        return scatter

    attend(0)
    attend(1)
    wait_local(wo_load)
    attn_sums = [project_out(0)]
    attend(2)
    attn_sums.append(project_out(1))
    ob_copy = send_one(ob, ob_p, core_peer)

    hn_parts = []

    def norm(part):
        m = x[z_rows(part, iz), :].astype(F32) + attn_sums[part].result()
        mid[kept[part], :] = m
        hn[z_rows(part, iz), :] = (m * inv_rms(m) * gf[...]).astype(BF16)
        hn_parts.append(ZGather(hn, part))

    attn_sums[0].second()
    attn_sums[1].second()
    norm(0)
    norm(1)
    hn_parts[0].second()
    hn_parts[1].second()

    xp, xm, x2 = (ix + 1) % 4, (ix + 3) % 4, (ix + 2) % 4
    yp, ym, y2 = (iy + 1) % 4, (iy + 3) % 4, (iy + 2) % 4

    def own_part(ref):
        return lambda dy, dx, h: ref[dy, dx, core, h]

    def partner_part(ref):
        return lambda dy, dx, h: ref[dy, dx, h]

    all4 = pl.ds(0, 4)
    first_rows = [(all4, x2, 0), (y2, all4, 1)]
    other_rows = [(all4, dx, 0) for dx in (xp, xm, ix)] + [(dy, all4, 1) for dy in (yp, ym, iy)]

    def weight_grad(part, which, own_t, partner_t, own_b, partner_b, b0=0, n=None):
        ref, half, part_c0, part_n, _, _ = parts[part]
        n = part_n if n is None else n
        early = which is first_rows and part < 3
        get_own, get_partner = own_part(own_t), partner_part(partner_t)
        a_own = jnp.concatenate([get_own(*i).reshape(128, T) for i in which], 0)
        a_partner = jnp.concatenate([get_partner(*i).reshape(128, T) for i in which], 0)
        for s, w in tiles(n, 256):
            s = s + b0
            r = dot(a_own, own_b[:, s : s + w]) + dot(a_partner, partner_b[:, s : s + w])
            r = r.astype(BF16)
            cols = slice(part_c0 + s, part_c0 + s + w)
            for i, (dy, dx, h) in enumerate(which):
                rows = r[i * 128 : (i + 1) * 128].reshape(4, 32, w)
                if early:
                    g_first[part, i, :, :, cols] = rows
                else:
                    ref[half, dy, dx, h, :, cols] = rows

    f_bufs = [[r.at[i] for r in (r1f, r2f, r3f, r4f)] for i in range(3)]
    a_bufs = [r1a, r2a, r3a, r4a]
    parts = [
        (wg, 1, 0, FC, f_bufs[0], 0),
        (wg, 0, 0, FC, f_bufs[1], 0),
        (wu, 0, 0, FC, f_bufs[2], 0),
        (wu, 1, 0, 512, a_bufs, 0),
        (wu, 1, 512, 512, a_bufs, 512),
        (wu, 1, 1024, 128, a_bufs, 1024),
    ]
    flights = {}
    lo2, hi2 = pl.ds(0, 2), pl.ds(2, 2)
    all32, lo16, hi16 = pl.ds(0, 32), pl.ds(0, 16), pl.ds(16, 16)

    def g_index(part, dy, dx, h, rows=None):
        ref, half, c0, n, _, _ = parts[part]
        return (half, dy, dx, h, all32 if rows is None else rows, pl.ds(c0, n))

    def first_piece(part, flow, pair, s, n):
        if part < 3:
            return g_first.at[part, flow, pair, :, pl.ds(s, n)]
        ref, half, c0, _, _, _ = parts[part]
        dy, dx = (pair, x2) if flow == 0 else (y2, pair)
        return ref.at[half, dy, dx, flow, :, pl.ds(c0 + s, n)]

    def outgoing(part, step, s, n):
        if step == 0:
            return tuple(
                tuple(first_piece(part, flow, pair, s, n) for pair in (lo2, hi2))
                for flow in range(2)
            )
        if step == 1:
            index = (
                (g_index(part, all4, xp, 0), g_index(part, all4, xm, 0)),
                (g_index(part, yp, all4, 1), g_index(part, ym, all4, 1)),
            )
        elif step == 2:
            index = (
                (g_index(part, y2, ix, 0, lo16), g_index(part, y2, ix, 0, hi16)),
                (g_index(part, iy, x2, 1, lo16), g_index(part, iy, x2, 1, hi16)),
            )
        else:
            index = (
                (g_index(part, yp, ix, 0), g_index(part, ym, ix, 0)),
                (g_index(part, iy, xp, 1), g_index(part, iy, xm, 1)),
            )
        ref = parts[part][0]
        return tuple(tuple(ref.at[i] for i in flow) for flow in index)

    def landing(part, step, flow, way, s=0, n=None):
        _, _, _, part_n, bufs, b0 = parts[part]
        return bufs[step].at[flow, way, ..., pl.ds(b0 + s, part_n if n is None else n)]

    def rs_send(part, step, s=0, n=None, flows=(0, 1)):
        _, _, _, part_n, bufs, b0 = parts[part]
        n = part_n if n is None else n
        out = outgoing(part, step, s, n)
        for flow in flows:
            if (part, step, flow) not in flights:
                flights[part, step, flow] = Group(bufs[step].at[flow, ..., pl.ds(b0, part_n)])
            group = flights[part, step, flow]
            along_x = (flow == 0) == (step < 2)
            for way, k in ((0, 1), (1, 3)):
                peer = x_peer(k) if along_x else y_peer(k)
                group.send(out[flow][way], landing(part, step, flow, way, s, n), peer)

    def add_in(ref, index, *arrived):
        total = ref[index].astype(F32)
        for a in arrived:
            total = total + a[...].astype(F32)
        ref[index] = total.astype(BF16)

    def rs_recv(part, step, flows=(0, 1)):
        ref = parts[part][0]
        for flow in flows:
            flights[part, step, flow].wait_recv()
            got = [landing(part, step, flow, way) for way in range(2)]
            if step == 0:
                if flow == 0:
                    add_in(ref, g_index(part, lo2, xp, 0), got[0])
                    add_in(ref, g_index(part, hi2, xm, 0), got[1])
                else:
                    add_in(ref, g_index(part, yp, lo2, 1), got[0])
                    add_in(ref, g_index(part, ym, hi2, 1), got[1])
            elif step == 1:
                if flow == 0:
                    add_in(ref, g_index(part, all4, ix, 0), *got)
                else:
                    add_in(ref, g_index(part, iy, all4, 1), *got)
            elif step == 2:
                if flow == 0:
                    add_in(ref, g_index(part, yp, ix, 0, lo16), got[0])
                    add_in(ref, g_index(part, ym, ix, 0, hi16), got[1])
                else:
                    add_in(ref, g_index(part, iy, xp, 1, lo16), got[0])
                    add_in(ref, g_index(part, iy, xm, 1, hi16), got[1])

    def rs_turn(part, step, flows=(0, 1)):
        for flow in flows:
            rs_recv(part, step, (flow,))
            rs_send(part, step + 1, flows=(flow,))

    def rs_last(part, outs):
        rs_recv(part, 3)
        ref = parts[part][0]
        for flow in range(2):
            total = ref[g_index(part, iy, ix, flow)].astype(F32)
            for way in range(2):
                total = total + landing(part, 3, flow, way)[...].astype(F32)
            for stage, out, s, n in outs:
                stage[flow * 32 : (flow + 1) * 32, :] = total[:, s : s + n]
        for stage, out, s, n in outs:
            copy_local(stage, out)

    wait_local(wg_load, wu_load)
    for part in hn_parts:
        part.wait_recv()
    hidden = hn[...]
    hn_t[...] = hidden.T.reshape(turned)
    hnt_copy = send_one(hn_t.at[:, :, other], hn_p, core_peer)
    act_groups = [Group(act_p.at[:, :, pl.ds(s, n)]) for s, n in FF_TILES]

    def first_of_tile(t):
        s, n = FF_TILES[t]
        act_groups[t].wait_recv()
        for part, own_t, partner_t in ((0, c_t, c_p), (1, hn_t, hn_p), (2, hn_t, hn_p)):
            weight_grad(part, first_rows, own_t, partner_t, act.at[part], act_p.at[part], s, n)
            rs_send(part, 0, s, n)

    for t, (s, n) in enumerate(FF_TILES):
        cols = slice(s, s + n)
        g = dot(hidden, wg[:, :, :, :, :, cols].reshape(D, n))
        u = dot(hidden, wu[:, :, :, :, :, cols].reshape(D, n))
        sig = 1.0 / (1.0 + jnp.exp(-g))
        a = g * sig
        di = dinner[:, cols]
        act[0, :, cols] = (a * u).astype(BF16)
        act[1, :, cols] = (di * u * sig * (1.0 + g * (1.0 - sig))).astype(BF16)
        act[2, :, cols] = (di * a).astype(BF16)
        piece = pl.ds(s, n)
        act_groups[t].send(act.at[:, :, piece], act_p.at[:, :, piece], core_peer)
        if t == 0:
            ct_copy.wait_recv()
            hnt_copy.wait_recv()
        else:
            first_of_tile(t - 1)

    for scatter in attn_sums:
        scatter.wait_send()
    dhn_sums = [ZScatter(zs, 1, part) for part in range(2)]
    for t in (0, 2, 1, 3):
        cols = slice(t * 512, (t + 1) * 512)
        block = (t // 2, slice((t % 2) * 2, (t % 2) * 2 + 2))
        r = dot_nt(act[1], wg[block].reshape(512, FC)) + dot_nt(act[2], wu[block].reshape(512, FC))
        zs[:, cols] = r.astype(BF16)
        dhn_sums[0].first((t * 512, None, 512) if t < 2 else (None, t * 512, 512))
        if t == 0:
            first_of_tile(3)
    dhn_sums[1].first()
    inner = act[0]
    for s, n in tiles(D, 512):
        xn[:, s : s + n] = dot(inner, wd[..., s : s + n].reshape(FC, n)).astype(BF16)
    weight_grad(0, other_rows, c_t, c_p, act.at[0], act_p.at[0])
    dhn_sums[0].second()
    rs_turn(0, 0)
    dhn_sums[1].second()
    weight_grad(1, other_rows, hn_t, hn_p, act.at[1], act_p.at[1])
    weight_grad(2, other_rows, hn_t, hn_p, act.at[2], act_p.at[2])

    da_parts = []

    def norm_back(part):
        m = mid[kept[part], :]
        r2 = inv_rms(m)
        mhat = m * r2
        scaled = dhn_sums[part].result() * gf[...]
        rows = z_rows(part, iz)
        dm = cot[rows, :].astype(F32) + r2 * (
            scaled - mhat * jnp.mean(scaled * mhat, -1, keepdims=True)
        )
        dmid[kept[part], :] = dm
        da[rows, :] = dm.astype(BF16)
        da_parts.append(ZGather(da, part))

    norm_back(0)
    norm_back(1)
    rs_turn(1, 0)
    da_parts[0].second()
    da_parts[1].second()
    rs_turn(2, 0, (1,))
    rs_turn(0, 1)

    for part in da_parts:
        part.wait_recv()
    ffn_sums = [ZScatter(xn, 2, part) for part in range(2)]
    for scatter in ffn_sums:
        scatter.first()
    grad_attn = da[...]
    for s, n in tiles(QC, 256):
        grad_rows = dot_nt(grad_attn, wo[s : s + n, :])
        for j in range(n // 128):
            p = s // 128 + j
            pair = slice(p * 128, (p + 1) * 128)
            g = grad_rows[:, j * 128 : (j + 1) * 128] * rl[:, pair]
            by_query(p, g, kk)
            by_row = (g * ob[:, pair].astype(F32)).T
            for i in range(2):
                h = p * 2 + i
                sums = jnp.sum(by_row[i * HD : (i + 1) * HD], 0, keepdims=True)
                delta[:, h * TA : (h + 1) * TA] = sums[:, 0:TA]
                delta[:, 8 * TA + h * 64 : 8 * TA + (h + 1) * 64] = sums[:, TA:T]
    ct_copy.wait_send()
    c_t[...] = grad_attn.T.reshape(turned)
    dat_copy = send_one(c_t.at[:, :, other], da_p, core_peer)
    dob = kk

    kv_group.wait_send()
    dkv_group = Group(kvall.at[pl.ds(0, 7)])
    for i, step in enumerate((2, 1, 3, 0)):
        chip = (ix + step) % 4
        rows = pl.ds(pl.multiple_of(chip * CHIP_KEYS, CHIP_KEYS), CHIP_KEYS)
        weights = pt[rows, :]
        dv = dot(weights, dob[...])
        for s, n in tiles(QUERIES, CHUNK):
            lanes = slice(s, s + n)
            grad_weights = dot_nt(vv[rows, :], dob[lanes, :])
            pt[rows, lanes] = (
                weights[:, lanes].astype(F32) * (grad_weights - delta[:, lanes])
            ).astype(BF16)
        dk = dot(pt[rows, :], qst[...])
        both = jnp.where(
            lane_of((CHIP_KEYS, 128)) < HD, dk + pltpu.roll(dk, HD, 1), dv + pltpu.roll(dv, HD, 1)
        ).astype(BF16)
        for c in range(2):
            kvall[chip * 2 + c] = both[c * T : (c + 1) * T]
        for c, goal in ((0, core), (1, other)):
            if step != 0 or c == 1:
                dkv_group.send(kvall.at[chip * 2 + goal], dkv_r.at[i, c], (iy, chip * 2 + goal, iz))
        if i == 2:
            dat_copy.wait_recv()
            ob_copy.wait_recv()
            weight_grad(3, first_rows, c_t, da_p, ob, ob_p)
            rs_send(3, 0)
            rs_turn(2, 0, (0,))
    for scatter in ffn_sums:
        scatter.second()
    dq_t = dot(kt[...], pt[...]) * (HD ** -0.5)
    for p in range(PAIRS):
        a0 = dq_t[:, p * 256 : p * 256 + 128].T
        a1 = dq_t[:, p * 256 + 128 : p * 256 + 256].T
        b = dq_t[:, 8 * TA + p * 128 : 8 * TA + (p + 1) * 128].T
        dq = jnp.concatenate(
            [jnp.where(low_a, a0, a1), jnp.where(low_b, b[0:64], b[64:128])], 0
        )
        dqp[:, p * 128 : (p + 1) * 128] = rot_back(dq).astype(BF16)
    dqp_copy = send_one(dqp, dqp_p, core_peer)

    xnt_copy.wait_recv()
    dqp_copy.wait_recv()
    weight_grad(4, first_rows, xn_t, xn_p, dqp, dqp_p)
    rs_send(4, 0)
    rs_turn(1, 1)

    dkv_group.wait_recv()
    home = kvall[ictx].astype(F32) + dkv_r[3, 1].astype(F32)
    for i in range(3):
        for c in range(2):
            home = home + dkv_r[i, c].astype(F32)
    dkvp[...] = jnp.where(low_lane, rot_back(home), home).astype(BF16)
    dkvp_copy = send_one(dkvp, dkvp_p, core_peer)
    for scatter in dhn_sums:
        scatter.wait_send()
    q_rows, kv_rows = dqp[...], dkvp[...]
    dxn_sums = [ZScatter(zs, 3, part) for part in range(2)]
    for l in (0, 512):
        for s in (l, l + D // 2):
            cols = slice(s, s + 512)
            r = dot_nt(q_rows, wq[cols, :]) + dot_nt(kv_rows, wkv[cols, :])
            zs[:, cols] = r.astype(BF16)
        dxn_sums[0].first((l, l + D // 2, 512))
    dxn_sums[1].first()

    dkvp_copy.wait_recv()
    weight_grad(5, first_rows, xn_t, xn_p, dkvp, dkvp_p)
    rs_send(5, 0)
    weight_grad(3, other_rows, c_t, da_p, ob, ob_p)
    dxn_sums[0].second()
    dxn_sums[1].second()
    bo_parts = []
    for part in range(2):
        bo_s[kept[part], :] = (mid[kept[part], :] + ffn_sums[part].result()).astype(BF16)
        copy_local(bo_s.at[kept[part]], bo.at[z_rows(part, iz)])
        bo_parts.append(ZGather(bo, part, bo_s))
    weight_grad(4, other_rows, xn_t, xn_p, dqp, dqp_p)
    weight_grad(5, other_rows, xn_t, xn_p, dkvp, dkvp_p)
    rs_turn(3, 0)
    rs_turn(4, 0)
    rs_turn(5, 0)
    rs_turn(0, 2)

    gi_parts = []

    def first_norm_back(part):
        rows = x[z_rows(part, iz), :].astype(F32)
        r1 = inv_rms(rows)
        xhat = rows * r1
        scaled = dxn_sums[part].result() * ga[...]
        gi_s[kept[part], :] = (
            dmid[kept[part], :]
            + r1 * (scaled - xhat * jnp.mean(scaled * xhat, -1, keepdims=True))
        ).astype(BF16)
        copy_local(gi_s.at[kept[part]], gi.at[z_rows(part, iz)])
        gi_parts.append(ZGather(gi, part, gi_s))

    first_norm_back(0)
    first_norm_back(1)
    for part in bo_parts:
        part.second()
    rs_turn(2, 1)
    rs_turn(1, 2)
    gi_parts[0].second()
    gi_parts[1].second()
    rs_turn(3, 1)
    rs_turn(4, 1)
    rs_turn(5, 1)
    rs_last(0, [(g_d, o_d, 0, FC)])
    rs_turn(2, 2)
    rs_last(1, [(g_g, o_g, 0, FC)])
    rs_turn(4, 2)
    rs_turn(5, 2)
    rs_turn(3, 2)
    rs_last(2, [(g_u, o_u, 0, FC)])

    wait_local(*row_loads)

    def row_products(pairs):
        total = jnp.zeros((64, 128), F32)
        for grad, weight in pairs:
            n = grad.shape[-1]
            w = weight[...].reshape(64, n)
            for s, _ in tiles(n, 128):
                total = total + grad[:, s : s + 128] * w[:, s : s + 128].astype(F32)
        return jnp.sum(total.T, 0, keepdims=True)

    def exchange_gain(i, pairs):
        gain_s[i] = jnp.broadcast_to(row_products(pairs), (8, 64))
        group = Group(gain_r.at[i])
        for k in range(1, 4):
            group.send(gain_s.at[i], gain_r.at[i, k - 1], z_peer(k))
        return group

    def gain_total(i, group):
        group.wait_recv()
        total = gain_s[i]
        for k in range(3):
            total = total + gain_r[i, k]
        return total[0:1]

    gain_f_group = exchange_gain(0, [(g_g, row_g), (g_u, row_u)])
    rs_last(4, [(g_q, o_q, 0, 512)])
    rs_last(5, [(g_kv, o_kv, 0, 128)])
    gain_a_group = exchange_gain(1, [(g_q, row_q), (g_kv, row_kv)])
    rs_last(3, [(g_o, o_o, 0, 512)])
    chip_cols = pl.ds(pl.multiple_of((iy * 4 + ix) * 128, 128), 128)

    def own_gain(ref):
        v = ref[:, chip_cols]
        return jnp.where(core == 1, pltpu.roll(v, 64, 1), v)[:, 0:64]

    gain_f[...] = gain_total(0, gain_f_group) / own_gain(gf)
    gain_a[...] = gain_total(1, gain_a_group) / own_gain(ga)

    for group in groups:
        group.wait_recv()
    for group in groups:
        group.wait_send()
    wait_local(*[copy for copy in local if id(copy) not in local_done])


def store_kernel(*refs):
    n = 10
    src, dst, held = refs[:n], refs[n : 2 * n], refs[2 * n : 3 * n]
    wide, in_sem, out_sem = refs[3 * n :]
    moves = []
    for i in range(n):
        if i < 2:
            for j in range(4):
                rows = pl.ds(j * R, R)
                moves.append((src[i].at[rows], held[i].at[rows], dst[i].at[rows], (i, rows)))
        else:
            moves.append((src[i], held[i], dst[i], (i, None)))
    moves.sort(key=lambda move: move[3][0] != 1)
    fetches = []
    for k, (a, b, _, _) in enumerate(moves):
        copy = pltpu.make_async_copy(a, b, in_sem.at[k])
        copy.start()
        fetches.append(copy)
    stores = []
    for k, (_, b, c, (i, rows)) in enumerate(moves):
        fetches[k].wait()
        if i == 1:
            wide[rows, :] = b[...].astype(F32)
            b = wide.at[rows]
        copy = pltpu.make_async_copy(b, c, out_sem.at[k])
        copy.start()
        stores.append(copy)
    for copy in stores:
        copy.wait()


N_GROUPS = 95
N_LOCAL = 26


def per_device(
    hidden_in, block_order, w_query, w_keyval, w_output, w_gate, w_up, w_down,
    gain_attn, gain_ffn, cotangent,
):
    coarse, fine = rope_tables()
    any_spec = pl.BlockSpec(memory_space=pl.ANY)
    vmem = pl.BlockSpec(memory_space=pltpu.VMEM)
    smem = pl.BlockSpec(memory_space=pltpu.SMEM)
    shape = jax.ShapeDtypeStruct
    wide = (2, 4, 4, 2, 32, FC)
    turned = (4, 4, 2, 2, 32, T)
    half_turned = (4, 4, 2, 32, T)
    scratch = [
        pltpu.VMEM(s, t)
        for s, t in (
            ((1, D), F32), ((1, D), F32), ((2, 16, 128), F32), ((2, BLOCK, 128), F32),
            ((T, D), BF16), ((T, D), BF16),
            ((D, QC), BF16), ((D, 128), BF16), ((QC, D), BF16),
            (wide, BF16), (wide, BF16), ((11, 4, 32, D), BF16),
            ((2, 32, FC), BF16), ((2, 32, FC), BF16), ((64, QC), BF16), ((64, 128), BF16),
            ((T, D), BF16), ((8, T, 128), BF16),
            ((KEYS, 128), BF16), ((KEYS, 128), BF16),
            ((128, KEYS), BF16), ((144, KEYS), BF16),
            ((QUERIES, 128), BF16), ((T, 128), F32), ((T, 128), F32),
            ((KEYS, CHUNK), F32), ((KEYS, QUERIES), BF16),
            ((T, QC), BF16), ((T, QC), F32),
            ((T, D), BF16), ((4, 2, R, D), BF16), ((4, 2, R, D // 2), BF16),
            ((R, D), F32), ((R, D), F32),
            ((T, D), BF16), ((T, D), BF16), ((R, D), BF16), ((R, D), BF16),
            ((T, FC), F32), ((3, T, FC), BF16), ((3, T, FC), BF16),
            ((3, 2, 4, 32, FC), BF16),
            (turned, BF16), (turned, BF16), (turned, BF16),
            (half_turned, BF16), (half_turned, BF16), (half_turned, BF16), (half_turned, BF16),
            ((T, QC), BF16), ((T, QC), BF16), ((T, QC), BF16),
            ((T, 128), BF16), ((T, 128), BF16),
            ((4, 2, T, 128), BF16), ((1, QUERIES), F32),
            ((3, 2, 2, 2, 32, FC), BF16), ((3, 2, 2, 4, 32, FC), BF16),
            ((3, 2, 2, 16, FC), BF16), ((3, 2, 2, 32, FC), BF16),
            ((2, 2, 2, 32, 1152), BF16), ((2, 2, 4, 32, 1152), BF16),
            ((2, 2, 16, 1152), BF16), ((2, 2, 32, 1152), BF16),
            ((2, 8, 64), F32), ((2, 3, 8, 64), F32),
        )
    ] + [
        pltpu.SemaphoreType.DMA((N_LOCAL,)),
        pltpu.SemaphoreType.DMA((N_GROUPS,)),
        pltpu.SemaphoreType.DMA((N_GROUPS,)),
    ]
    grads = (
        shape((64, QC), F32), shape((64, 128), F32), shape((64, QC), F32),
        shape((64, FC), F32), shape((64, FC), F32), shape((64, FC), F32),
        shape((1, 64), F32), shape((1, 64), F32),
    )
    outs = pl.pallas_call(
        layer_kernel,
        out_shape=(shape((T, D), BF16), shape((T, D), BF16)) + grads,
        in_specs=[smem] + [any_spec] * 12,
        out_specs=(any_spec,) * 8 + (vmem,) * 2,
        scratch_shapes=scratch,
        compiler_params=pltpu.CompilerParams(
            collective_id=0, has_side_effects=True, vmem_limit_bytes=65200 * 1024
        ),
    )(
        block_order, hidden_in.reshape(T, D), cotangent.reshape(T, D),
        w_query, w_keyval, w_output, w_gate.reshape(wide), w_up.reshape(wide),
        w_down.reshape(11, 4, 32, D),
        gain_attn.reshape(1, D), gain_ffn.reshape(1, D), coarse, fine,
    )
    outs = pl.pallas_call(
        store_kernel,
        out_shape=(shape((T, D), BF16), shape((T, D), F32)) + grads,
        in_specs=[any_spec] * 10,
        out_specs=(any_spec,) * 10,
        scratch_shapes=[pltpu.VMEM((T, D), BF16)] * 2
        + [pltpu.VMEM(g.shape, F32) for g in grads]
        + [
            pltpu.VMEM((T, D), F32),
            pltpu.SemaphoreType.DMA((16,)), pltpu.SemaphoreType.DMA((16,)),
        ],
        compiler_params=pltpu.CompilerParams(vmem_limit_bytes=65200 * 1024),
    )(*outs)
    bo, gi, g_q, g_kv, g_o, g_g, g_u, g_d, gain_a, gain_f = outs
    return (
        bo.reshape(1, T, D),
        gi.reshape(1, T, D),
        g_q,
        g_kv,
        g_o.T,
        g_g,
        g_u,
        g_d.T,
        gain_a.reshape(64),
        gain_f.reshape(64),
    )


def solution(mesh):
    return jax.shard_map(
        per_device,
        mesh=mesh,
        in_specs=(
            P("dp", "ctx", None),
            P("dp", None),
            P(None, "tensor"),
            P(None, "tensor"),
            P("tensor", None),
            P(None, "tensor"),
            P(None, "tensor"),
            P("tensor", None),
            P(),
            P(),
            P("dp", "ctx", None),
        ),
        out_specs=(
            P("dp", "ctx", None),
            P("dp", "ctx", None),
            P(("dp", "ctx"), "tensor"),
            P(("dp", "ctx"), "tensor"),
            P("tensor", ("dp", "ctx")),
            P(("dp", "ctx"), "tensor"),
            P(("dp", "ctx"), "tensor"),
            P("tensor", ("dp", "ctx")),
            P(("dp", "ctx")),
            P(("dp", "ctx")),
        ),
        check_vma=False,
    )
```

```python
import jax
import jax.numpy as jnp
import numpy as np
from jax import lax
from jax.experimental import pallas as pl
from jax.experimental.pallas import tpu as pltpu
from jax.sharding import PartitionSpec as P

MESH = pl.DeviceIdType.MESH
F32 = jnp.float32
BF16 = jnp.bfloat16
EPSILON = 1e-05
NEG_FILL = -1e30
ROPE_BASE = 10000.0

D = 2048
HD = 64
T = 192
BLOCK = 96
TA = 128
R = 48
QC = 512
FC = 1408
KEYS = 1536
PAIRS = 4
QUERIES = 1536
CHUNK = 512
GROUP = 768
CHIP_KEYS = 384
FF_TILES = ((0, 384), (384, 384), (768, 384), (1152, 256))


def rope_tables():
    half = HD // 2
    freq = ROPE_BASE ** (-np.arange(half, dtype=np.float64) / half)
    freq = np.tile(freq, 4)[None, :]
    coarse = np.arange(16, dtype=np.float64)[:, None] * BLOCK * freq
    fine = np.arange(BLOCK, dtype=np.float64)[:, None] * freq
    coarse = np.stack([np.cos(coarse), np.sin(coarse)]).astype(np.float32)
    fine = np.stack([np.cos(fine), np.sin(fine)]).astype(np.float32)
    return coarse, fine


def dot(a, b):
    return jnp.dot(a, b, preferred_element_type=F32)


def dot_nt(a, b):
    return lax.dot_general(a, b, (((1,), (1,)), ((), ())), preferred_element_type=F32)


def tiles(total, size):
    return [(s, min(size, total - s)) for s in range(0, total, size)]


def lane_of(shape):
    return lax.broadcasted_iota(jnp.int32, shape, len(shape) - 1)


def swap_halves(t):
    first = lane_of(t.shape) % HD < HD // 2
    return jnp.where(first, pltpu.roll(t, 96, 1), pltpu.roll(t, 32, 1))


def layer_kernel(
    order, x_h, c_h, wq_h, wkv_h, wo_h, wg_h, wu_h, wd_h, ga_h, gf_h, coarse_h, fine_h,
    bo, gi, o_q, o_kv, o_o, o_g, o_u, o_d, gain_a, gain_f,
    ga, gf, coarse, fine, x, cot, wq, wkv, wo, wg, wu, wd, row_g, row_u, row_q, row_kv,
    xn, kvall, kk, vv, kt, vt, qst, cos_t, sin_t, s_buf, pt, ob, rl,
    zs, z_near, z_far, mid, dmid, hn, da, bo_s, gi_s, dinner, act, act_p, g_first,
    xn_t, c_t, hn_t, xn_p, c_p, hn_p, da_p, ob_p, dqp, dqp_p, dkvp, dkvp_p,
    dkv_r, delta, r1f, r2f, r3f, r4f, r1a, r2a, r3a, r4a,
    gain_s, gain_r,
    local_sem, send_sem, recv_sem,
):
    g_g, g_u, g_d = (dinner.at[i * 64 : (i + 1) * 64] for i in range(3))
    g_q, g_o, g_kv = (s_buf.at[i * 64 : (i + 1) * 64] for i in range(3))
    g_kv = g_kv.at[:, 0:128]

    iy = lax.axis_index("dp")
    ictx = lax.axis_index("ctx")
    iz = lax.axis_index("tensor")
    ix = ictx // 2
    core = ictx % 2
    other = 1 - core

    def z_peer(k):
        return (iy, ictx, (iz + k) % 4)

    def ctx_peer(k):
        return (iy, (ictx + k) % 8, iz)

    def x_peer(k):
        return (iy, ((ix + k) % 4) * 2 + core, iz)

    def y_peer(k):
        return ((iy + k) % 4, ictx, iz)

    core_peer = (iy, ix * 2 + other, iz)

    local = []
    local_done = set()

    def copy_local(src, dst):
        copy = pltpu.make_async_copy(src, dst, local_sem.at[len(local)])
        copy.start()
        local.append(copy)
        return copy

    def wait_local(*copies):
        for copy in copies:
            copy.wait()
            local_done.add(id(copy))

    x_load = copy_local(x_h, x)
    table_loads = [
        copy_local(ga_h, ga), copy_local(gf_h, gf),
        copy_local(coarse_h, coarse), copy_local(fine_h, fine),
    ]
    wkv_load = copy_local(wkv_h, wkv)
    wq_load = copy_local(wq_h, wq)

    barrier = pltpu.get_barrier_semaphore()
    greeted = (
        [ctx_peer(k) for k in range(1, 8)]
        + [z_peer(k) for k in range(1, 4)]
        + [y_peer(1), y_peer(3)]
    )
    for peer in greeted:
        pl.semaphore_signal(barrier, inc=1, device_id=peer, device_id_type=MESH)

    groups = []

    class Group:
        def __init__(self, size):
            self.n = len(groups)
            self.size = size
            self.arrived = self.released = self.used = False
            groups.append(self)

        def copy(self, src, dst, peer):
            return pltpu.make_async_remote_copy(
                src_ref=src, dst_ref=dst, send_sem=send_sem.at[self.n],
                recv_sem=recv_sem.at[self.n], device_id=peer, device_id_type=MESH,
            )

        def send(self, src, dst, peer):
            self.used = True
            self.copy(src, dst, peer).start()

        def wait_recv(self):
            if self.used and not self.arrived:
                self.copy(self.size, self.size, core_peer).wait_recv()
                self.arrived = True

        def wait_send(self):
            if self.used and not self.released:
                self.copy(self.size, self.size, core_peer).wait_send()
                self.released = True

    def send_one(src, dst, peer):
        group = Group(dst)
        group.send(src, dst, peer)
        return group

    wait_local(*table_loads)
    pick = lax.broadcasted_iota(jnp.int32, (16, 128), 0)
    sign = jnp.where(lane_of((BLOCK, 128)) % HD < HD // 2, -1.0, 1.0).astype(F32)
    for b in range(2):
        chosen = pick == order[0, ictx * 2 + b]
        ca = jnp.sum(jnp.where(chosen, coarse[0], 0.0), 0, keepdims=True)
        sa = jnp.sum(jnp.where(chosen, coarse[1], 0.0), 0, keepdims=True)
        cos_t[b * BLOCK : (b + 1) * BLOCK, :] = ca * fine[0] - sa * fine[1]
        sin_t[b * BLOCK : (b + 1) * BLOCK, :] = (sa * fine[0] + ca * fine[1]) * sign

    def rot(t):
        return t * cos_t[...] + swap_halves(t) * sin_t[...]

    def rot_back(t):
        return t * cos_t[...] - swap_halves(t) * sin_t[...]

    def inv_rms(v):
        return lax.rsqrt(jnp.mean(v * v, -1, keepdims=True) + EPSILON)

    low_lane = lane_of((T, 128)) < HD
    low_a, low_b = low_lane[0:TA], low_lane[0 : T - TA]

    wait_local(x_load)
    for i in range(4):
        rows = x[i * R : (i + 1) * R, :].astype(F32)
        xn[i * R : (i + 1) * R, :] = (rows * inv_rms(rows) * ga[...]).astype(BF16)
    wait_local(wkv_load)
    cot_load = copy_local(c_h, cot)
    wd_load = copy_local(wd_h, wd)
    normed = xn[...]
    kvp = dot(normed, wkv[...])
    kvall[ictx] = jnp.where(low_lane, rot(kvp), kvp).astype(BF16)
    pl.semaphore_wait(barrier, len(greeted))
    kv_group = Group(kvall.at[pl.ds(0, 7)])
    for k in (4, 5, 3, 2, 6, 7, 1):
        kv_group.send(kvall.at[ictx], kvall.at[ictx], ctx_peer(k))
    wait_local(wq_load)
    wo_load = copy_local(wo_h, wo)
    wg_load = copy_local(wg_h, wg)
    wu_load = copy_local(wu_h, wu)
    own_h, own_a, own_b = iy // 2, (iy % 2) * 2 + ix // 2, (ix % 2) * 2 + core
    own_rows = pl.ds(pl.multiple_of(((iy * 4 + ix) * 2 + core) * 64, 64), 64)
    row_loads = [
        copy_local(wg_h.at[own_h, own_a, own_b], row_g),
        copy_local(wu_h.at[own_h, own_a, own_b], row_u),
        copy_local(wq_h.at[own_rows], row_q),
        copy_local(wkv_h.at[own_rows], row_kv),
    ]

    def by_query(pair, value, ref):
        for i in range(2):
            h = pair * 2 + i
            one = jnp.where(low_lane, value, 0.0) if i == 0 else jnp.where(low_lane, 0.0, value)
            one = one.astype(BF16)
            ref[h * TA : (h + 1) * TA, :] = one[0:TA]
            ref[8 * TA + h * 64 : 8 * TA + (h + 1) * 64, :] = one[TA:T]

    for s, n in tiles(QC, 256):
        qp = dot(normed, wq[:, s : s + n])
        for j in range(n // 128):
            by_query(s // 128 + j, rot(qp[:, j * 128 : (j + 1) * 128]) * (HD ** -0.5), qst)

    turned = (4, 4, 2, 2, 32, T)
    xn_t[...] = normed.T.reshape(turned)
    xnt_copy = send_one(xn_t.at[:, :, other], xn_p, core_peer)
    wait_local(cot_load)
    cot_rows = cot[...]
    c_t[...] = cot_rows.T.reshape(turned)
    ct_copy = send_one(c_t.at[:, :, other], c_p, core_peer)
    wait_local(wd_load)
    for s, n in tiles(FC, 512):
        rows = slice(s // 128, (s + n) // 128)
        dinner[:, s : s + n] = dot_nt(cot_rows, wd[rows].reshape(n, D))

    kv_group.wait_recv()
    for j in range(8):
        wide = kvall[j].astype(F32)
        rolled = pltpu.roll(wide, HD, 1)
        rows = pl.ds(j * T, T)
        kk[rows, :] = jnp.where(low_lane, wide, rolled).astype(BF16)
        vv[rows, :] = jnp.where(low_lane, rolled, wide).astype(BF16)
    kv_t = kvall[...].reshape(KEYS, 128).T
    kt[0:HD, :] = kv_t[0:HD]
    kt[HD : 2 * HD, :] = kv_t[0:HD]
    vt[0:HD, :] = kv_t[HD : 2 * HD]
    vt[HD : 2 * HD, :] = kv_t[HD : 2 * HD]
    vt[2 * HD : 2 * HD + 16, :] = jnp.ones((16, KEYS), BF16)

    lane = lane_of((1, CHUNK))
    token = lane % TA
    start_0, start_1 = order[0, ictx * 2] * BLOCK, order[0, ictx * 2 + 1] * BLOCK
    place_a = jnp.where(token >= BLOCK, start_1 + token - BLOCK, start_0 + token)
    place_b = start_1 + (TA - BLOCK) + lane % 64
    key_row = lax.broadcasted_iota(jnp.int32, (BLOCK, CHUNK), 0)

    def attend(chunk):
        q_place = place_a if chunk < 2 else place_b
        lanes = slice(chunk * CHUNK, (chunk + 1) * CHUNK)
        top = jnp.full((8, CHUNK), NEG_FILL, F32)
        for r0 in range(0, KEYS, GROUP):
            scores = dot_nt(kk[r0 : r0 + GROUP, :], qst[lanes, :])
            for b in range(GROUP // BLOCK):
                limit = q_place - order[0, r0 // BLOCK + b] * BLOCK
                rows = slice(b * BLOCK, (b + 1) * BLOCK)
                seen = jnp.where(key_row <= limit, scores[rows], NEG_FILL)
                s_buf[r0 + b * BLOCK : r0 + (b + 1) * BLOCK, :] = seen
                top = jnp.maximum(top, jnp.max(seen.reshape(BLOCK // 8, 8, CHUNK), 0))
        top = jnp.max(top, 0, keepdims=True)
        for r0 in range(0, KEYS, GROUP):
            rows = slice(r0, r0 + GROUP)
            pt[rows, lanes] = jnp.exp(s_buf[rows, :] - top).astype(BF16)
        summed = dot(vt[...], pt[:, lanes])
        inv = 1.0 / summed[2 * HD : 2 * HD + 1]
        out = summed[0 : 2 * HD] * inv
        inv = jnp.broadcast_to(inv, (2 * HD, CHUNK))
        if chunk < 2:
            for j in range(2):
                pair = slice((chunk * 2 + j) * 128, (chunk * 2 + j + 1) * 128)
                one, two = slice(j * 256, j * 256 + 128), slice(j * 256 + 128, j * 256 + 256)
                ob[0:TA, pair] = jnp.where(low_a, out[:, one].T, out[:, two].T).astype(BF16)
                rl[0:TA, pair] = jnp.where(low_a, inv[:, one].T, inv[:, two].T)
        else:
            for p in range(PAIRS):
                pair = slice(p * 128, (p + 1) * 128)
                o2, i2 = out[:, pair].T, inv[:, pair].T
                ob[TA:T, pair] = jnp.where(low_b, o2[0:64], o2[64:128]).astype(BF16)
                rl[TA:T, pair] = jnp.where(low_b, i2[0:64], i2[64:128])

    def z_rows(part, z):
        if part == 0:
            return pl.ds(pl.multiple_of(z * 32, 32), 32)
        return pl.ds(pl.multiple_of(TA + z * 16, 16), 16)

    kept = (slice(0, 32), slice(32, 48))
    cols_l, cols_r, all_cols = pl.ds(0, D // 2), pl.ds(D // 2, D // 2), pl.ds(0, D)
    zp, zm, z2 = (iz + 1) % 4, (iz + 3) % 4, (iz + 2) % 4

    class ZScatter:
        def __init__(self, src, n, part):
            self.src, self.n, self.part = src, n, part
            self.far = Group(z_far.at[n, :, kept[part]])
            self.near = Group(z_near.at[n, :, kept[part]])

        def first(self, cols=(0, D // 2, D // 2)):
            l, r, width = cols
            src, n, part = self.src, self.n, self.part
            keep = kept[part]
            left, right = pl.ds(l, width), pl.ds(r, width)
            if l is not None:
                far = z_far.at[n, 0, keep, left]
                self.far.send(src.at[z_rows(part, z2), left], far, z_peer(1))
            if r is not None:
                far = z_far.at[n, 1, keep, pl.ds(r - D // 2, width)]
                self.far.send(src.at[z_rows(part, z2), right], far, z_peer(3))
            if l is not None:
                near = z_near.at[n, 1, keep, left]
                self.near.send(src.at[z_rows(part, zm), left], near, z_peer(3))
            if r is not None:
                near = z_near.at[n, 0, keep, right]
                self.near.send(src.at[z_rows(part, zp), right], near, z_peer(1))

        def second(self):
            src, n, part = self.src, self.n, self.part
            keep = kept[part]
            self.far.wait_recv()
            for way, z, cols, k in ((0, zp, cols_l, 1), (1, zm, cols_r, 3)):
                rows = z_rows(part, z)
                total = src[rows, cols].astype(F32) + z_far[n, way, keep, :].astype(F32)
                src[rows, cols] = total.astype(BF16)
                self.near.send(src.at[rows, cols], z_near.at[n, way, keep, cols], z_peer(k))

        def result(self):
            self.near.wait_recv()
            total = self.src[z_rows(self.part, iz), :].astype(F32)
            for way in range(2):
                total = total + z_near[self.n, way, kept[self.part], :].astype(F32)
            return total

        def wait_send(self):
            self.far.wait_send()
            self.near.wait_send()

    class ZGather:
        def __init__(self, buf, part, own=None):
            self.buf, self.part = buf, part
            self.far = Group(z_far.at[0, :, kept[part]])
            self.near = Group(z_near.at[0, :, kept[part]])
            rows = z_rows(part, iz)
            for cols, way, k, group in (
                (cols_l, 0, 1, self.far), (cols_r, 1, 3, self.far),
                (cols_r, 0, 1, self.near), (cols_l, 1, 3, self.near),
            ):
                src = buf.at[rows, cols] if own is None else own.at[kept[part], cols]
                group.send(src, buf.at[rows, cols], z_peer(k))

        def second(self):
            self.far.wait_recv()
            for z, cols, k in ((zm, cols_l, 1), (zp, cols_r, 3)):
                piece = self.buf.at[z_rows(self.part, z), cols]
                self.near.send(piece, piece, z_peer(k))

        def wait_recv(self):
            self.near.wait_recv()

    def project_out(part):
        rows = slice(0, TA) if part == 0 else slice(TA, T)
        scatter = ZScatter(zs, 0, part)
        for l in (0, 512):
            for s in (l, l + D // 2):
                zs[rows, s : s + 512] = dot(ob[rows, :], wo[:, s : s + 512]).astype(BF16)
            scatter.first((l, l + D // 2, 512))
        return scatter

    attend(0)
    attend(1)
    wait_local(wo_load)
    attn_sums = [project_out(0)]
    attend(2)
    attn_sums.append(project_out(1))
    ob_copy = send_one(ob, ob_p, core_peer)

    hn_parts = []

    def norm(part):
        m = x[z_rows(part, iz), :].astype(F32) + attn_sums[part].result()
        mid[kept[part], :] = m
        hn[z_rows(part, iz), :] = (m * inv_rms(m) * gf[...]).astype(BF16)
        hn_parts.append(ZGather(hn, part))

    attn_sums[0].second()
    attn_sums[1].second()
    norm(0)
    norm(1)
    hn_parts[0].second()
    hn_parts[1].second()

    xp, xm, x2 = (ix + 1) % 4, (ix + 3) % 4, (ix + 2) % 4
    yp, ym, y2 = (iy + 1) % 4, (iy + 3) % 4, (iy + 2) % 4

    def own_part(ref):
        return lambda dy, dx, h: ref[dy, dx, core, h]

    def partner_part(ref):
        return lambda dy, dx, h: ref[dy, dx, h]

    all4 = pl.ds(0, 4)
    first_rows = [(all4, x2, 0), (y2, all4, 1)]
    other_rows = [(all4, dx, 0) for dx in (xp, xm, ix)] + [(dy, all4, 1) for dy in (yp, ym, iy)]

    def weight_grad(part, which, own_t, partner_t, own_b, partner_b, b0=0, n=None):
        ref, half, part_c0, part_n, _, _ = parts[part]
        n = part_n if n is None else n
        early = which is first_rows and part < 3
        get_own, get_partner = own_part(own_t), partner_part(partner_t)
        a_own = jnp.concatenate([get_own(*i).reshape(128, T) for i in which], 0)
        a_partner = jnp.concatenate([get_partner(*i).reshape(128, T) for i in which], 0)
        for s, w in tiles(n, 256):
            s = s + b0
            r = dot(a_own, own_b[:, s : s + w]) + dot(a_partner, partner_b[:, s : s + w])
            r = r.astype(BF16)
            cols = slice(part_c0 + s, part_c0 + s + w)
            for i, (dy, dx, h) in enumerate(which):
                rows = r[i * 128 : (i + 1) * 128].reshape(4, 32, w)
                if early:
                    g_first[part, i, :, :, cols] = rows
                else:
                    ref[half, dy, dx, h, :, cols] = rows

    f_bufs = [[r.at[i] for r in (r1f, r2f, r3f, r4f)] for i in range(3)]
    a_bufs = [r1a, r2a, r3a, r4a]
    parts = [
        (wg, 1, 0, FC, f_bufs[0], 0),
        (wg, 0, 0, FC, f_bufs[1], 0),
        (wu, 0, 0, FC, f_bufs[2], 0),
        (wu, 1, 0, 512, a_bufs, 0),
        (wu, 1, 512, 512, a_bufs, 512),
        (wu, 1, 1024, 128, a_bufs, 1024),
    ]
    flights = {}
    lo2, hi2 = pl.ds(0, 2), pl.ds(2, 2)
    all32, lo16, hi16 = pl.ds(0, 32), pl.ds(0, 16), pl.ds(16, 16)

    def g_index(part, dy, dx, h, rows=None):
        ref, half, c0, n, _, _ = parts[part]
        return (half, dy, dx, h, all32 if rows is None else rows, pl.ds(c0, n))

    def first_piece(part, flow, pair, s, n):
        if part < 3:
            return g_first.at[part, flow, pair, :, pl.ds(s, n)]
        ref, half, c0, _, _, _ = parts[part]
        dy, dx = (pair, x2) if flow == 0 else (y2, pair)
        return ref.at[half, dy, dx, flow, :, pl.ds(c0 + s, n)]

    def outgoing(part, step, s, n):
        if step == 0:
            return tuple(
                tuple(first_piece(part, flow, pair, s, n) for pair in (lo2, hi2))
                for flow in range(2)
            )
        if step == 1:
            index = (
                (g_index(part, all4, xp, 0), g_index(part, all4, xm, 0)),
                (g_index(part, yp, all4, 1), g_index(part, ym, all4, 1)),
            )
        elif step == 2:
            index = (
                (g_index(part, y2, ix, 0, lo16), g_index(part, y2, ix, 0, hi16)),
                (g_index(part, iy, x2, 1, lo16), g_index(part, iy, x2, 1, hi16)),
            )
        else:
            index = (
                (g_index(part, yp, ix, 0), g_index(part, ym, ix, 0)),
                (g_index(part, iy, xp, 1), g_index(part, iy, xm, 1)),
            )
        ref = parts[part][0]
        return tuple(tuple(ref.at[i] for i in flow) for flow in index)

    def landing(part, step, flow, way, s=0, n=None):
        _, _, _, part_n, bufs, b0 = parts[part]
        return bufs[step].at[flow, way, ..., pl.ds(b0 + s, part_n if n is None else n)]

    def rs_send(part, step, s=0, n=None, flows=(0, 1)):
        _, _, _, part_n, bufs, b0 = parts[part]
        n = part_n if n is None else n
        out = outgoing(part, step, s, n)
        for flow in flows:
            if (part, step, flow) not in flights:
                flights[part, step, flow] = Group(bufs[step].at[flow, ..., pl.ds(b0, part_n)])
            group = flights[part, step, flow]
            along_x = (flow == 0) == (step < 2)
            for way, k in ((0, 1), (1, 3)):
                peer = x_peer(k) if along_x else y_peer(k)
                group.send(out[flow][way], landing(part, step, flow, way, s, n), peer)

    def add_in(ref, index, *arrived):
        total = ref[index].astype(F32)
        for a in arrived:
            total = total + a[...].astype(F32)
        ref[index] = total.astype(BF16)

    def rs_recv(part, step, flows=(0, 1)):
        ref = parts[part][0]
        for flow in flows:
            flights[part, step, flow].wait_recv()
            got = [landing(part, step, flow, way) for way in range(2)]
            if step == 0:
                if flow == 0:
                    add_in(ref, g_index(part, lo2, xp, 0), got[0])
                    add_in(ref, g_index(part, hi2, xm, 0), got[1])
                else:
                    add_in(ref, g_index(part, yp, lo2, 1), got[0])
                    add_in(ref, g_index(part, ym, hi2, 1), got[1])
            elif step == 1:
                if flow == 0:
                    add_in(ref, g_index(part, all4, ix, 0), *got)
                else:
                    add_in(ref, g_index(part, iy, all4, 1), *got)
            elif step == 2:
                if flow == 0:
                    add_in(ref, g_index(part, yp, ix, 0, lo16), got[0])
                    add_in(ref, g_index(part, ym, ix, 0, hi16), got[1])
                else:
                    add_in(ref, g_index(part, iy, xp, 1, lo16), got[0])
                    add_in(ref, g_index(part, iy, xm, 1, hi16), got[1])

    def rs_turn(part, step, flows=(0, 1)):
        for flow in flows:
            rs_recv(part, step, (flow,))
            rs_send(part, step + 1, flows=(flow,))

    def rs_last(part, outs):
        rs_recv(part, 3)
        ref = parts[part][0]
        for flow in range(2):
            total = ref[g_index(part, iy, ix, flow)].astype(F32)
            for way in range(2):
                total = total + landing(part, 3, flow, way)[...].astype(F32)
            for stage, out, s, n in outs:
                stage[flow * 32 : (flow + 1) * 32, :] = total[:, s : s + n]
        for stage, out, s, n in outs:
            copy_local(stage, out)

    wait_local(wg_load, wu_load)
    for part in hn_parts:
        part.wait_recv()
    hidden = hn[...]
    hn_t[...] = hidden.T.reshape(turned)
    hnt_copy = send_one(hn_t.at[:, :, other], hn_p, core_peer)
    act_groups = [Group(act_p.at[:, :, pl.ds(s, n)]) for s, n in FF_TILES]

    def first_of_tile(t):
        s, n = FF_TILES[t]
        act_groups[t].wait_recv()
        for part, own_t, partner_t in ((0, c_t, c_p), (1, hn_t, hn_p), (2, hn_t, hn_p)):
            weight_grad(part, first_rows, own_t, partner_t, act.at[part], act_p.at[part], s, n)
            rs_send(part, 0, s, n)

    for t, (s, n) in enumerate(FF_TILES):
        cols = slice(s, s + n)
        g = dot(hidden, wg[:, :, :, :, :, cols].reshape(D, n))
        u = dot(hidden, wu[:, :, :, :, :, cols].reshape(D, n))
        sig = 1.0 / (1.0 + jnp.exp(-g))
        a = g * sig
        di = dinner[:, cols]
        act[0, :, cols] = (a * u).astype(BF16)
        act[1, :, cols] = (di * u * sig * (1.0 + g * (1.0 - sig))).astype(BF16)
        act[2, :, cols] = (di * a).astype(BF16)
        piece = pl.ds(s, n)
        act_groups[t].send(act.at[:, :, piece], act_p.at[:, :, piece], core_peer)
        if t == 0:
            ct_copy.wait_recv()
            hnt_copy.wait_recv()
        else:
            first_of_tile(t - 1)

    for scatter in attn_sums:
        scatter.wait_send()
    dhn_sums = [ZScatter(zs, 1, part) for part in range(2)]
    for t in (0, 2, 1, 3):
        cols = slice(t * 512, (t + 1) * 512)
        block = (t // 2, slice((t % 2) * 2, (t % 2) * 2 + 2))
        r = dot_nt(act[1], wg[block].reshape(512, FC)) + dot_nt(act[2], wu[block].reshape(512, FC))
        zs[:, cols] = r.astype(BF16)
        dhn_sums[0].first((t * 512, None, 512) if t < 2 else (None, t * 512, 512))
        if t == 0:
            first_of_tile(3)
    dhn_sums[1].first()
    inner = act[0]
    for s, n in tiles(D, 512):
        xn[:, s : s + n] = dot(inner, wd[..., s : s + n].reshape(FC, n)).astype(BF16)
    weight_grad(0, other_rows, c_t, c_p, act.at[0], act_p.at[0])
    dhn_sums[0].second()
    dhn_sums[1].second()
    rs_turn(0, 0)
    weight_grad(1, other_rows, hn_t, hn_p, act.at[1], act_p.at[1])
    weight_grad(2, other_rows, hn_t, hn_p, act.at[2], act_p.at[2])

    da_parts = []

    def norm_back(part):
        m = mid[kept[part], :]
        r2 = inv_rms(m)
        mhat = m * r2
        scaled = dhn_sums[part].result() * gf[...]
        rows = z_rows(part, iz)
        dm = cot[rows, :].astype(F32) + r2 * (
            scaled - mhat * jnp.mean(scaled * mhat, -1, keepdims=True)
        )
        dmid[kept[part], :] = dm
        da[rows, :] = dm.astype(BF16)
        da_parts.append(ZGather(da, part))

    norm_back(0)
    norm_back(1)
    rs_turn(1, 0)
    da_parts[0].second()
    da_parts[1].second()
    rs_turn(2, 0, (1,))
    rs_turn(0, 1)

    for part in da_parts:
        part.wait_recv()
    ffn_sums = [ZScatter(xn, 2, part) for part in range(2)]
    for scatter in ffn_sums:
        scatter.first()
    grad_attn = da[...]
    for s, n in tiles(QC, 256):
        grad_rows = dot_nt(grad_attn, wo[s : s + n, :])
        for j in range(n // 128):
            p = s // 128 + j
            pair = slice(p * 128, (p + 1) * 128)
            g = grad_rows[:, j * 128 : (j + 1) * 128] * rl[:, pair]
            by_query(p, g, kk)
            by_row = (g * ob[:, pair].astype(F32)).T
            for i in range(2):
                h = p * 2 + i
                sums = jnp.sum(by_row[i * HD : (i + 1) * HD], 0, keepdims=True)
                delta[:, h * TA : (h + 1) * TA] = sums[:, 0:TA]
                delta[:, 8 * TA + h * 64 : 8 * TA + (h + 1) * 64] = sums[:, TA:T]
    ct_copy.wait_send()
    c_t[...] = grad_attn.T.reshape(turned)
    dat_copy = send_one(c_t.at[:, :, other], da_p, core_peer)
    dob = kk

    kv_group.wait_send()
    dkv_group = Group(kvall.at[pl.ds(0, 7)])
    for i, step in enumerate((2, 1, 3, 0)):
        chip = (ix + step) % 4
        rows = pl.ds(pl.multiple_of(chip * CHIP_KEYS, CHIP_KEYS), CHIP_KEYS)
        weights = pt[rows, :]
        dv = dot(weights, dob[...])
        for s, n in tiles(QUERIES, CHUNK):
            lanes = slice(s, s + n)
            grad_weights = dot_nt(vv[rows, :], dob[lanes, :])
            pt[rows, lanes] = (
                weights[:, lanes].astype(F32) * (grad_weights - delta[:, lanes])
            ).astype(BF16)
        dk = dot(pt[rows, :], qst[...])
        both = jnp.where(
            lane_of((CHIP_KEYS, 128)) < HD, dk + pltpu.roll(dk, HD, 1), dv + pltpu.roll(dv, HD, 1)
        ).astype(BF16)
        for c in range(2):
            kvall[chip * 2 + c] = both[c * T : (c + 1) * T]
        for c, goal in ((0, core), (1, other)):
            if step != 0 or c == 1:
                dkv_group.send(kvall.at[chip * 2 + goal], dkv_r.at[i, c], (iy, chip * 2 + goal, iz))
        if i == 2:
            dat_copy.wait_recv()
            ob_copy.wait_recv()
            weight_grad(3, first_rows, c_t, da_p, ob, ob_p)
            rs_send(3, 0)
            rs_turn(2, 0, (0,))
    for scatter in ffn_sums:
        scatter.second()
    dq_t = dot(kt[...], pt[...]) * (HD ** -0.5)
    for p in range(PAIRS):
        a0 = dq_t[:, p * 256 : p * 256 + 128].T
        a1 = dq_t[:, p * 256 + 128 : p * 256 + 256].T
        b = dq_t[:, 8 * TA + p * 128 : 8 * TA + (p + 1) * 128].T
        dq = jnp.concatenate(
            [jnp.where(low_a, a0, a1), jnp.where(low_b, b[0:64], b[64:128])], 0
        )
        dqp[:, p * 128 : (p + 1) * 128] = rot_back(dq).astype(BF16)
    dqp_copy = send_one(dqp, dqp_p, core_peer)

    xnt_copy.wait_recv()
    dqp_copy.wait_recv()
    weight_grad(4, first_rows, xn_t, xn_p, dqp, dqp_p)
    rs_send(4, 0)
    rs_turn(1, 1)

    dkv_group.wait_recv()
    home = kvall[ictx].astype(F32) + dkv_r[3, 1].astype(F32)
    for i in range(3):
        for c in range(2):
            home = home + dkv_r[i, c].astype(F32)
    dkvp[...] = jnp.where(low_lane, rot_back(home), home).astype(BF16)
    dkvp_copy = send_one(dkvp, dkvp_p, core_peer)
    for scatter in dhn_sums:
        scatter.wait_send()
    q_rows, kv_rows = dqp[...], dkvp[...]
    dxn_sums = [ZScatter(zs, 3, part) for part in range(2)]
    for l in (0, 512):
        for s in (l, l + D // 2):
            cols = slice(s, s + 512)
            r = dot_nt(q_rows, wq[cols, :]) + dot_nt(kv_rows, wkv[cols, :])
            zs[:, cols] = r.astype(BF16)
        dxn_sums[0].first((l, l + D // 2, 512))
    dxn_sums[1].first()

    dkvp_copy.wait_recv()
    weight_grad(5, first_rows, xn_t, xn_p, dkvp, dkvp_p)
    rs_send(5, 0)
    weight_grad(3, other_rows, c_t, da_p, ob, ob_p)
    dxn_sums[0].second()
    dxn_sums[1].second()
    bo_parts = []
    for part in range(2):
        bo_s[kept[part], :] = (mid[kept[part], :] + ffn_sums[part].result()).astype(BF16)
        copy_local(bo_s.at[kept[part]], bo.at[z_rows(part, iz)])
        bo_parts.append(ZGather(bo, part, bo_s))
    weight_grad(4, other_rows, xn_t, xn_p, dqp, dqp_p)
    weight_grad(5, other_rows, xn_t, xn_p, dkvp, dkvp_p)
    rs_turn(3, 0)
    rs_turn(4, 0)
    rs_turn(5, 0)
    rs_turn(0, 2)

    gi_parts = []

    def first_norm_back(part):
        rows = x[z_rows(part, iz), :].astype(F32)
        r1 = inv_rms(rows)
        xhat = rows * r1
        scaled = dxn_sums[part].result() * ga[...]
        gi_s[kept[part], :] = (
            dmid[kept[part], :]
            + r1 * (scaled - xhat * jnp.mean(scaled * xhat, -1, keepdims=True))
        ).astype(BF16)
        copy_local(gi_s.at[kept[part]], gi.at[z_rows(part, iz)])
        gi_parts.append(ZGather(gi, part, gi_s))

    first_norm_back(0)
    first_norm_back(1)
    for part in bo_parts:
        part.second()
    rs_turn(2, 1)
    rs_turn(1, 2)
    gi_parts[0].second()
    gi_parts[1].second()
    rs_turn(3, 1)
    rs_turn(4, 1)
    rs_turn(5, 1)
    rs_last(0, [(g_d, o_d, 0, FC)])
    rs_turn(2, 2)
    rs_last(1, [(g_g, o_g, 0, FC)])
    rs_turn(4, 2)
    rs_turn(5, 2)
    rs_turn(3, 2)
    rs_last(2, [(g_u, o_u, 0, FC)])

    wait_local(*row_loads)

    def row_products(pairs):
        total = jnp.zeros((64, 128), F32)
        for grad, weight in pairs:
            n = grad.shape[-1]
            w = weight[...].reshape(64, n)
            for s, _ in tiles(n, 128):
                total = total + grad[:, s : s + 128] * w[:, s : s + 128].astype(F32)
        return jnp.sum(total.T, 0, keepdims=True)

    def exchange_gain(i, pairs):
        gain_s[i] = jnp.broadcast_to(row_products(pairs), (8, 64))
        group = Group(gain_r.at[i])
        for k in range(1, 4):
            group.send(gain_s.at[i], gain_r.at[i, k - 1], z_peer(k))
        return group

    def gain_total(i, group):
        group.wait_recv()
        total = gain_s[i]
        for k in range(3):
            total = total + gain_r[i, k]
        return total[0:1]

    gain_f_group = exchange_gain(0, [(g_g, row_g), (g_u, row_u)])
    rs_last(4, [(g_q, o_q, 0, 512)])
    rs_last(5, [(g_kv, o_kv, 0, 128)])
    gain_a_group = exchange_gain(1, [(g_q, row_q), (g_kv, row_kv)])
    rs_last(3, [(g_o, o_o, 0, 512)])
    chip_cols = pl.ds(pl.multiple_of((iy * 4 + ix) * 128, 128), 128)

    def own_gain(ref):
        v = ref[:, chip_cols]
        return jnp.where(core == 1, pltpu.roll(v, 64, 1), v)[:, 0:64]

    gain_f[...] = gain_total(0, gain_f_group) / own_gain(gf)
    gain_a[...] = gain_total(1, gain_a_group) / own_gain(ga)

    for group in groups:
        group.wait_recv()
    for group in groups:
        group.wait_send()
    wait_local(*[copy for copy in local if id(copy) not in local_done])


def store_kernel(*refs):
    n = 10
    src, dst, held = refs[:n], refs[n : 2 * n], refs[2 * n : 3 * n]
    wide, in_sem, out_sem = refs[3 * n :]
    moves = []
    for i in range(n):
        if i < 2:
            for j in range(4):
                rows = pl.ds(j * R, R)
                moves.append((src[i].at[rows], held[i].at[rows], dst[i].at[rows], (i, rows)))
        else:
            moves.append((src[i], held[i], dst[i], (i, None)))
    moves.sort(key=lambda move: move[3][0] != 1)
    fetches = []
    for k, (a, b, _, _) in enumerate(moves):
        copy = pltpu.make_async_copy(a, b, in_sem.at[k])
        copy.start()
        fetches.append(copy)
    stores = []
    for k, (_, b, c, (i, rows)) in enumerate(moves):
        fetches[k].wait()
        if i == 1:
            wide[rows, :] = b[...].astype(F32)
            b = wide.at[rows]
        copy = pltpu.make_async_copy(b, c, out_sem.at[k])
        copy.start()
        stores.append(copy)
    for copy in stores:
        copy.wait()


N_GROUPS = 95
N_LOCAL = 26


def per_device(
    hidden_in, block_order, w_query, w_keyval, w_output, w_gate, w_up, w_down,
    gain_attn, gain_ffn, cotangent,
):
    coarse, fine = rope_tables()
    any_spec = pl.BlockSpec(memory_space=pl.ANY)
    vmem = pl.BlockSpec(memory_space=pltpu.VMEM)
    smem = pl.BlockSpec(memory_space=pltpu.SMEM)
    shape = jax.ShapeDtypeStruct
    wide = (2, 4, 4, 2, 32, FC)
    turned = (4, 4, 2, 2, 32, T)
    half_turned = (4, 4, 2, 32, T)
    scratch = [
        pltpu.VMEM(s, t)
        for s, t in (
            ((1, D), F32), ((1, D), F32), ((2, 16, 128), F32), ((2, BLOCK, 128), F32),
            ((T, D), BF16), ((T, D), BF16),
            ((D, QC), BF16), ((D, 128), BF16), ((QC, D), BF16),
            (wide, BF16), (wide, BF16), ((11, 4, 32, D), BF16),
            ((2, 32, FC), BF16), ((2, 32, FC), BF16), ((64, QC), BF16), ((64, 128), BF16),
            ((T, D), BF16), ((8, T, 128), BF16),
            ((KEYS, 128), BF16), ((KEYS, 128), BF16),
            ((128, KEYS), BF16), ((144, KEYS), BF16),
            ((QUERIES, 128), BF16), ((T, 128), F32), ((T, 128), F32),
            ((KEYS, CHUNK), F32), ((KEYS, QUERIES), BF16),
            ((T, QC), BF16), ((T, QC), F32),
            ((T, D), BF16), ((4, 2, R, D), BF16), ((4, 2, R, D // 2), BF16),
            ((R, D), F32), ((R, D), F32),
            ((T, D), BF16), ((T, D), BF16), ((R, D), BF16), ((R, D), BF16),
            ((T, FC), F32), ((3, T, FC), BF16), ((3, T, FC), BF16),
            ((3, 2, 4, 32, FC), BF16),
            (turned, BF16), (turned, BF16), (turned, BF16),
            (half_turned, BF16), (half_turned, BF16), (half_turned, BF16), (half_turned, BF16),
            ((T, QC), BF16), ((T, QC), BF16), ((T, QC), BF16),
            ((T, 128), BF16), ((T, 128), BF16),
            ((4, 2, T, 128), BF16), ((1, QUERIES), F32),
            ((3, 2, 2, 2, 32, FC), BF16), ((3, 2, 2, 4, 32, FC), BF16),
            ((3, 2, 2, 16, FC), BF16), ((3, 2, 2, 32, FC), BF16),
            ((2, 2, 2, 32, 1152), BF16), ((2, 2, 4, 32, 1152), BF16),
            ((2, 2, 16, 1152), BF16), ((2, 2, 32, 1152), BF16),
            ((2, 8, 64), F32), ((2, 3, 8, 64), F32),
        )
    ] + [
        pltpu.SemaphoreType.DMA((N_LOCAL,)),
        pltpu.SemaphoreType.DMA((N_GROUPS,)),
        pltpu.SemaphoreType.DMA((N_GROUPS,)),
    ]
    grads = (
        shape((64, QC), F32), shape((64, 128), F32), shape((64, QC), F32),
        shape((64, FC), F32), shape((64, FC), F32), shape((64, FC), F32),
        shape((1, 64), F32), shape((1, 64), F32),
    )
    outs = pl.pallas_call(
        layer_kernel,
        out_shape=(shape((T, D), BF16), shape((T, D), BF16)) + grads,
        in_specs=[smem] + [any_spec] * 12,
        out_specs=(any_spec,) * 8 + (vmem,) * 2,
        scratch_shapes=scratch,
        compiler_params=pltpu.CompilerParams(
            collective_id=0, has_side_effects=True, vmem_limit_bytes=65200 * 1024
        ),
    )(
        block_order, hidden_in.reshape(T, D), cotangent.reshape(T, D),
        w_query, w_keyval, w_output, w_gate.reshape(wide), w_up.reshape(wide),
        w_down.reshape(11, 4, 32, D),
        gain_attn.reshape(1, D), gain_ffn.reshape(1, D), coarse, fine,
    )
    outs = pl.pallas_call(
        store_kernel,
        out_shape=(shape((T, D), BF16), shape((T, D), F32)) + grads,
        in_specs=[any_spec] * 10,
        out_specs=(any_spec,) * 10,
        scratch_shapes=[pltpu.VMEM((T, D), BF16)] * 2
        + [pltpu.VMEM(g.shape, F32) for g in grads]
        + [
            pltpu.VMEM((T, D), F32),
            pltpu.SemaphoreType.DMA((16,)), pltpu.SemaphoreType.DMA((16,)),
        ],
        compiler_params=pltpu.CompilerParams(vmem_limit_bytes=65200 * 1024),
    )(*outs)
    bo, gi, g_q, g_kv, g_o, g_g, g_u, g_d, gain_a, gain_f = outs
    return (
        bo.reshape(1, T, D),
        gi.reshape(1, T, D),
        g_q,
        g_kv,
        g_o.T,
        g_g,
        g_u,
        g_d.T,
        gain_a.reshape(64),
        gain_f.reshape(64),
    )


def solution(mesh):
    return jax.shard_map(
        per_device,
        mesh=mesh,
        in_specs=(
            P("dp", "ctx", None),
            P("dp", None),
            P(None, "tensor"),
            P(None, "tensor"),
            P("tensor", None),
            P(None, "tensor"),
            P(None, "tensor"),
            P("tensor", None),
            P(),
            P(),
            P("dp", "ctx", None),
        ),
        out_specs=(
            P("dp", "ctx", None),
            P("dp", "ctx", None),
            P(("dp", "ctx"), "tensor"),
            P(("dp", "ctx"), "tensor"),
            P("tensor", ("dp", "ctx")),
            P(("dp", "ctx"), "tensor"),
            P(("dp", "ctx"), "tensor"),
            P("tensor", ("dp", "ctx")),
            P(("dp", "ctx")),
            P(("dp", "ctx")),
        ),
        check_vma=False,
    )
```
